32 devices in a mesh: groups: 2 (over y), wide: 16 (over z, x, core).
Axes of the slice: x: 2, y: 2, z: 4, core: 2. Of those that a mesh axis runs over, the one named last changes fastest.
Arguments:
- tokens: bfloat16 [4096, 16384], P(('groups', 'wide')), parts along dimension 0, may hold values from -36 to 36, as said below
- norm_gain: float32 [16384], replicated, may hold values from 0.5 to 1.5
- gate_weight: bfloat16 [16384, 256], P('wide'), may hold values from -0.046875 to 0.046875
- up_weight: bfloat16 [16384, 256], P('wide'), may hold values from -0.046875 to 0.046875
- down_weight: bfloat16 [256, 16384], P(None, 'wide'), may hold values from -0.375 to 0.375
- owner_rows: int32 [16], replicated, may hold values from 0 to 15, each once
- seg_counts: int32 [32], P(('groups', 'wide')), parts along dimension 0, may hold values from 1 to 112, as said below
Outputs:
- mlp_out: bfloat16 [4096, 16384], P(('groups', 'wide')), parts along dimension 0
The draws below stay inside these ranges and needn't reach their ends.
There are 2 independent parts, one for each index of `groups`. The reference program is written for one: setup_inputs(seed, part) draws one part's arguments, and reference() takes and returns one part's arrays. A program takes and returns all parts, laid end to end along the dimension named above; an argument that names none is the same for every part. Nothing has to cross between parts.
Inputs may be any that keep to these rules, and one draw needn't show every extreme that they name: `tokens`: activations of mixed scale. `owner_rows`: each index of wide stores exactly one block. `seg_counts`: some document has all 112 segment tokens live.
All inputs are finite; a program needn't handle non-finite values.
Results may differ from the reference program's by a relative error of at most 0.0065.
Values may be sent and summed in bfloat16 or wider, within the bound.
No kernel may reach another device: no remote copies, remote signals or barrier semaphores. Data moves between devices by JAX's collectives and lax.ppermute only.
A program may use at most 128 MiB of HBM per device.

```python
import jax
import jax.numpy as jnp
from jax import lax

D = 16384
HID = 256
SEG = 112
MEM = 16
ROWS = 128
DOCS = 16
TOKENS = 2048
BLOCK = 1024
N_WIDE = 16


def draw_tokens(key, part):
    key = jax.random.fold_in(key, 11)
    key_base, key_rows, key_cols = jax.random.split(key, 3)
    noise = jnp.clip(jax.random.normal(key_base, (TOKENS, D), jnp.float32), -4.0, 4.0)
    row_scale = jnp.exp(jax.random.uniform(key_rows, (TOKENS, 1), jnp.float32, jnp.log(0.3), jnp.log(3.0)))
    col_scale = jnp.exp(jax.random.uniform(key_cols, (1, D), jnp.float32, jnp.log(0.3), jnp.log(3.0)))
    return (noise * row_scale * col_scale).astype(jnp.bfloat16)


def draw_seg_counts(key, part):
    key = jax.random.fold_in(key, 5)
    key_counts, key_full = jax.random.split(key)
    counts = jax.random.randint(key_counts, (DOCS,), 1, SEG + 1, dtype=jnp.int32)
    full_doc = jax.random.randint(key_full, (), 0, DOCS, dtype=jnp.int32)
    return jnp.where(jnp.arange(DOCS, dtype=jnp.int32) == full_doc, SEG, counts).astype(jnp.int32)


def block_levels(key, shape, cuts, smallest, top_value):
    loudness = 1.0
    for dim, parts in cuts:
        heights = jax.random.uniform(jax.random.fold_in(jax.random.fold_in(key, 6), dim), (parts,), jnp.float32, smallest / len(cuts), top_value / len(cuts))
        loudness = loudness * jnp.repeat(jnp.exp(heights), shape[dim] // parts).reshape((-1,) + (1,) * (len(shape) - 1 - dim))
    return loudness


def normal_values(rng, shape, spread, most, cuts=(), held_as=jnp.bfloat16):
    entries = jax.random.normal(rng, shape, jnp.float32) * spread
    if len(cuts) > 0:
        entries = block_levels(rng, shape, cuts, -0.22, 0.18) * entries
    return jnp.clip(entries, min=-most, max=most).astype(held_as)


def setup_inputs(seed: int = 0, part: int = 0) -> dict:
    seeds = jax.random.split(jax.random.key(seed), 8)
    part_splits = jax.random.split(jax.random.fold_in(seeds[7], part), 8)
    tokens = draw_tokens(jax.random.fold_in(jax.random.fold_in(seeds[7], part), 71), part)
    norm_gain = jnp.clip(1.0 + 0.1 * jax.random.normal(seeds[1], (D,), jnp.float32), 0.5, 1.5)
    gate_weight = normal_values(seeds[2], (D, HID), D ** -0.5, 0.046875, ((0, 16),))
    up_weight = normal_values(seeds[3], (D, HID), D ** -0.5, 0.046875, ((0, 16),))
    down_weight = normal_values(seeds[4], (HID, D), HID ** -0.5, 0.375, ((1, 16),))
    owner_rows = jax.random.permutation(seeds[5], N_WIDE).astype(jnp.int32)
    seg_counts = draw_seg_counts(jax.random.fold_in(jax.random.fold_in(seeds[7], part), 71), part)
    return {"tokens": tokens, "norm_gain": norm_gain, "gate_weight": gate_weight, "up_weight": up_weight, "down_weight": down_weight, "owner_rows": owner_rows, "seg_counts": seg_counts}


def reference(tokens, norm_gain, gate_weight, up_weight, down_weight, owner_rows, seg_counts):
    gate_logical = gate_weight.reshape(N_WIDE, BLOCK, HID)[owner_rows].reshape(D, HID)
    up_logical = up_weight.reshape(N_WIDE, BLOCK, HID)[owner_rows].reshape(D, HID)
    down_logical = down_weight.reshape(HID, N_WIDE, BLOCK)[:, owner_rows, :].reshape(HID, D)
    features = tokens.astype(jnp.float32)
    mean_square = lax.optimization_barrier(jnp.mean(features * features, axis=1, keepdims=True))
    normed = (features * lax.rsqrt(mean_square + 1e-05) * norm_gain[None, :]).astype(jnp.bfloat16)
    gate_sum = jnp.dot(normed, gate_logical, preferred_element_type=jnp.float32)
    up_sum = jnp.dot(normed, up_logical, preferred_element_type=jnp.float32)
    hidden = (jax.nn.silu(gate_sum) * up_sum).astype(jnp.bfloat16)
    product = jnp.dot(hidden, down_logical, preferred_element_type=jnp.float32).astype(jnp.bfloat16)
    position = jnp.arange(TOKENS, dtype=jnp.int32) % ROWS
    limits = jnp.repeat(seg_counts, ROWS) + MEM
    live_mask = (position < limits).astype(jnp.bfloat16)
    return product * live_mask[:, None]
```

```python
import functools

import jax
import jax.numpy as jnp
from jax import lax
from jax.experimental import pallas as pl
from jax.experimental.pallas import tpu as pltpu
from jax.sharding import PartitionSpec as P

MEM = 16
ALL = ("groups", "wide")
F32, BF16 = jnp.float32, jnp.bfloat16
VMEM = pl.BlockSpec(memory_space=pltpu.VMEM)
SMEM = pl.BlockSpec(memory_space=pltpu.SMEM)


def gathered(tokens, norm_gain, gate_weight, up_weight, down_weight, owner_rows, seg_counts):
    row_count, model_width = tokens.shape
    owners = lax.axis_size("wide")
    block_rows = model_width // owners
    indices = jnp.arange(owners, dtype=jnp.int32)
    holder = jnp.sum(
        indices[:, None] * (owner_rows[:, None] == indices[None, :]).astype(jnp.int32), axis=0
    )
    features = tokens.astype(F32)
    mean_square = jnp.mean(features * features, axis=1, keepdims=True)
    normed = (features * lax.rsqrt(mean_square + 1e-05) * norm_gain[None, :]).astype(BF16)
    stored = normed.reshape(row_count, owners, block_rows)[:, holder, :].reshape(
        row_count, model_width
    )

    def partial_product(portion):
        return jnp.dot(stored, portion, preferred_element_type=F32)

    gate_sum = partial_product(lax.all_gather(gate_weight, "wide", axis=0, tiled=True))
    up_sum = partial_product(lax.all_gather(up_weight, "wide", axis=0, tiled=True))
    hidden = (jax.nn.silu(gate_sum) * up_sum).astype(BF16)
    stored_out = jnp.dot(
        hidden,
        lax.all_gather(down_weight, "wide", axis=1, tiled=True),
        preferred_element_type=F32,
    ).astype(BF16)
    product = stored_out.reshape(row_count, owners, block_rows)[:, owner_rows, :].reshape(
        row_count, model_width
    )
    live_mask = (jnp.arange(row_count, dtype=jnp.int32) < MEM + seg_counts[0]).astype(BF16)
    return product * live_mask[:, None]


def norm_kernel(places_ref, tokens_ref, gain_ref, *rest):
    *outs, scale_ref = rest
    i = pl.program_id(0)
    per_quarter = pl.num_programs(0) // len(outs)
    width = outs[0].shape[2]

    @pl.when(i == 0)
    def _():
        total = jnp.zeros((tokens_ref.shape[0], 128), F32)
        for start in range(0, tokens_ref.shape[1], 128):
            part = tokens_ref[:, start : start + 128].astype(F32)
            total += part * part
        mean = jnp.sum(total, axis=1, keepdims=True) / tokens_ref.shape[1]
        scale_ref[...] = jnp.broadcast_to(lax.rsqrt(mean + 1e-05), scale_ref.shape)

    columns = pl.ds(pl.multiple_of(places_ref[i] * width, width), width)
    normed = tokens_ref[:, columns].astype(F32) * scale_ref[:, :1] * gain_ref[:, columns]
    for q, out in enumerate(outs):

        @pl.when(i // per_quarter == q)
        def _(out=out):
            out[0] = normed.astype(BF16)


def normed_quarters(tokens, gain, places, quarters):
    rows, model_width = tokens.shape
    blocks = places.shape[0]
    per_quarter = blocks // quarters
    width = model_width // blocks

    def out_spec(q):
        return pl.BlockSpec(
            (1, rows, width),
            lambda i, places: (jnp.clip(i - q * per_quarter, 0, per_quarter - 1), 0, 0),
        )

    return pl.pallas_call(
        norm_kernel,
        grid_spec=pltpu.PrefetchScalarGridSpec(
            num_scalar_prefetch=1,
            grid=(blocks,),
            in_specs=[
                pl.BlockSpec((rows, model_width), lambda i, places: (0, 0)),
                pl.BlockSpec((1, model_width), lambda i, places: (0, 0)),
            ],
            out_specs=[out_spec(q) for q in range(quarters)],
            scratch_shapes=[pltpu.VMEM((rows, 128), F32)],
        ),
        out_shape=[jax.ShapeDtypeStruct((per_quarter, rows, width), BF16)] * quarters,
        compiler_params=pltpu.CompilerParams(vmem_limit_bytes=20 << 20),
        cost_estimate=pl.CostEstimate(
            flops=6 * rows * model_width, bytes_accessed=4 * rows * model_width, transcendentals=0
        ),
        name="norm_quarters",
    )(places, tokens, gain.reshape(1, model_width))


def partial_kernel(count, types, where_ref, *refs):
    inputs, rest = refs[:count], refs[count:]
    outs = rest[-len(types) :]
    weights = rest[: -len(types)]
    half = len(weights) // 2
    hid = weights[0].shape[1]
    swap = where_ref[half]
    for rows, out, kind in zip(inputs, outs, types):
        sums = []
        for side in range(2):
            total = jnp.zeros((rows.shape[1], hid), F32)
            for j in range(half):
                total += jnp.dot(
                    rows[where_ref[j]], weights[side * half + j][...], preferred_element_type=F32
                )
            sums.append(total)
        mine, other = sums
        first = swap == 0
        out[:, :hid] = jnp.where(first, mine, other).astype(kind)
        out[:, hid:] = jnp.where(first, other, mine).astype(kind)


def partial_sums(where, inputs, weights, types):
    rows, hid = inputs[0].shape[1], weights[0].shape[1]
    depth = weights[0].shape[0] * len(weights) // 2
    return pl.pallas_call(
        functools.partial(partial_kernel, len(inputs), types),
        in_specs=[SMEM] + [VMEM] * (len(inputs) + len(weights)),
        out_specs=[VMEM] * len(inputs),
        out_shape=[jax.ShapeDtypeStruct((rows, 2 * hid), kind) for kind in types],
        compiler_params=pltpu.CompilerParams(vmem_limit_bytes=20 << 20),
        cost_estimate=pl.CostEstimate(
            flops=4 * len(inputs) * rows * depth * hid,
            bytes_accessed=2 * depth * (len(inputs) * rows + 2 * hid),
            transcendentals=0,
        ),
        name="partial_sums",
    )(where, *inputs, *weights)


def down_kernel(shapes, at_ref, live_ref, own, *refs):
    partials, weights, out = refs[:3], refs[3:-1], refs[-1]
    hid = own.shape[1] // 2
    total = own[...]
    for part in partials:
        total += part[...].astype(F32)
    gate, up = total[:, :hid], total[:, hid:]
    hidden = (gate / (1.0 + jnp.exp(-gate)) * up).astype(BF16)
    rows = lax.broadcasted_iota(jnp.int32, (out.shape[0], 1), 0)
    live = (rows < MEM + live_ref[0]).astype(F32)
    piece = 0
    for ref, stacked in zip(weights, shapes):
        for k in range(stacked):
            block = ref[k]
            width = block.shape[1]
            product = jnp.dot(hidden, block, preferred_element_type=F32).astype(BF16)
            columns = pl.ds(pl.multiple_of(at_ref[piece], 128), width)
            out[:, columns] = (product.astype(F32) * live).astype(BF16)
            piece += 1


def down_product(at, seg_counts, own, partials, weights, model_width):
    rows = own.shape[0]
    shapes = tuple(w.shape[0] for w in weights)
    hid = own.shape[1] // 2
    return pl.pallas_call(
        functools.partial(down_kernel, shapes),
        in_specs=[SMEM, SMEM] + [VMEM] * (1 + len(partials) + len(weights)),
        out_specs=VMEM,
        out_shape=jax.ShapeDtypeStruct((rows, model_width), BF16),
        compiler_params=pltpu.CompilerParams(vmem_limit_bytes=24 << 20),
        cost_estimate=pl.CostEstimate(
            flops=2 * rows * hid * model_width,
            bytes_accessed=2 * model_width * (rows + hid),
            transcendentals=rows * hid,
        ),
        name="down_product",
    )(at, seg_counts, own, *partials, *weights)


def split(groups, owners, tokens, norm_gain, gate_weight, up_weight, down_weight, owner_rows, seg_counts):
    model_width = tokens.shape[1]
    block = model_width // owners
    half = block // 2
    group, here = lax.axis_index("groups"), lax.axis_index("wide")
    core, across, near, far, other = (0, 1), (0, 2), (0, 4), (0, 8), (1, 0)
    both = (0, 3)

    def swap(value, way):
        pairs = [
            (g * owners + w, (g ^ way[0]) * owners + (w ^ way[1]))
            for g in range(groups)
            for w in range(owners)
        ]
        return lax.ppermute(value, ALL, pairs)

    first = group == 0
    indices = jnp.arange(owners, dtype=jnp.int32)
    holder = jnp.sum(
        indices[:, None] * (owner_rows[:, None] == indices[None, :]).astype(jnp.int32), axis=0
    )

    halves = (down_weight[:, :half], down_weight[:, half:])
    mine = jnp.where(first, halves[0], halves[1])
    rest = jnp.where(first, halves[1], halves[0])
    mine_x = swap(mine, across)
    rest_x = swap(mine_x, other)

    a0 = jnp.where(first, gate_weight, up_weight)
    b0 = jnp.where(first, up_weight, gate_weight)
    a1 = swap(a0, near)
    a2 = swap(a0, far)
    a3 = swap(a2, near)
    b1, b2, b3 = (swap(a, other) for a in (a1, a2, a3))

    turns = (3, 2, 1, 0)
    slots = jnp.concatenate(
        [(jnp.arange(owners // 4, dtype=jnp.int32) * 4 + ((here & 3) ^ turn)) for turn in turns]
    )
    t3, t2, t1, t0 = normed_quarters(tokens, norm_gain, holder[slots], 4)
    t3 = swap(t3, both)
    t2 = swap(t2, across)
    t1 = swap(t1, core)

    d0 = jnp.stack([mine, mine_x])
    d1 = swap(d0, near)
    d2 = swap(d0, far)
    d3 = swap(d2, near)
    e1, e2, e3 = (swap(d, other) for d in (d1, d2, d3))
    e0 = jnp.stack([rest, rest_x])

    z = here >> 2
    where = jnp.stack([z, z ^ 1, z ^ 2, z ^ 3, group]).astype(jnp.int32)
    weights = (a0, a1, a2, a3, b0, b1, b2, b3)
    p0, p1 = partial_sums(where, (t0, t1), weights, (F32, F32))
    p2, p3 = partial_sums(where, (t2, t3), weights, (BF16, BF16))
    p1 = swap(p1, core)
    p2 = swap(p2, across)
    p3 = swap(p3, both)

    downs = [d0, e0, d1, e1, d2, e2, d3, e3]
    downs = downs + [swap(d, core) for d in downs]
    at = []
    for turn in (0, 1):
        for hop in range(4):
            for plane in (group, 1 - group):
                for x in (0, 2):
                    at.append(holder[here ^ (4 * hop + x + turn)] * block + plane * half)
    return down_product(jnp.stack(at).astype(jnp.int32), seg_counts, p0, (p1, p2, p3), downs, model_width)


def solution(mesh):
    placed = (
        P(("groups", "wide"), None),
        P(),
        P("wide", None),
        P("wide", None),
        P(None, "wide"),
        P(),
        P(("groups", "wide")),
    )
    groups, owners = mesh.shape["groups"], mesh.shape["wide"]
    plan = functools.partial(split, groups, owners) if (groups, owners) == (2, 16) else gathered
    return jax.shard_map(
        plan, mesh=mesh, in_specs=placed, out_specs=P(("groups", "wide"), None), check_vma=False
    )
```

```python
import functools

import jax
import jax.numpy as jnp
from jax import lax
from jax.experimental import pallas as pl
from jax.experimental.pallas import tpu as pltpu
from jax.sharding import PartitionSpec as P

MEM = 16
FULL = 60 << 20
ALL = ("groups", "wide")
F32, BF16 = jnp.float32, jnp.bfloat16
VMEM = pl.BlockSpec(memory_space=pltpu.VMEM)
SMEM = pl.BlockSpec(memory_space=pltpu.SMEM)
HBM = pl.BlockSpec(memory_space=pltpu.HBM)


def gathered(tokens, norm_gain, gate_weight, up_weight, down_weight, owner_rows, seg_counts):
    row_count, model_width = tokens.shape
    owners = lax.axis_size("wide")
    block_rows = model_width // owners
    indices = jnp.arange(owners, dtype=jnp.int32)
    holder = jnp.sum(
        indices[:, None] * (owner_rows[:, None] == indices[None, :]).astype(jnp.int32), axis=0
    )
    features = tokens.astype(F32)
    mean_square = jnp.mean(features * features, axis=1, keepdims=True)
    normed = (features * lax.rsqrt(mean_square + 1e-05) * norm_gain[None, :]).astype(BF16)
    stored = normed.reshape(row_count, owners, block_rows)[:, holder, :].reshape(
        row_count, model_width
    )

    def partial_product(portion):
        return jnp.dot(stored, portion, preferred_element_type=F32)

    gate_sum = partial_product(lax.all_gather(gate_weight, "wide", axis=0, tiled=True))
    up_sum = partial_product(lax.all_gather(up_weight, "wide", axis=0, tiled=True))
    hidden = (jax.nn.silu(gate_sum) * up_sum).astype(BF16)
    stored_out = jnp.dot(
        hidden,
        lax.all_gather(down_weight, "wide", axis=1, tiled=True),
        preferred_element_type=F32,
    ).astype(BF16)
    product = stored_out.reshape(row_count, owners, block_rows)[:, owner_rows, :].reshape(
        row_count, model_width
    )
    live_mask = (jnp.arange(row_count, dtype=jnp.int32) < MEM + seg_counts[0]).astype(BF16)
    return product * live_mask[:, None]


def norm_kernel(firsts, places_ref, tokens_ref, gain_ref, *rest):
    *outs, scale_ref = rest
    i = pl.program_id(0)
    width = outs[0].shape[2]

    @pl.when(i == 0)
    def _():
        total = jnp.zeros((tokens_ref.shape[0], 128), F32)
        for start in range(0, tokens_ref.shape[1], 128):
            part = tokens_ref[:, start : start + 128].astype(F32)
            total += part * part
        mean = jnp.sum(total, axis=1, keepdims=True) / tokens_ref.shape[1]
        scale_ref[...] = jnp.broadcast_to(lax.rsqrt(mean + 1e-05), scale_ref.shape)

    columns = pl.ds(pl.multiple_of(places_ref[i] * width, width), width)
    normed = tokens_ref[:, columns].astype(F32) * scale_ref[:, :1] * gain_ref[:, columns]
    for q, out in enumerate(outs):

        @pl.when((i >= firsts[q]) & (i < firsts[q + 1]))
        def _(out=out):
            out[0] = normed.astype(BF16)


def normed_blocks(tokens, gain, places, counts):
    rows, model_width = tokens.shape
    blocks = places.shape[0]
    width = model_width // blocks
    firsts = tuple(sum(counts[:q]) for q in range(len(counts) + 1))

    def out_spec(q):
        return pl.BlockSpec(
            (1, rows, width),
            lambda i, places: (jnp.clip(i - firsts[q], 0, counts[q] - 1), 0, 0),
        )

    return pl.pallas_call(
        functools.partial(norm_kernel, firsts),
        grid_spec=pltpu.PrefetchScalarGridSpec(
            num_scalar_prefetch=1,
            grid=(blocks,),
            in_specs=[
                pl.BlockSpec((rows, model_width), lambda i, places: (0, 0)),
                pl.BlockSpec((1, model_width), lambda i, places: (0, 0)),
            ],
            out_specs=[out_spec(q) for q in range(len(counts))],
            scratch_shapes=[pltpu.VMEM((rows, 128), F32)],
        ),
        out_shape=[pltpu.HBM((count, rows, width), BF16) for count in counts],
        compiler_params=pltpu.CompilerParams(vmem_limit_bytes=20 << 20),
        cost_estimate=pl.CostEstimate(
            flops=6 * rows * model_width, bytes_accessed=4 * rows * model_width, transcendentals=0
        ),
        name="norm_blocks",
    )(places, tokens, gain.reshape(1, model_width))


def fetch(refs, buffers, sem):
    copies = [pltpu.make_async_copy(r, v, sem.at[i]) for i, (r, v) in enumerate(zip(refs, buffers))]
    for copy in copies:
        copy.start()
    return copies


def partial_kernel(count, types, where_ref, *refs):
    rows, weights, sem = refs[-count - 2 : -2], refs[-2], refs[-1]
    outs = refs[-count - 2 - len(types) : -count - 2]
    given = refs[: -count - 2 - len(types)]
    half = (len(given) - count) // 2
    hid = weights.shape[2]
    order = [count + i + side * half for i in range(half) for side in range(2)]
    copies = fetch(
        [ref.at[:half] for ref in given[:count]] + [given[i] for i in order],
        list(rows) + [weights.at[i - count] for i in order],
        sem,
    )
    sums = [[jnp.zeros((ref.shape[1], hid), F32) for _ in range(2)] for ref in rows]
    for copy in copies[:count]:
        copy.wait()
    for n, i in enumerate(order):
        copies[count + n].wait()
        side, j = divmod(i - count, half)
        for ref, pair in zip(rows, sums):
            pair[side] += jnp.dot(
                ref[where_ref[j]], weights[i - count], preferred_element_type=F32
            )
    first = where_ref[half] == 0
    for (mine, other), out, kind in zip(sums, outs, types):
        out[:, :hid] = jnp.where(first, mine, other).astype(kind)
        out[:, hid:] = jnp.where(first, other, mine).astype(kind)


def partial_sums(where, inputs, weights, types):
    rows, hid = inputs[0].shape[1], weights[0].shape[1]
    depth = weights[0].shape[0] * len(weights) // 2
    return pl.pallas_call(
        functools.partial(partial_kernel, len(inputs), types),
        in_specs=[SMEM] + [HBM] * (len(inputs) + len(weights)),
        out_specs=[VMEM] * len(inputs),
        out_shape=[jax.ShapeDtypeStruct((rows, 2 * hid), kind) for kind in types],
        scratch_shapes=[pltpu.VMEM((len(weights) // 2,) + v.shape[1:], v.dtype) for v in inputs]
        + [
            pltpu.VMEM((len(weights),) + weights[0].shape, BF16),
            pltpu.SemaphoreType.DMA((len(inputs) + len(weights),)),
        ],
        compiler_params=pltpu.CompilerParams(vmem_limit_bytes=FULL),
        cost_estimate=pl.CostEstimate(
            flops=4 * len(inputs) * rows * depth * hid,
            bytes_accessed=2 * depth * (len(inputs) * rows + 2 * hid),
            transcendentals=0,
        ),
        name="partial_sums",
    )(where, *inputs, *weights)


def down_kernel(pieces, holder_ref, info_ref, live_ref, own, *refs):
    count = len(pieces)
    partials, weights, out = refs[:3], refs[3 : 3 + count], refs[3 + count]
    held, sem, results, out_sem = refs[4 + count : 4 + 2 * count], *refs[4 + 2 * count :]
    copies = fetch(weights, held, sem)
    group, here = info_ref[0], info_ref[1]
    block = out.shape[1] // holder_ref.shape[0]
    hid = own.shape[1] // 2
    total = own[...]
    for part in partials:
        total += part[...].astype(F32)
    gate, up = total[:, :hid], total[:, hid:]
    hidden = (gate / (1.0 + jnp.exp(-gate)) * up).astype(BF16)
    rows = lax.broadcasted_iota(jnp.int32, (out.shape[0], 1), 0)
    live = (rows < MEM + live_ref[0]).astype(F32)
    start, sent = 0, []
    for copy, ref, parts in zip(copies, held, pieces):
        copy.wait()
        for k, (turn, plane) in enumerate(parts):
            width = ref.shape[2]
            product = jnp.dot(hidden, ref[k], preferred_element_type=F32).astype(BF16)
            results[:, start : start + width] = (product.astype(F32) * live).astype(BF16)
            side = group ^ plane if width < block else 0
            place = holder_ref[here ^ turn] * block + side * width
            sent.append(
                pltpu.make_async_copy(
                    results.at[:, start : start + width],
                    out.at[:, pl.ds(pl.multiple_of(place, 128), width)],
                    out_sem.at[len(sent)],
                )
            )
            sent[-1].start()
            start += width
    for copy in sent:
        copy.wait()


def down_product(holder, info, seg_counts, own, partials, downs, model_width):
    rows = own.shape[0]
    weights, pieces = zip(*downs)
    hid = own.shape[1] // 2
    return pl.pallas_call(
        functools.partial(down_kernel, pieces),
        in_specs=[SMEM, SMEM, SMEM] + [VMEM] * (1 + len(partials)) + [HBM] * len(weights),
        out_specs=HBM,
        out_shape=jax.ShapeDtypeStruct((rows, model_width), BF16),
        scratch_shapes=[pltpu.VMEM(w.shape, w.dtype) for w in weights]
        + [
            pltpu.SemaphoreType.DMA((len(weights),)),
            pltpu.VMEM((rows, model_width), BF16),
            pltpu.SemaphoreType.DMA((sum(len(p) for p in pieces),)),
        ],
        compiler_params=pltpu.CompilerParams(vmem_limit_bytes=FULL),
        cost_estimate=pl.CostEstimate(
            flops=2 * rows * hid * model_width,
            bytes_accessed=2 * model_width * (rows + hid),
            transcendentals=rows * hid,
        ),
        name="down_product",
    )(holder, info, seg_counts, own, *partials, *weights)


def stack_kernel(a_ref, b_ref, out_ref):
    out_ref[0] = a_ref[0]
    out_ref[1] = b_ref[0]


def stacked(a, b, flops):
    return pl.pallas_call(
        stack_kernel,
        out_shape=jax.ShapeDtypeStruct((2,) + a.shape[1:], a.dtype),
        compiler_params=pltpu.CompilerParams(vmem_limit_bytes=8 << 20),
        cost_estimate=pl.CostEstimate(flops=flops, bytes_accessed=4 * a.size, transcendentals=0),
        name="stack_halves",
    )(a, b)


def after(value, *others):
    return lax.optimization_barrier((value, *others))[0]


def split(groups, owners, tokens, norm_gain, gate_weight, up_weight, down_weight, owner_rows, seg_counts):
    model_width = tokens.shape[1]
    half = model_width // owners // 2
    group, here = lax.axis_index("groups"), lax.axis_index("wide")
    core, across, near, far, other = (0, 1), (0, 2), (0, 4), (0, 8), (1, 0)
    both = (0, 3)

    def swap(value, way):
        pairs = [
            (g * owners + w, (g ^ way[0]) * owners + (w ^ way[1]))
            for g in range(groups)
            for w in range(owners)
        ]
        return lax.ppermute(value, ALL, pairs)

    first = group == 0
    indices = jnp.arange(owners, dtype=jnp.int32)
    holder = jnp.sum(
        indices[:, None] * (owner_rows[:, None] == indices[None, :]).astype(jnp.int32), axis=0
    )
    info = jnp.stack([group, here]).astype(jnp.int32)

    a0 = jnp.where(first, gate_weight, up_weight)
    b0 = jnp.where(first, up_weight, gate_weight)
    halves = (down_weight[:, :half], down_weight[:, half:])
    mine = jnp.where(first, halves[0], halves[1])[None]
    rest = jnp.where(first, halves[1], halves[0])[None]

    a1 = swap(a0, near)
    a2 = swap(a0, far)
    mine_x = swap(mine, across)

    quarter = owners // 4
    slots = jnp.concatenate(
        [jnp.arange(quarter, dtype=jnp.int32) * 4 + ((here & 3) ^ turn) for turn in (2, 3, 1, 0)]
    )
    t23, t1, t0 = normed_blocks(tokens, norm_gain, holder[slots], (2 * quarter, quarter, quarter))
    r23 = swap(after(t23, mine_x), across)
    r1 = swap(t1, core)
    rest_x = swap(mine_x, other)
    d0 = stacked(after(mine, a1, a2), mine_x, 10**11)

    b1 = swap(after(a1, a2, rest_x), other)
    a3 = swap(after(a2, a1), near)
    d2 = swap(d0, far)
    b2 = swap(after(a2, b1), other)

    b3 = swap(after(a3, b2), other)
    d3 = swap(after(d2, a3), near)
    d1 = swap(after(down_weight[None], a3, d2), near)
    r3 = swap(after(r23, d2, b2)[quarter:], core)
    e2 = swap(after(d2, b3), other)

    z = here >> 2
    where = jnp.stack([z, z ^ 1, z ^ 2, z ^ 3, group]).astype(jnp.int32)
    weights = (a0, a1, a2, a3, b0, b1, b2, b3)
    p2, p3 = partial_sums(where, (r23, r3), weights, (BF16, BF16))
    q2 = swap(p2, across)
    q3 = swap(p3, both)
    p0, p1 = partial_sums(where, (t0, after(r1, p2)), weights, (F32, F32))
    q1 = swap(p1, core)

    e3 = swap(after(d3, e2, p1), other)
    x1 = swap(after(d1, q2, q3), across)

    def pieces(turn, plane):
        return ((turn, plane), (turn ^ 2, plane))

    downs = [
        (down_weight[None], ((0, 0),)),
        (mine_x, ((2, 0),)),
        (rest_x, ((2, 1),)),
        (d2, pieces(8, 0)),
        (d3, pieces(12, 0)),
        (d1, ((4, 0),)),
        (e2, pieces(8, 1)),
        (x1, ((6, 0),)),
        (e3, pieces(12, 1)),
    ]
    crossed = [(swap(w, core), tuple((turn ^ 1, plane) for turn, plane in p)) for w, p in downs]
    downs = downs + crossed
    return down_product(holder, info, seg_counts, p0, (q1, q2, q3), downs, model_width)


def solution(mesh):
    placed = (
        P(("groups", "wide"), None),
        P(),
        P("wide", None),
        P("wide", None),
        P(None, "wide"),
        P(),
        P(("groups", "wide")),
    )
    groups, owners = mesh.shape["groups"], mesh.shape["wide"]
    plan = functools.partial(split, groups, owners) if (groups, owners) == (2, 16) else gathered
    return jax.shard_map(
        plan, mesh=mesh, in_specs=placed, out_specs=P(("groups", "wide"), None), check_vma=False
    )
```

```python
import functools

import jax
import jax.numpy as jnp
from jax import lax
from jax.experimental import pallas as pl
from jax.experimental.pallas import tpu as pltpu
from jax.sharding import PartitionSpec as P

MEM = 16
FULL = 60 << 20
ALL = ("groups", "wide")
F32, BF16 = jnp.float32, jnp.bfloat16
VMEM = pl.BlockSpec(memory_space=pltpu.VMEM)
SMEM = pl.BlockSpec(memory_space=pltpu.SMEM)
HBM = pl.BlockSpec(memory_space=pltpu.HBM)


def gathered(tokens, norm_gain, gate_weight, up_weight, down_weight, owner_rows, seg_counts):
    row_count, model_width = tokens.shape
    owners = lax.axis_size("wide")
    block_rows = model_width // owners
    indices = jnp.arange(owners, dtype=jnp.int32)
    holder = jnp.sum(
        indices[:, None] * (owner_rows[:, None] == indices[None, :]).astype(jnp.int32), axis=0
    )
    features = tokens.astype(F32)
    mean_square = jnp.mean(features * features, axis=1, keepdims=True)
    normed = (features * lax.rsqrt(mean_square + 1e-05) * norm_gain[None, :]).astype(BF16)
    stored = normed.reshape(row_count, owners, block_rows)[:, holder, :].reshape(
        row_count, model_width
    )

    def partial_product(portion):
        return jnp.dot(stored, portion, preferred_element_type=F32)

    gate_sum = partial_product(lax.all_gather(gate_weight, "wide", axis=0, tiled=True))
    up_sum = partial_product(lax.all_gather(up_weight, "wide", axis=0, tiled=True))
    hidden = (jax.nn.silu(gate_sum) * up_sum).astype(BF16)
    stored_out = jnp.dot(
        hidden,
        lax.all_gather(down_weight, "wide", axis=1, tiled=True),
        preferred_element_type=F32,
    ).astype(BF16)
    product = stored_out.reshape(row_count, owners, block_rows)[:, owner_rows, :].reshape(
        row_count, model_width
    )
    live_mask = (jnp.arange(row_count, dtype=jnp.int32) < MEM + seg_counts[0]).astype(BF16)
    return product * live_mask[:, None]


def norm_kernel(owner_ref, tokens_ref, gain_ref, *rest):
    (own, near, far), (held, made, scale_ref, in_sem, out_sem) = rest[:3], rest[3:]
    here = lax.axis_index("wide")
    rows, model_width = held.shape
    blocks = owner_ref.shape[0]
    width = model_width // blocks
    step = rows // in_sem.shape[0]
    outs = (own, near, far, far.at[blocks // 4 :])
    copies = [
        pltpu.make_async_copy(
            tokens_ref.at[r : r + step], held.at[r : r + step], in_sem.at[r // step]
        )
        for r in range(0, rows, step)
    ]
    for copy in copies:
        copy.start()
    for r, copy in zip(range(0, rows, step), copies):
        copy.wait()
        total = jnp.zeros((step, 128), F32)
        for start in range(0, model_width, 128):
            part = held[r : r + step, start : start + 128].astype(F32)
            total += part * part
        mean = jnp.sum(total, axis=1, keepdims=True) / model_width
        scale_ref[r : r + step] = jnp.broadcast_to(lax.rsqrt(mean + 1e-05), (step, 128))
    scale = scale_ref[:, :1]
    for p in range(blocks):
        columns = slice(p * width, (p + 1) * width)
        made[p] = (held[:, columns].astype(F32) * scale * gain_ref[:, columns]).astype(BF16)
        stored = owner_ref[p]
        for turn, out in enumerate(outs):

            @pl.when(((stored ^ here) & 3) == turn)
            def _(out=out, p=p, stored=stored):
                pltpu.make_async_copy(made.at[p], out.at[stored >> 2], out_sem.at[p]).start()

    for p in range(blocks):
        pltpu.make_async_copy(made.at[p], outs[0].at[0], out_sem.at[p]).wait()


def normed_quarters(tokens, gain, owner_rows):
    rows, model_width = tokens.shape
    blocks = owner_rows.shape[0]
    width = model_width // blocks
    return pl.pallas_call(
        norm_kernel,
        in_specs=[SMEM, HBM, VMEM],
        out_specs=[HBM] * 3,
        out_shape=[pltpu.HBM((n * blocks // 4, rows, width), BF16) for n in (1, 1, 2)],
        scratch_shapes=[
            pltpu.VMEM((rows, model_width), BF16),
            pltpu.VMEM((blocks, rows, width), BF16),
            pltpu.VMEM((rows, 128), F32),
            pltpu.SemaphoreType.DMA((rows // 16,)),
            pltpu.SemaphoreType.DMA((blocks,)),
        ],
        compiler_params=pltpu.CompilerParams(vmem_limit_bytes=FULL),
        cost_estimate=pl.CostEstimate(
            flops=6 * rows * model_width, bytes_accessed=4 * rows * model_width, transcendentals=0
        ),
        name="norm_quarters",
    )(owner_rows, tokens, gain.reshape(1, model_width))


def fetch(pairs, sem):
    copies = [pltpu.make_async_copy(r, v, sem.at[i]) for i, (r, v) in enumerate(pairs)]
    for copy in copies:
        copy.start()
    return copies


def partial_kernel(given, kinds, *refs):
    outs, (rows, held, mine, other, row_sem, sem) = refs[-6 - len(kinds) : -6], refs[-6:]
    inputs, weights = refs[:given], refs[given : -6 - len(kinds)]
    z, plane = lax.axis_index("wide") >> 2, lax.axis_index("groups")
    size = inputs[0].shape[1]
    hid = held.shape[2]
    hops = len(weights) // 2
    parts = [ref.at[: rows.shape[0]] for ref in inputs]
    row_copies = fetch(
        [(part, rows.at[:, k * size : (k + 1) * size]) for k, part in enumerate(parts)], row_sem
    )
    copies = fetch([(ref, held.at[i]) for i, ref in enumerate(weights)], sem)
    for copy in row_copies:
        copy.wait()
    first = plane == 0
    for hop in range(hops):
        part = rows[z ^ hop]
        for side, total in enumerate((mine, other)):
            i = 2 * hop + side
            copies[i].wait()
            product = jnp.dot(part, held[i], preferred_element_type=F32)
            total[...] = product if hop == 0 else total[...] + product
        if hop == 0:
            gate, up = mine[...], other[...]
            mine[...] = jnp.where(first, gate, up)
            other[...] = jnp.where(first, up, gate)
    for k, (out, kind) in enumerate(zip(outs, kinds)):
        a, b = mine[k * size : (k + 1) * size], other[k * size : (k + 1) * size]
        out[:, :hid] = jnp.where(first, a, b).astype(kind)
        out[:, hid:] = jnp.where(first, b, a).astype(kind)


def partial_sums(inputs, weights, kinds):
    count = len(kinds)
    hops, rows, depth = inputs[0].shape
    hid = weights[0].shape[1]
    return pl.pallas_call(
        functools.partial(partial_kernel, len(inputs), kinds),
        in_specs=[HBM] * (len(inputs) + len(weights)),
        out_specs=[VMEM] * count,
        out_shape=[jax.ShapeDtypeStruct((rows, 2 * hid), kind) for kind in kinds],
        scratch_shapes=[
            pltpu.VMEM((hops, count * rows, depth), BF16),
            pltpu.VMEM((len(weights), depth, hid), BF16),
            pltpu.VMEM((count * rows, hid), F32),
            pltpu.VMEM((count * rows, hid), F32),
            pltpu.SemaphoreType.DMA((count,)),
            pltpu.SemaphoreType.DMA((len(weights),)),
        ],
        compiler_params=pltpu.CompilerParams(vmem_limit_bytes=FULL),
        cost_estimate=pl.CostEstimate(
            flops=4 * hops * count * rows * depth * hid,
            bytes_accessed=2 * hops * depth * (count * rows + 2 * hid),
            transcendentals=0,
        ),
        name="partial_sums",
    )(*inputs, *weights)


def multiply_out(hidden, pieces, owner_ref, live_ref, weights, out, held, sem, results, out_sem, places):
    copies = fetch(list(zip(weights, held)), sem)
    group, here = lax.axis_index("groups"), lax.axis_index("wide")
    blocks = owner_ref.shape[0]
    block = out.shape[1] // blocks
    for p in range(blocks):
        places[owner_ref[p]] = p * block
    rows = lax.broadcasted_iota(jnp.int32, (out.shape[0], 1), 0)
    live = (rows < MEM + live_ref[0]).astype(F32)
    hidden = hidden()
    start, sent = 0, []
    for copy, ref, parts in zip(copies, held, pieces):
        copy.wait()
        for k, (turn, plane) in enumerate(parts):
            width = ref.shape[2]
            product = jnp.dot(hidden, ref[k], preferred_element_type=F32).astype(BF16)
            results[:, start : start + width] = (product.astype(F32) * live).astype(BF16)
            side = group ^ plane if width < block else 0
            place = places[here ^ turn] + side * width
            sent.append(
                pltpu.make_async_copy(
                    results.at[:, start : start + width],
                    out.at[:, pl.ds(pl.multiple_of(place, 128), width)],
                    out_sem.at[len(sent)],
                )
            )
            sent[-1].start()
            start += width
    for copy in sent:
        copy.wait()


def first_kernel(pieces, owner_ref, live_ref, own, *refs):
    count = len(pieces)
    partials, weights, (out, hidden_ref) = refs[:3], refs[3 : 3 + count], refs[3 + count : 5 + count]
    held, rest = refs[5 + count : 5 + 2 * count], refs[5 + 2 * count :]
    hid = own.shape[1] // 2

    def hidden():
        total = own[...]
        for part in partials:
            total += part[...].astype(F32)
        gate, up = total[:, :hid], total[:, hid:]
        hidden_ref[...] = (gate / (1.0 + jnp.exp(-gate)) * up).astype(BF16)
        return hidden_ref[...]

    multiply_out(hidden, pieces, owner_ref, live_ref, weights, out, held, *rest)


def second_kernel(pieces, owner_ref, live_ref, hidden_ref, _, *refs):
    count = len(pieces)
    weights, out, held, rest = refs[:count], refs[count], refs[count + 1 : 2 * count + 1], refs[2 * count + 1 :]
    multiply_out(lambda: hidden_ref[...], pieces, owner_ref, live_ref, weights, out, held, *rest)


def down_call(kernel, name, owner_rows, seg_counts, operands, specs, downs, outs, out_specs, aliases):
    weights, pieces = zip(*downs)
    rows = outs[0].shape[0]
    columns = sum(w.size for w in weights) // weights[0].shape[1]
    return pl.pallas_call(
        functools.partial(kernel, pieces),
        in_specs=[SMEM, SMEM] + specs + [HBM] * len(weights),
        out_specs=out_specs,
        out_shape=outs,
        scratch_shapes=[pltpu.VMEM(w.shape, w.dtype) for w in weights]
        + [
            pltpu.SemaphoreType.DMA((len(weights),)),
            pltpu.VMEM((rows, columns), BF16),
            pltpu.SemaphoreType.DMA((sum(len(p) for p in pieces),)),
            pltpu.SMEM(owner_rows.shape, jnp.int32),
        ],
        input_output_aliases=aliases,
        compiler_params=pltpu.CompilerParams(vmem_limit_bytes=FULL),
        cost_estimate=pl.CostEstimate(
            flops=2 * rows * weights[0].shape[1] * columns,
            bytes_accessed=2 * columns * (rows + weights[0].shape[1]),
            transcendentals=0,
        ),
        name=name,
    )(owner_rows, seg_counts, *operands, *weights)


def stack_kernel(a_ref, b_ref, out_ref):
    out_ref[0] = a_ref[0]
    out_ref[1] = b_ref[0]


def stacked(a, b, flops):
    return pl.pallas_call(
        stack_kernel,
        out_shape=jax.ShapeDtypeStruct((2,) + a.shape[1:], a.dtype),
        compiler_params=pltpu.CompilerParams(vmem_limit_bytes=8 << 20),
        cost_estimate=pl.CostEstimate(flops=flops, bytes_accessed=4 * a.size, transcendentals=0),
        name="stack_halves",
    )(a, b)


def after(value, *others):
    return lax.optimization_barrier((value, *others))[0]


def split(groups, owners, tokens, norm_gain, gate_weight, up_weight, down_weight, owner_rows, seg_counts):
    model_width = tokens.shape[1]
    half = model_width // owners // 2
    group, here = lax.axis_index("groups"), lax.axis_index("wide")
    core, across, near, far, other = (0, 1), (0, 2), (0, 4), (0, 8), (1, 0)
    both = (0, 3)

    def swap(value, way):
        pairs = [
            (g * owners + w, (g ^ way[0]) * owners + (w ^ way[1]))
            for g in range(groups)
            for w in range(owners)
        ]
        return lax.ppermute(value, ALL, pairs)

    first = group == 0
    a0 = jnp.where(first, gate_weight, up_weight)
    mine = jnp.where(first, down_weight[:, :half], down_weight[:, half:])[None]

    a1 = swap(a0, near)
    a2 = swap(a0, far)
    mine_x = swap(mine, across)

    t0, t1, t2 = normed_quarters(tokens, norm_gain, owner_rows)
    r2 = swap(t2, across)
    r1 = swap(t1, core)
    rest_x = swap(after(mine_x, t2), other)
    d0 = stacked(after(mine, a1, a2, t2), mine_x, 10**11)

    b1 = swap(after(a1, d0, rest_x), other)
    a3 = swap(after(a2, d0), near)
    d2 = swap(d0, far)
    b2 = swap(after(a2, d0, rest_x), other)

    b3 = swap(after(a3, b1, b2, d2), other)
    d3 = swap(after(d2, a3), near)
    d1 = swap(after(down_weight[None], d3), near)
    e2 = swap(after(d2, b3), other)

    r3 = swap(after(r2, b3, d3)[owners // 4 :], core)
    def crossed(downs):
        return downs + [
            (swap(w, core), tuple((turn ^ 1, plane) for turn, plane in p)) for w, p in downs
        ]

    crossed_first = crossed(
        [
            (down_weight[None], ((0, 0),)),
            (mine_x, ((2, 0),)),
            (rest_x, ((2, 1),)),
            (d2, ((8, 0), (10, 0))),
        ]
    )
    weights = (gate_weight, up_weight, a1, b1, a2, b2, a3, b3)
    p0, p1, p2, p3 = partial_sums(
        (t0, after(r1, *(w for w, _ in crossed_first)), r2, r3), weights, (F32, F32, BF16, BF16)
    )
    q1 = swap(p1, core)
    q2 = swap(p2, across)
    q3 = swap(p3, both)

    e3 = swap(after(d3, e2, p1), other)
    x1 = swap(after(d1, q2, q3), across)

    early = crossed_first + crossed(
        [
            (after(e2, q2), ((8, 1), (10, 1))),
            (after(d3, q2), ((12, 0), (14, 0))),
            (after(d1, q2), ((4, 0),)),
        ]
    )
    out = pltpu.HBM(tokens.shape, BF16)
    rows, hid = tokens.shape[0], gate_weight.shape[1]
    product, hidden = down_call(
        first_kernel, "down_first", owner_rows, seg_counts, (p0, q1, q2, q3), [VMEM] * 4, early,
        [out, jax.ShapeDtypeStruct((rows, hid), BF16)], [HBM, VMEM], {},
    )
    late = crossed([(after(x1, hidden), ((6, 0),)), (after(e3, hidden), ((12, 1), (14, 1)))])
    return down_call(
        second_kernel, "down_second", owner_rows, seg_counts, (hidden, product), [VMEM, HBM], late,
        [out], [HBM], {3: 0},
    )[0]


def solution(mesh):
    placed = (
        P(("groups", "wide"), None),
        P(),
        P("wide", None),
        P("wide", None),
        P(None, "wide"),
        P(),
        P(("groups", "wide")),
    )
    groups, owners = mesh.shape["groups"], mesh.shape["wide"]
    plan = functools.partial(split, groups, owners) if (groups, owners) == (2, 16) else gathered
    return jax.shard_map(
        plan, mesh=mesh, in_specs=placed, out_specs=P(("groups", "wide"), None), check_vma=False
    )
```

```python
import functools

import jax
import jax.numpy as jnp
from jax import lax
from jax.experimental import pallas as pl
from jax.experimental.pallas import tpu as pltpu
from jax.sharding import PartitionSpec as P

MEM = 16
FULL = 60 << 20
ALL = ("groups", "wide")
F32, BF16 = jnp.float32, jnp.bfloat16
VMEM = pl.BlockSpec(memory_space=pltpu.VMEM)
SMEM = pl.BlockSpec(memory_space=pltpu.SMEM)
HBM = pl.BlockSpec(memory_space=pltpu.HBM)


def gathered(tokens, norm_gain, gate_weight, up_weight, down_weight, owner_rows, seg_counts):
    row_count, model_width = tokens.shape
    owners = lax.axis_size("wide")
    block_rows = model_width // owners
    indices = jnp.arange(owners, dtype=jnp.int32)
    holder = jnp.sum(
        indices[:, None] * (owner_rows[:, None] == indices[None, :]).astype(jnp.int32), axis=0
    )
    features = tokens.astype(F32)
    mean_square = jnp.mean(features * features, axis=1, keepdims=True)
    normed = (features * lax.rsqrt(mean_square + 1e-05) * norm_gain[None, :]).astype(BF16)
    stored = normed.reshape(row_count, owners, block_rows)[:, holder, :].reshape(
        row_count, model_width
    )

    def partial_product(portion):
        return jnp.dot(stored, portion, preferred_element_type=F32)

    gate_sum = partial_product(lax.all_gather(gate_weight, "wide", axis=0, tiled=True))
    up_sum = partial_product(lax.all_gather(up_weight, "wide", axis=0, tiled=True))
    hidden = (jax.nn.silu(gate_sum) * up_sum).astype(BF16)
    stored_out = jnp.dot(
        hidden,
        lax.all_gather(down_weight, "wide", axis=1, tiled=True),
        preferred_element_type=F32,
    ).astype(BF16)
    product = stored_out.reshape(row_count, owners, block_rows)[:, owner_rows, :].reshape(
        row_count, model_width
    )
    live_mask = (jnp.arange(row_count, dtype=jnp.int32) < MEM + seg_counts[0]).astype(BF16)
    return product * live_mask[:, None]


def norm_kernel(owner_ref, tokens_ref, gain_ref, *rest):
    (own, near, far), (held, made, scale_ref, in_sem, out_sem) = rest[:3], rest[3:]
    here = lax.axis_index("wide")
    rows, model_width = held.shape
    blocks = owner_ref.shape[0]
    width = model_width // blocks
    step = rows // in_sem.shape[0]
    outs = (own, near, far, far.at[blocks // 4 :])
    copies = [
        pltpu.make_async_copy(
            tokens_ref.at[r : r + step], held.at[r : r + step], in_sem.at[r // step]
        )
        for r in range(0, rows, step)
    ]
    for copy in copies:
        copy.start()
    for r, copy in zip(range(0, rows, step), copies):
        copy.wait()
        parts = [jnp.zeros((step, 128), F32) for _ in range(8)]
        for start in range(0, model_width, 128):
            part = held[r : r + step, start : start + 128].astype(F32)
            parts[start // 128 % 8] += part * part
        mean = jnp.sum(sum(parts), axis=1, keepdims=True) / model_width
        scale_ref[r : r + step] = jnp.broadcast_to(lax.rsqrt(mean + 1e-05), (step, 128))
    scale = scale_ref[...]
    for p in range(blocks):
        for start in range(0, width, 128):
            columns = slice(p * width + start, p * width + start + 128)
            normed = held[:, columns].astype(F32) * scale * gain_ref[:, columns]
            made[p, :, start : start + 128] = normed.astype(BF16)
        stored = owner_ref[p]
        for turn, out in enumerate(outs):

            @pl.when(((stored ^ here) & 3) == turn)
            def _(out=out, p=p, stored=stored):
                pltpu.make_async_copy(made.at[p], out.at[stored >> 2], out_sem.at[p]).start()

    for p in range(blocks):
        pltpu.make_async_copy(made.at[p], outs[0].at[0], out_sem.at[p]).wait()


def normed_quarters(tokens, gain, owner_rows):
    rows, model_width = tokens.shape
    blocks = owner_rows.shape[0]
    width = model_width // blocks
    return pl.pallas_call(
        norm_kernel,
        in_specs=[SMEM, HBM, VMEM],
        out_specs=[HBM] * 3,
        out_shape=[pltpu.HBM((n * blocks // 4, rows, width), BF16) for n in (1, 1, 2)],
        scratch_shapes=[
            pltpu.VMEM((rows, model_width), BF16),
            pltpu.VMEM((blocks, rows, width), BF16),
            pltpu.VMEM((rows, 128), F32),
            pltpu.SemaphoreType.DMA((rows // 16,)),
            pltpu.SemaphoreType.DMA((blocks,)),
        ],
        compiler_params=pltpu.CompilerParams(vmem_limit_bytes=FULL),
        cost_estimate=pl.CostEstimate(
            flops=6 * rows * model_width, bytes_accessed=4 * rows * model_width, transcendentals=0
        ),
        name="norm_quarters",
    )(owner_rows, tokens, gain.reshape(1, model_width))


def fetch(pairs, sem):
    copies = [pltpu.make_async_copy(r, v, sem.at[i]) for i, (r, v) in enumerate(pairs)]
    for copy in copies:
        copy.start()
    return copies


def partial_kernel(given, kinds, *refs):
    outs, (rows, held, mine, other, row_sem, sem) = refs[-6 - len(kinds) : -6], refs[-6:]
    inputs, weights = refs[:given], refs[given : -6 - len(kinds)]
    z, plane = lax.axis_index("wide") >> 2, lax.axis_index("groups")
    size = inputs[0].shape[1]
    hid = held.shape[2]
    hops = len(weights) // 2
    parts = [ref.at[: rows.shape[0]] for ref in inputs]
    row_copies = fetch(
        [(part, rows.at[:, k * size : (k + 1) * size]) for k, part in enumerate(parts)], row_sem
    )
    copies = fetch([(ref, held.at[i]) for i, ref in enumerate(weights)], sem)
    for copy in row_copies:
        copy.wait()
    first = plane == 0
    step = hops // 2
    for start in range(0, hops, step):
        for i in range(2 * start, 2 * (start + step)):
            copies[i].wait()
        for k, (out, kind) in enumerate(zip(outs, kinds)):
            here = slice(k * size, (k + 1) * size)
            sums = []
            for side in range(2):
                total = jnp.zeros((size, hid), F32) if start == 0 else (mine, other)[side][here]
                for hop in range(max(start, 1), start + step):
                    total += jnp.dot(
                        rows[z ^ hop, here], held[2 * hop + side], preferred_element_type=F32
                    )
                sums.append(total)
            if start == 0:
                (mine[here], other[here]) = sums
            else:
                a, b = sums
                gate, up = (
                    jnp.dot(rows[z, here], held[side], preferred_element_type=F32)
                    for side in range(2)
                )
                out[:, :hid] = (gate + jnp.where(first, a, b)).astype(kind)
                out[:, hid:] = (up + jnp.where(first, b, a)).astype(kind)


def partial_sums(inputs, weights, kinds):
    count = len(kinds)
    hops, rows, depth = inputs[0].shape
    hid = weights[0].shape[1]
    return pl.pallas_call(
        functools.partial(partial_kernel, len(inputs), kinds),
        in_specs=[HBM] * (len(inputs) + len(weights)),
        out_specs=[VMEM] * count,
        out_shape=[jax.ShapeDtypeStruct((rows, 2 * hid), kind) for kind in kinds],
        scratch_shapes=[
            pltpu.VMEM((hops, count * rows, depth), BF16),
            pltpu.VMEM((len(weights), depth, hid), BF16),
            pltpu.VMEM((count * rows, hid), F32),
            pltpu.VMEM((count * rows, hid), F32),
            pltpu.SemaphoreType.DMA((count,)),
            pltpu.SemaphoreType.DMA((len(weights),)),
        ],
        compiler_params=pltpu.CompilerParams(vmem_limit_bytes=FULL),
        cost_estimate=pl.CostEstimate(
            flops=4 * hops * count * rows * depth * hid,
            bytes_accessed=2 * hops * depth * (count * rows + 2 * hid),
            transcendentals=0,
        ),
        name="partial_sums",
    )(*inputs, *weights)


def multiply_out(hidden, pieces, owner_ref, weights, out, held, sem, results, out_sem, places):
    copies = fetch(list(zip(weights, held)), sem)
    group, here = lax.axis_index("groups"), lax.axis_index("wide")
    blocks = owner_ref.shape[0]
    block = out.shape[1] // blocks
    for p in range(blocks):
        places[owner_ref[p]] = p * block
    hidden = hidden()
    start, sent = 0, []
    for copy, ref, parts in zip(copies, held, pieces):
        copy.wait()
        for k, (turn, plane) in enumerate(parts):
            width = ref.shape[2]
            for n in range(0, width, 256):
                product = jnp.dot(hidden, ref[k, :, n : n + 256], preferred_element_type=F32)
                results[:, start + n : start + n + 256] = product.astype(BF16)
            side = group ^ plane if width < block else 0
            place = places[here ^ turn] + side * width
            sent.append(
                pltpu.make_async_copy(
                    results.at[:, start : start + width],
                    out.at[:, pl.ds(pl.multiple_of(place, 128), width)],
                    out_sem.at[len(sent)],
                )
            )
            sent[-1].start()
            start += width
    for copy in sent:
        copy.wait()


def first_kernel(pieces, owner_ref, live_ref, own, *refs):
    count = len(pieces)
    partials, weights, (out, hidden_ref) = refs[:3], refs[3 : 3 + count], refs[3 + count : 5 + count]
    held, rest = refs[5 + count : 5 + 2 * count], refs[5 + 2 * count :]
    hid = own.shape[1] // 2

    def hidden():
        total = own[...]
        for part in partials:
            total += part[...].astype(F32)
        gate, up = total[:, :hid], total[:, hid:]
        hidden = gate / (1.0 + jnp.exp(-gate)) * up
        rows = lax.broadcasted_iota(jnp.int32, hidden.shape, 0)
        hidden_ref[...] = jnp.where(rows < MEM + live_ref[0], hidden, 0.0).astype(BF16)
        return hidden_ref[...]

    multiply_out(hidden, pieces, owner_ref, weights, out, held, *rest)


def second_kernel(pieces, owner_ref, live_ref, hidden_ref, _, *refs):
    count = len(pieces)
    weights, out, held, rest = refs[:count], refs[count], refs[count + 1 : 2 * count + 1], refs[2 * count + 1 :]
    multiply_out(lambda: hidden_ref[...], pieces, owner_ref, weights, out, held, *rest)


def down_call(kernel, name, owner_rows, seg_counts, operands, specs, downs, outs, out_specs, aliases):
    weights, pieces = zip(*downs)
    rows = outs[0].shape[0]
    columns = sum(w.size for w in weights) // weights[0].shape[1]
    return pl.pallas_call(
        functools.partial(kernel, pieces),
        in_specs=[SMEM, SMEM] + specs + [HBM] * len(weights),
        out_specs=out_specs,
        out_shape=outs,
        scratch_shapes=[pltpu.VMEM(w.shape, w.dtype) for w in weights]
        + [
            pltpu.SemaphoreType.DMA((len(weights),)),
            pltpu.VMEM((rows, columns), BF16),
            pltpu.SemaphoreType.DMA((sum(len(p) for p in pieces),)),
            pltpu.SMEM(owner_rows.shape, jnp.int32),
        ],
        input_output_aliases=aliases,
        compiler_params=pltpu.CompilerParams(vmem_limit_bytes=FULL),
        cost_estimate=pl.CostEstimate(
            flops=2 * rows * weights[0].shape[1] * columns,
            bytes_accessed=2 * columns * (rows + weights[0].shape[1]),
            transcendentals=0,
        ),
        name=name,
    )(owner_rows, seg_counts, *operands, *weights)


def stack_kernel(a_ref, b_ref, out_ref):
    out_ref[0] = a_ref[0]
    out_ref[1] = b_ref[0]


def stacked(a, b, flops):
    return pl.pallas_call(
        stack_kernel,
        out_shape=jax.ShapeDtypeStruct((2,) + a.shape[1:], a.dtype),
        compiler_params=pltpu.CompilerParams(vmem_limit_bytes=8 << 20),
        cost_estimate=pl.CostEstimate(flops=flops, bytes_accessed=4 * a.size, transcendentals=0),
        name="stack_halves",
    )(a, b)


def after(value, *others):
    return lax.optimization_barrier((value, *others))[0]


def split(groups, owners, tokens, norm_gain, gate_weight, up_weight, down_weight, owner_rows, seg_counts):
    model_width = tokens.shape[1]
    half = model_width // owners // 2
    group, here = lax.axis_index("groups"), lax.axis_index("wide")
    core, across, near, far, other = (0, 1), (0, 2), (0, 4), (0, 8), (1, 0)
    both = (0, 3)

    def swap(value, way):
        pairs = [
            (g * owners + w, (g ^ way[0]) * owners + (w ^ way[1]))
            for g in range(groups)
            for w in range(owners)
        ]
        return lax.ppermute(value, ALL, pairs)

    first = group == 0
    a0 = jnp.where(first, gate_weight, up_weight)
    mine = jnp.where(first, down_weight[:, :half], down_weight[:, half:])[None]

    a1 = swap(a0, near)
    a2 = swap(a0, far)
    mine_x = swap(mine, across)

    t0, t1, t2 = normed_quarters(tokens, norm_gain, owner_rows)
    r2 = swap(t2, across)
    r1 = swap(t1, core)
    rest_x = swap(after(mine_x, t2), other)

    def cross(weights, parts):
        return swap(weights, core), tuple((turn ^ 1, plane) for turn, plane in parts)

    own = [(down_weight[None], ((0, 0),))]
    own = own + [cross(*w) for w in own]
    d0 = stacked(
        after(mine, a1, a2, t2, own[1][0]), mine_x, 10**11
    )

    b1 = swap(after(a1, d0, rest_x), other)
    a3 = swap(after(a2, d0), near)
    d2 = swap(d0, far)
    b2 = swap(after(a2, d0, rest_x), other)

    b3 = swap(after(a3, b1, b2, d2), other)
    d3 = swap(after(d2, a3), near)
    d1 = swap(after(down_weight[None], d3), near)
    e2 = swap(after(d2, b3), other)

    second = [(mine_x, ((2, 0),)), (rest_x, ((2, 1),)), (d2, ((8, 0), (10, 0))), (d3, ((12, 0), (14, 0)))]
    second = second + [cross(*w) for w in second]
    r3 = swap(after(r2, b3, d3, second[4][0], second[5][0], second[6][0])[owners // 4 :], core)
    weights = (gate_weight, up_weight, a1, b1, a2, b2, a3, b3)
    p0, p1, p2, p3 = partial_sums(
        (t0, after(r1, second[7][0]), r2, r3), weights, (F32, F32, BF16, BF16)
    )
    q1 = swap(p1, core)
    q2 = swap(p2, across)
    q3 = swap(p3, both)

    e3 = swap(after(d3, e2, q1), other)
    e0 = stacked(mine_x, rest_x, 0)
    x1 = swap(after(e0, d1, q1), near)

    third = [(e2, ((8, 1), (10, 1))), (d1, ((4, 0),))]
    early = own + second + third
    out = pltpu.HBM(tokens.shape, BF16)
    rows, hid = tokens.shape[0], gate_weight.shape[1]
    product, hidden = down_call(
        first_kernel, "down_first", owner_rows, seg_counts, (p0, q1, q2, q3), [VMEM] * 4, early,
        [out, jax.ShapeDtypeStruct((rows, hid), BF16)], [HBM, VMEM], {},
    )
    late = [(after(x1, hidden), ((6, 0), (6, 1))), (after(e3, hidden), ((12, 1), (14, 1)))]
    late = [cross(after(w, q3), parts) for w, parts in third] + late + [cross(*w) for w in late]
    return down_call(
        second_kernel, "down_second", owner_rows, seg_counts, (hidden, product), [VMEM, HBM], late,
        [out], [HBM], {3: 0},
    )[0]


def solution(mesh):
    placed = (
        P(("groups", "wide"), None),
        P(),
        P("wide", None),
        P("wide", None),
        P(None, "wide"),
        P(),
        P(("groups", "wide")),
    )
    groups, owners = mesh.shape["groups"], mesh.shape["wide"]
    plan = functools.partial(split, groups, owners) if (groups, owners) == (2, 16) else gathered
    return jax.shard_map(
        plan, mesh=mesh, in_specs=placed, out_specs=P(("groups", "wide"), None), check_vma=False
    )
```

```python
import functools

import jax
import jax.numpy as jnp
from jax import lax
from jax.experimental import pallas as pl
from jax.experimental.pallas import tpu as pltpu
from jax.sharding import PartitionSpec as P

MEM = 16
FULL = 60 << 20
ALL = ("groups", "wide")
F32, BF16 = jnp.float32, jnp.bfloat16
VMEM = pl.BlockSpec(memory_space=pltpu.VMEM)
SMEM = pl.BlockSpec(memory_space=pltpu.SMEM)
HBM = pl.BlockSpec(memory_space=pltpu.HBM)


def gathered(tokens, norm_gain, gate_weight, up_weight, down_weight, owner_rows, seg_counts):
    row_count, model_width = tokens.shape
    owners = lax.axis_size("wide")
    block_rows = model_width // owners
    indices = jnp.arange(owners, dtype=jnp.int32)
    holder = jnp.sum(
        indices[:, None] * (owner_rows[:, None] == indices[None, :]).astype(jnp.int32), axis=0
    )
    features = tokens.astype(F32)
    mean_square = jnp.mean(features * features, axis=1, keepdims=True)
    normed = (features * lax.rsqrt(mean_square + 1e-05) * norm_gain[None, :]).astype(BF16)
    stored = normed.reshape(row_count, owners, block_rows)[:, holder, :].reshape(
        row_count, model_width
    )

    def partial_product(portion):
        return jnp.dot(stored, portion, preferred_element_type=F32)

    gate_sum = partial_product(lax.all_gather(gate_weight, "wide", axis=0, tiled=True))
    up_sum = partial_product(lax.all_gather(up_weight, "wide", axis=0, tiled=True))
    hidden = (jax.nn.silu(gate_sum) * up_sum).astype(BF16)
    stored_out = jnp.dot(
        hidden,
        lax.all_gather(down_weight, "wide", axis=1, tiled=True),
        preferred_element_type=F32,
    ).astype(BF16)
    product = stored_out.reshape(row_count, owners, block_rows)[:, owner_rows, :].reshape(
        row_count, model_width
    )
    live_mask = (jnp.arange(row_count, dtype=jnp.int32) < MEM + seg_counts[0]).astype(BF16)
    return product * live_mask[:, None]


def norm_kernel(owner_ref, tokens_ref, gain_ref, *rest):
    (own, near, far), (held, made, scale_ref, in_sem, out_sem) = rest[:3], rest[3:]
    here = lax.axis_index("wide")
    rows, model_width = held.shape
    blocks = owner_ref.shape[0]
    width = model_width // blocks
    step = rows // in_sem.shape[0]
    outs = (own, near, far, far.at[blocks // 4 :])
    copies = [
        pltpu.make_async_copy(
            tokens_ref.at[r : r + step], held.at[r : r + step], in_sem.at[r // step]
        )
        for r in range(0, rows, step)
    ]
    for copy in copies:
        copy.start()
    for r, copy in zip(range(0, rows, step), copies):
        copy.wait()
        parts = [jnp.zeros((step, 128), F32) for _ in range(8)]
        for start in range(0, model_width, 128):
            part = held[r : r + step, start : start + 128].astype(F32)
            parts[start // 128 % 8] += part * part
        mean = jnp.sum(sum(parts), axis=1, keepdims=True) / model_width
        scale_ref[r : r + step] = jnp.broadcast_to(lax.rsqrt(mean + 1e-05), (step, 128))
    scale = scale_ref[...]
    for p in range(blocks):
        for start in range(0, width, 128):
            columns = slice(p * width + start, p * width + start + 128)
            normed = held[:, columns].astype(F32) * scale * gain_ref[:, columns]
            made[p, :, start : start + 128] = normed.astype(BF16)
        stored = owner_ref[p]
        for turn, out in enumerate(outs):

            @pl.when(((stored ^ here) & 3) == turn)
            def _(out=out, p=p, stored=stored):
                pltpu.make_async_copy(made.at[p], out.at[stored >> 2], out_sem.at[p]).start()

    for p in range(blocks):
        pltpu.make_async_copy(made.at[p], outs[0].at[0], out_sem.at[p]).wait()


def normed_quarters(tokens, gain, owner_rows):
    rows, model_width = tokens.shape
    blocks = owner_rows.shape[0]
    width = model_width // blocks
    return pl.pallas_call(
        norm_kernel,
        in_specs=[SMEM, HBM, VMEM],
        out_specs=[HBM] * 3,
        out_shape=[pltpu.HBM((n * blocks // 4, rows, width), BF16) for n in (1, 1, 2)],
        scratch_shapes=[
            pltpu.VMEM((rows, model_width), BF16),
            pltpu.VMEM((blocks, rows, width), BF16),
            pltpu.VMEM((rows, 128), F32),
            pltpu.SemaphoreType.DMA((rows // 16,)),
            pltpu.SemaphoreType.DMA((blocks,)),
        ],
        compiler_params=pltpu.CompilerParams(vmem_limit_bytes=FULL),
        cost_estimate=pl.CostEstimate(
            flops=6 * rows * model_width, bytes_accessed=4 * rows * model_width, transcendentals=0
        ),
        name="norm_quarters",
    )(owner_rows, tokens, gain.reshape(1, model_width))


def fetch(pairs, sem):
    copies = [pltpu.make_async_copy(r, v, sem.at[i]) for i, (r, v) in enumerate(pairs)]
    for copy in copies:
        copy.start()
    return copies


def partial_kernel(given, kinds, *refs):
    count = len(kinds)
    made, (rows, held, mine, other, row_sem, sem, out_sem) = refs[-7 - count : -7], refs[-7:]
    outs = refs[-7 - 2 * count : -7 - count]
    inputs, weights = refs[:given], refs[given : -7 - 2 * count]
    z, plane = lax.axis_index("wide") >> 2, lax.axis_index("groups")
    size = inputs[0].shape[1]
    hid = held.shape[2]
    hops = len(weights) // 2
    parts = [ref.at[: rows.shape[0]] for ref in inputs]
    row_copies = fetch(
        [(part, rows.at[:, k * size : (k + 1) * size]) for k, part in enumerate(parts)], row_sem
    )
    copies = fetch([(ref, held.at[i]) for i, ref in enumerate(weights)], sem)
    for copy in row_copies:
        copy.wait()
    first = plane == 0
    step = hops // 2
    for start in range(0, hops, step):
        for i in range(2 * start, 2 * (start + step)):
            copies[i].wait()
        sent = []
        for k, (out, kind) in enumerate(zip(made, kinds)):
            here = slice(k * size, (k + 1) * size)
            sums = []
            for side in range(2):
                total = jnp.zeros((size, hid), F32) if start == 0 else (mine, other)[side][here]
                for hop in range(max(start, 1), start + step):
                    total += jnp.dot(
                        rows[z ^ hop, here], held[2 * hop + side], preferred_element_type=F32
                    )
                sums.append(total)
            if start == 0:
                (mine[here], other[here]) = sums
            else:
                a, b = sums
                gate, up = (
                    jnp.dot(rows[z, here], held[side], preferred_element_type=F32)
                    for side in range(2)
                )
                out[:, :hid] = (gate + jnp.where(first, a, b)).astype(kind)
                out[:, hid:] = (up + jnp.where(first, b, a)).astype(kind)
                sent.append(pltpu.make_async_copy(out, outs[k], out_sem.at[k]))
                sent[-1].start()
    for copy in sent:
        copy.wait()


def partial_sums(inputs, weights, kinds):
    count = len(kinds)
    hops, rows, depth = inputs[0].shape
    hid = weights[0].shape[1]
    return pl.pallas_call(
        functools.partial(partial_kernel, len(inputs), kinds),
        in_specs=[HBM] * (len(inputs) + len(weights)),
        out_specs=[HBM] * count,
        out_shape=[pltpu.HBM((rows, 2 * hid), kind) for kind in kinds],
        scratch_shapes=[pltpu.VMEM((rows, 2 * hid), kind) for kind in kinds]
        + [
            pltpu.VMEM((hops, count * rows, depth), BF16),
            pltpu.VMEM((len(weights), depth, hid), BF16),
            pltpu.VMEM((count * rows, hid), F32),
            pltpu.VMEM((count * rows, hid), F32),
            pltpu.SemaphoreType.DMA((count,)),
            pltpu.SemaphoreType.DMA((len(weights),)),
            pltpu.SemaphoreType.DMA((count,)),
        ],
        compiler_params=pltpu.CompilerParams(vmem_limit_bytes=FULL),
        cost_estimate=pl.CostEstimate(
            flops=4 * hops * count * rows * depth * hid,
            bytes_accessed=2 * hops * depth * (count * rows + 2 * hid),
            transcendentals=0,
        ),
        name="partial_sums",
    )(*inputs, *weights)


def multiply_out(hidden, copies, pieces, owner, out, held, results, out_sem, places):
    group, here = lax.axis_index("groups"), lax.axis_index("wide")
    blocks = owner.shape[0]
    block = out.shape[1] // blocks
    for p in range(blocks):
        places[owner[p]] = p * block
    start, sent = 0, []
    for copy, ref, parts in zip(copies, held, pieces):
        copy.wait()
        for k, (turn, plane) in enumerate(parts):
            width = ref.shape[2]
            for n in range(0, width, 256):
                product = jnp.dot(hidden, ref[k, :, n : n + 256], preferred_element_type=F32)
                results[:, start + n : start + n + 256] = product.astype(BF16)
            side = group ^ plane if width < block else 0
            place = places[here ^ turn] + side * width
            sent.append(
                pltpu.make_async_copy(
                    results.at[:, start : start + width],
                    out.at[:, pl.ds(pl.multiple_of(place, 128), width)],
                    out_sem.at[len(sent)],
                )
            )
            sent[-1].start()
            start += width
    for copy in sent:
        copy.wait()


def first_kernel(pieces, live_ref, owner_ref, *refs):
    count = len(pieces)
    sums, weights, (out, hidden_ref) = refs[:4], refs[4 : 4 + count], refs[4 + count : 6 + count]
    owner, *rest = refs[6 + count :]
    sums_held, held = rest[:4], rest[4 : 4 + count]
    sem, results, out_sem, places, hidden, hidden_sem = rest[4 + count :]
    first, *copies = fetch(
        list(zip((owner_ref, *sums, *weights), (owner, *sums_held, *held))), sem
    )
    for copy in (first, *copies[:4]):
        copy.wait()
    hid = hidden.shape[1]
    total = sums_held[0][...]
    for part in sums_held[1:]:
        total += part[...].astype(F32)
    gate, up = total[:, :hid], total[:, hid:]
    units = gate / (1.0 + jnp.exp(-gate)) * up
    rows = lax.broadcasted_iota(jnp.int32, units.shape, 0)
    hidden[...] = jnp.where(rows < MEM + live_ref[0], units, 0.0).astype(BF16)
    handed = pltpu.make_async_copy(hidden, hidden_ref, hidden_sem)
    handed.start()
    multiply_out(hidden[...], copies[4:], pieces, owner, out, held, results, out_sem, places)
    handed.wait()


def second_kernel(pieces, owner_ref, hidden_ref, _, *refs):
    count = len(pieces)
    weights, out, owner, held = refs[:count], refs[count], refs[count + 1], refs[count + 2 : 2 * count + 2]
    sem, results, out_sem, places, hidden = refs[2 * count + 2 :]
    first, second, *copies = fetch(
        list(zip((owner_ref, hidden_ref, *weights), (owner, hidden, *held))), sem
    )
    first.wait()
    second.wait()
    multiply_out(hidden[...], copies, pieces, owner, out, held, results, out_sem, places)


def down_call(kernel, name, live, fetched, passed, downs, outs, scratch, aliases):
    weights, pieces = zip(*downs)
    rows = outs[0].shape[0]
    hid = weights[0].shape[1]
    columns = sum(w.size for w in weights) // hid
    places = [pltpu.SMEM(v.shape, v.dtype) for v in fetched[:1]]
    kept = [pltpu.VMEM(v.shape, v.dtype) for v in fetched[1:] if v.shape != (rows, hid)]
    return pl.pallas_call(
        functools.partial(kernel, pieces),
        in_specs=[SMEM] * len(live) + [HBM] * (len(fetched) + len(passed) + len(weights)),
        out_specs=[HBM] * len(outs),
        out_shape=outs,
        scratch_shapes=places
        + kept
        + [pltpu.VMEM(w.shape, w.dtype) for w in weights]
        + [
            pltpu.SemaphoreType.DMA((len(fetched) + len(weights),)),
            pltpu.VMEM((rows, columns), BF16),
            pltpu.SemaphoreType.DMA((sum(len(p) for p in pieces),)),
            *places,
            pltpu.VMEM((rows, hid), BF16),
            *scratch,
        ],
        input_output_aliases=aliases,
        compiler_params=pltpu.CompilerParams(vmem_limit_bytes=FULL),
        cost_estimate=pl.CostEstimate(
            flops=20 * rows * hid * columns,
            bytes_accessed=2 * columns * (rows + hid),
            transcendentals=0,
        ),
        name=name,
    )(*live, *fetched, *passed, *weights)


def stack_kernel(a_ref, b_ref, out_ref):
    out_ref[0] = a_ref[0]
    out_ref[1] = b_ref[0]


def stacked(a, b, flops):
    return pl.pallas_call(
        stack_kernel,
        out_shape=jax.ShapeDtypeStruct((2,) + a.shape[1:], a.dtype),
        compiler_params=pltpu.CompilerParams(vmem_limit_bytes=8 << 20),
        cost_estimate=pl.CostEstimate(flops=flops, bytes_accessed=4 * a.size, transcendentals=0),
        name="stack_halves",
    )(a, b)


def after(value, *others):
    return lax.optimization_barrier((value, *others))[0]


def split(groups, owners, tokens, norm_gain, gate_weight, up_weight, down_weight, owner_rows, seg_counts):
    model_width = tokens.shape[1]
    half = model_width // owners // 2
    group, here = lax.axis_index("groups"), lax.axis_index("wide")
    core, across, near, far, other = (0, 1), (0, 2), (0, 4), (0, 8), (1, 0)
    both = (0, 3)

    def swap(value, way):
        pairs = [
            (g * owners + w, (g ^ way[0]) * owners + (w ^ way[1]))
            for g in range(groups)
            for w in range(owners)
        ]
        return lax.ppermute(value, ALL, pairs)

    first = group == 0
    a0 = jnp.where(first, gate_weight, up_weight)
    mine = jnp.where(first, down_weight[:, :half], down_weight[:, half:])[None]

    a1 = swap(a0, near)
    a2 = swap(a0, far)
    mine_x = swap(mine, across)

    t0, t1, t2 = normed_quarters(tokens, norm_gain, owner_rows)
    r2 = swap(t2, across)
    r1 = swap(t1, core)
    rest_x = swap(after(mine_x, t2), other)

    def cross(weights, parts):
        return swap(weights, core), tuple((turn ^ 1, plane) for turn, plane in parts)

    own = [(down_weight[None], ((0, 0),))]
    own = own + [cross(*w) for w in own]
    d0 = stacked(
        after(mine, a1, a2, t2, own[1][0]), mine_x, 10**11
    )

    b1 = swap(after(a1, d0, rest_x), other)
    a3 = swap(after(a2, d0), near)
    d2 = swap(d0, far)
    b2 = swap(after(a2, d0, rest_x), other)

    b3 = swap(after(a3, b1, b2, d2), other)
    d3 = swap(after(d2, a3), near)
    d1 = swap(after(down_weight[None], d3), near)
    e2 = swap(after(d2, b3), other)

    second = [(mine_x, ((2, 0),)), (rest_x, ((2, 1),)), (d2, ((8, 0), (10, 0)))]
    second = second + [cross(*w) for w in second]
    r3 = swap(after(r2, b3, d3, *(w for w, _ in second))[owners // 4 :], core)
    weights = (gate_weight, up_weight, a1, b1, a2, b2, a3, b3)
    p0, p1, p2, p3 = partial_sums(
        (t0, r1, r2, r3), weights, (F32, F32, BF16, BF16)
    )
    q1 = swap(p1, core)
    q2 = swap(p2, across)
    q3 = swap(p3, both)

    e3 = swap(after(d3, e2, q1), other)
    e0 = stacked(mine_x, rest_x, 0)
    x1 = swap(after(e0, d1, q1), near)

    third = [(d3, ((12, 0), (14, 0))), (e2, ((8, 1), (10, 1))), (d1, ((4, 0),))]
    early = own + second + third
    out = pltpu.HBM(tokens.shape, BF16)
    rows, hid = tokens.shape[0], gate_weight.shape[1]
    product, hidden = down_call(
        first_kernel, "down_first", [seg_counts], [owner_rows, p0, q1, q2, q3], [], early,
        [out, pltpu.HBM((rows, hid), BF16)], [pltpu.SemaphoreType.DMA], {},
    )
    late = [(after(x1, hidden), ((6, 0), (6, 1))), (after(e3, hidden), ((12, 1), (14, 1)))]
    late = [cross(after(w, hidden), parts) for w, parts in third] + late + [cross(*w) for w in late]
    return down_call(
        second_kernel, "down_second", [], [owner_rows, hidden], [product], late, [out], [], {2: 0}
    )[0]


def solution(mesh):
    placed = (
        P(("groups", "wide"), None),
        P(),
        P("wide", None),
        P("wide", None),
        P(None, "wide"),
        P(),
        P(("groups", "wide")),
    )
    groups, owners = mesh.shape["groups"], mesh.shape["wide"]
    plan = functools.partial(split, groups, owners) if (groups, owners) == (2, 16) else gathered
    return jax.shard_map(
        plan, mesh=mesh, in_specs=placed, out_specs=P(("groups", "wide"), None), check_vma=False
    )
```

```python
import functools

import jax
import jax.numpy as jnp
from jax import lax
from jax.experimental import pallas as pl
from jax.experimental.pallas import tpu as pltpu
from jax.sharding import PartitionSpec as P

MEM = 16
FULL = 60 << 20
ALL = ("groups", "wide")
F32, BF16 = jnp.float32, jnp.bfloat16
VMEM = pl.BlockSpec(memory_space=pltpu.VMEM)
SMEM = pl.BlockSpec(memory_space=pltpu.SMEM)
HBM = pl.BlockSpec(memory_space=pltpu.HBM)


def gathered(tokens, norm_gain, gate_weight, up_weight, down_weight, owner_rows, seg_counts):
    row_count, model_width = tokens.shape
    owners = lax.axis_size("wide")
    block_rows = model_width // owners
    indices = jnp.arange(owners, dtype=jnp.int32)
    holder = jnp.sum(
        indices[:, None] * (owner_rows[:, None] == indices[None, :]).astype(jnp.int32), axis=0
    )
    features = tokens.astype(F32)
    mean_square = jnp.mean(features * features, axis=1, keepdims=True)
    normed = (features * lax.rsqrt(mean_square + 1e-05) * norm_gain[None, :]).astype(BF16)
    stored = normed.reshape(row_count, owners, block_rows)[:, holder, :].reshape(
        row_count, model_width
    )

    def partial_product(portion):
        return jnp.dot(stored, portion, preferred_element_type=F32)

    gate_sum = partial_product(lax.all_gather(gate_weight, "wide", axis=0, tiled=True))
    up_sum = partial_product(lax.all_gather(up_weight, "wide", axis=0, tiled=True))
    hidden = (jax.nn.silu(gate_sum) * up_sum).astype(BF16)
    stored_out = jnp.dot(
        hidden,
        lax.all_gather(down_weight, "wide", axis=1, tiled=True),
        preferred_element_type=F32,
    ).astype(BF16)
    product = stored_out.reshape(row_count, owners, block_rows)[:, owner_rows, :].reshape(
        row_count, model_width
    )
    live_mask = (jnp.arange(row_count, dtype=jnp.int32) < MEM + seg_counts[0]).astype(BF16)
    return product * live_mask[:, None]


def norm_kernel(owner_ref, tokens_ref, gain_ref, *rest):
    (own, near, far), (held, made, scale_ref, in_sem, out_sem) = rest[:3], rest[3:]
    here = lax.axis_index("wide")
    rows, model_width = held.shape
    blocks = owner_ref.shape[0]
    width = model_width // blocks
    step = rows // in_sem.shape[0]
    outs = (own, near, far, far.at[blocks // 4 :])
    copies = [
        pltpu.make_async_copy(
            tokens_ref.at[r : r + step], held.at[r : r + step], in_sem.at[r // step]
        )
        for r in range(0, rows, step)
    ]
    for copy in copies:
        copy.start()
    for r, copy in zip(range(0, rows, step), copies):
        copy.wait()
        parts = [jnp.zeros((step, 128), F32) for _ in range(8)]
        for start in range(0, model_width, 128):
            part = held[r : r + step, start : start + 128].astype(F32)
            parts[start // 128 % 8] += part * part
        mean = jnp.sum(sum(parts), axis=1, keepdims=True) / model_width
        scale_ref[r : r + step] = jnp.broadcast_to(lax.rsqrt(mean + 1e-05), (step, 128))
    scale = scale_ref[...]
    for p in range(blocks):
        for start in range(0, width, 128):
            columns = slice(p * width + start, p * width + start + 128)
            normed = held[:, columns].astype(F32) * scale * gain_ref[:, columns]
            made[p, :, start : start + 128] = normed.astype(BF16)
        stored = owner_ref[p]
        for turn, out in enumerate(outs):

            @pl.when(((stored ^ here) & 3) == turn)
            def _(out=out, p=p, stored=stored):
                pltpu.make_async_copy(made.at[p], out.at[stored >> 2], out_sem.at[p]).start()

    for p in range(blocks):
        pltpu.make_async_copy(made.at[p], outs[0].at[0], out_sem.at[p]).wait()


def normed_quarters(tokens, gain, owner_rows):
    rows, model_width = tokens.shape
    blocks = owner_rows.shape[0]
    width = model_width // blocks
    return pl.pallas_call(
        norm_kernel,
        in_specs=[SMEM, HBM, VMEM],
        out_specs=[HBM] * 3,
        out_shape=[pltpu.HBM((n * blocks // 4, rows, width), BF16) for n in (1, 1, 2)],
        scratch_shapes=[
            pltpu.VMEM((rows, model_width), BF16),
            pltpu.VMEM((blocks, rows, width), BF16),
            pltpu.VMEM((rows, 128), F32),
            pltpu.SemaphoreType.DMA((rows // 16,)),
            pltpu.SemaphoreType.DMA((blocks,)),
        ],
        compiler_params=pltpu.CompilerParams(vmem_limit_bytes=FULL),
        cost_estimate=pl.CostEstimate(
            flops=6 * rows * model_width, bytes_accessed=4 * rows * model_width, transcendentals=0
        ),
        name="norm_quarters",
    )(owner_rows, tokens, gain.reshape(1, model_width))


def fetch(pairs, sem):
    copies = [pltpu.make_async_copy(r, v, sem.at[i]) for i, (r, v) in enumerate(pairs)]
    for copy in copies:
        copy.start()
    return copies


def partial_kernel(given, kinds, *refs):
    count = len(kinds)
    made, (rows, held, mine, other, row_sem, sem, out_sem) = refs[-7 - count : -7], refs[-7:]
    outs = refs[-7 - 2 * count : -7 - count]
    inputs, weights = refs[:given], refs[given : -7 - 2 * count]
    z, plane = lax.axis_index("wide") >> 2, lax.axis_index("groups")
    size = inputs[0].shape[1]
    hid = held.shape[2]
    hops = len(weights) // 2
    parts = [ref.at[: rows.shape[0]] for ref in inputs]
    row_copies = fetch(
        [(part, rows.at[:, k * size : (k + 1) * size]) for k, part in enumerate(parts)], row_sem
    )
    copies = fetch([(ref, held.at[i]) for i, ref in enumerate(weights)], sem)
    for copy in row_copies:
        copy.wait()
    first = plane == 0
    step = hops // 2
    for start in range(0, hops, step):
        for i in range(2 * start, 2 * (start + step)):
            copies[i].wait()
        sent = []
        for k, (out, kind) in enumerate(zip(made, kinds)):
            here = slice(k * size, (k + 1) * size)
            sums = []
            for side in range(2):
                total = jnp.zeros((size, hid), F32) if start == 0 else (mine, other)[side][here]
                for hop in range(max(start, 1), start + step):
                    total += jnp.dot(
                        rows[z ^ hop, here], held[2 * hop + side], preferred_element_type=F32
                    )
                sums.append(total)
            if start == 0:
                (mine[here], other[here]) = sums
            else:
                a, b = sums
                gate, up = (
                    jnp.dot(rows[z, here], held[side], preferred_element_type=F32)
                    for side in range(2)
                )
                out[:, :hid] = (gate + jnp.where(first, a, b)).astype(kind)
                out[:, hid:] = (up + jnp.where(first, b, a)).astype(kind)
                sent.append(pltpu.make_async_copy(out, outs[k], out_sem.at[k]))
                sent[-1].start()
    for copy in sent:
        copy.wait()


def partial_sums(inputs, weights, kinds):
    count = len(kinds)
    hops, rows, depth = inputs[0].shape
    hid = weights[0].shape[1]
    return pl.pallas_call(
        functools.partial(partial_kernel, len(inputs), kinds),
        in_specs=[HBM] * (len(inputs) + len(weights)),
        out_specs=[HBM] * count,
        out_shape=[pltpu.HBM((rows, 2 * hid), kind) for kind in kinds],
        scratch_shapes=[pltpu.VMEM((rows, 2 * hid), kind) for kind in kinds]
        + [
            pltpu.VMEM((hops, count * rows, depth), BF16),
            pltpu.VMEM((len(weights), depth, hid), BF16),
            pltpu.VMEM((count * rows, hid), F32),
            pltpu.VMEM((count * rows, hid), F32),
            pltpu.SemaphoreType.DMA((count,)),
            pltpu.SemaphoreType.DMA((len(weights),)),
            pltpu.SemaphoreType.DMA((count,)),
        ],
        compiler_params=pltpu.CompilerParams(vmem_limit_bytes=FULL),
        cost_estimate=pl.CostEstimate(
            flops=4 * hops * count * rows * depth * hid,
            bytes_accessed=2 * hops * depth * (count * rows + 2 * hid),
            transcendentals=0,
        ),
        name="partial_sums",
    )(*inputs, *weights)


def multiply_out(hidden, copies, pieces, owner, out, held, results, out_sem, places):
    group, here = lax.axis_index("groups"), lax.axis_index("wide")
    blocks = owner.shape[0]
    block = out.shape[1] // blocks
    for p in range(blocks):
        places[owner[p]] = p * block
    start, sent = 0, []
    for copy, ref, parts in zip(copies, held, pieces):
        copy.wait()
        for k, (turn, plane) in enumerate(parts):
            width = ref.shape[2]
            for n in range(0, width, 256):
                product = jnp.dot(hidden, ref[k, :, n : n + 256], preferred_element_type=F32)
                results[:, start + n : start + n + 256] = product.astype(BF16)
            side = group ^ plane if width < block else 0
            place = places[here ^ turn] + side * width
            sent.append(
                pltpu.make_async_copy(
                    results.at[:, start : start + width],
                    out.at[:, pl.ds(pl.multiple_of(place, 128), width)],
                    out_sem.at[len(sent)],
                )
            )
            sent[-1].start()
            start += width
    for copy in sent:
        copy.wait()


def first_kernel(pieces, live_ref, owner_ref, *refs):
    count = len(pieces)
    sums, weights, (out, hidden_ref) = refs[:4], refs[4 : 4 + count], refs[4 + count : 6 + count]
    owner, *rest = refs[6 + count :]
    sums_held, held = rest[:4], rest[4 : 4 + count]
    sem, results, out_sem, places, hidden, hidden_sem = rest[4 + count :]
    first, *copies = fetch(
        list(zip((owner_ref, *sums, *weights), (owner, *sums_held, *held))), sem
    )
    for copy in (first, *copies[:4]):
        copy.wait()
    hid = hidden.shape[1]
    total = sums_held[0][...]
    for part in sums_held[1:]:
        total += part[...].astype(F32)
    gate, up = total[:, :hid], total[:, hid:]
    units = gate / (1.0 + jnp.exp(-gate)) * up
    rows = lax.broadcasted_iota(jnp.int32, units.shape, 0)
    hidden[...] = jnp.where(rows < MEM + live_ref[0], units, 0.0).astype(BF16)
    handed = pltpu.make_async_copy(hidden, hidden_ref, hidden_sem)
    handed.start()
    multiply_out(hidden[...], copies[4:], pieces, owner, out, held, results, out_sem, places)
    handed.wait()


def second_kernel(pieces, owner_ref, hidden_ref, _, *refs):
    count = len(pieces)
    weights, out, owner, held = refs[:count], refs[count], refs[count + 1], refs[count + 2 : 2 * count + 2]
    sem, results, out_sem, places, hidden = refs[2 * count + 2 :]
    first, second, *copies = fetch(
        list(zip((owner_ref, hidden_ref, *weights), (owner, hidden, *held))), sem
    )
    first.wait()
    second.wait()
    multiply_out(hidden[...], copies, pieces, owner, out, held, results, out_sem, places)


def down_call(kernel, name, live, fetched, passed, downs, outs, scratch, aliases):
    weights, pieces = zip(*downs)
    rows = outs[0].shape[0]
    hid = weights[0].shape[1]
    columns = sum(w.size for w in weights) // hid
    places = [pltpu.SMEM(v.shape, v.dtype) for v in fetched[:1]]
    kept = [pltpu.VMEM(v.shape, v.dtype) for v in fetched[1:] if v.shape != (rows, hid)]
    return pl.pallas_call(
        functools.partial(kernel, pieces),
        in_specs=[SMEM] * len(live) + [HBM] * (len(fetched) + len(passed) + len(weights)),
        out_specs=[HBM] * len(outs),
        out_shape=outs,
        scratch_shapes=places
        + kept
        + [pltpu.VMEM(w.shape, w.dtype) for w in weights]
        + [
            pltpu.SemaphoreType.DMA((len(fetched) + len(weights),)),
            pltpu.VMEM((rows, columns), BF16),
            pltpu.SemaphoreType.DMA((sum(len(p) for p in pieces),)),
            *places,
            pltpu.VMEM((rows, hid), BF16),
            *scratch,
        ],
        input_output_aliases=aliases,
        compiler_params=pltpu.CompilerParams(vmem_limit_bytes=FULL),
        cost_estimate=pl.CostEstimate(
            flops=20 * rows * hid * columns,
            bytes_accessed=2 * columns * (rows + hid),
            transcendentals=0,
        ),
        name=name,
    )(*live, *fetched, *passed, *weights)


def stack_kernel(a_ref, b_ref, out_ref):
    out_ref[0] = a_ref[0]
    out_ref[1] = b_ref[0]


def stacked(a, b, flops):
    return pl.pallas_call(
        stack_kernel,
        out_shape=jax.ShapeDtypeStruct((2,) + a.shape[1:], a.dtype),
        compiler_params=pltpu.CompilerParams(vmem_limit_bytes=8 << 20),
        cost_estimate=pl.CostEstimate(flops=flops, bytes_accessed=4 * a.size, transcendentals=0),
        name="stack_halves",
    )(a, b)


def after(value, *others):
    return lax.optimization_barrier((value, *others))[0]


def split(groups, owners, tokens, norm_gain, gate_weight, up_weight, down_weight, owner_rows, seg_counts):
    model_width = tokens.shape[1]
    half = model_width // owners // 2
    group, here = lax.axis_index("groups"), lax.axis_index("wide")
    core, across, near, far, other = (0, 1), (0, 2), (0, 4), (0, 8), (1, 0)
    both = (0, 3)

    def swap(value, way):
        pairs = [
            (g * owners + w, (g ^ way[0]) * owners + (w ^ way[1]))
            for g in range(groups)
            for w in range(owners)
        ]
        return lax.ppermute(value, ALL, pairs)

    first = group == 0
    a0 = jnp.where(first, gate_weight, up_weight)
    mine = jnp.where(first, down_weight[:, :half], down_weight[:, half:])[None]

    a1 = swap(a0, near)
    a2 = swap(a0, far)
    mine_x = swap(mine, across)

    t0, t1, t2 = normed_quarters(tokens, norm_gain, owner_rows)
    r2 = swap(t2, across)
    r1 = swap(t1, core)
    rest_x = swap(after(mine_x, t2), other)

    def cross(weights, parts):
        return swap(weights, core), tuple((turn ^ 1, plane) for turn, plane in parts)

    own = [(down_weight[None], ((0, 0),))]
    own = own + [cross(*w) for w in own]
    d0 = stacked(
        after(mine, a1, a2, t2, own[1][0]), mine_x, 10**11
    )

    b1 = swap(after(a1, d0, rest_x), other)
    a3 = swap(after(a2, d0), near)
    d2 = swap(after(down_weight[None], d0), far)
    b2 = swap(after(a2, d0, rest_x), other)

    b3 = swap(after(a3, b1, b2), other)
    d1 = swap(after(d0, a3, d2), near)

    e1 = swap(after(d1, b3), other)
    d3 = swap(after(d2, d1), near)
    f2 = swap(after(d2, r2), across)

    second = [(mine_x, ((2, 0),)), (rest_x, ((2, 1),)), (d2, ((8, 0),))]
    second = second + [cross(*w) for w in second]
    r3 = swap(after(r2, b3, d1, *(w for w, _ in second))[owners // 4 :], core)
    weights = (gate_weight, up_weight, a1, b1, a2, b2, a3, b3)
    p0, p1, p2, p3 = partial_sums(
        (t0, r1, r2, r3), weights, (F32, F32, BF16, BF16)
    )
    q1 = swap(p1, core)
    q2 = swap(p2, across)
    q3 = swap(p3, both)

    f3 = swap(after(f2, d3, q1), near)

    third = [
        (d1, ((4, 0), (6, 0))),
        (e1, ((4, 1), (6, 1))),
        (f2, ((10, 0),)),
        (d3, ((12, 0),)),
    ]
    early = own + second + third
    out = pltpu.HBM(tokens.shape, BF16)
    rows, hid = tokens.shape[0], gate_weight.shape[1]
    product, hidden = down_call(
        first_kernel, "down_first", [seg_counts], [owner_rows, p0, q1, q2, q3], [], early,
        [out, pltpu.HBM((rows, hid), BF16)], [pltpu.SemaphoreType.DMA], {},
    )
    late = [(after(f3, hidden), ((14, 0),))]
    late = [cross(after(w, hidden), parts) for w, parts in third] + late + [cross(*w) for w in late]
    return down_call(
        second_kernel, "down_second", [], [owner_rows, hidden], [product], late, [out], [], {2: 0}
    )[0]


def solution(mesh):
    placed = (
        P(("groups", "wide"), None),
        P(),
        P("wide", None),
        P("wide", None),
        P(None, "wide"),
        P(),
        P(("groups", "wide")),
    )
    groups, owners = mesh.shape["groups"], mesh.shape["wide"]
    plan = functools.partial(split, groups, owners) if (groups, owners) == (2, 16) else gathered
    return jax.shard_map(
        plan, mesh=mesh, in_specs=placed, out_specs=P(("groups", "wide"), None), check_vma=False
    )
```

```python
import functools

import jax
import jax.numpy as jnp
from jax import lax
from jax.experimental import pallas as pl
from jax.experimental.pallas import tpu as pltpu
from jax.sharding import PartitionSpec as P

MEM = 16
FULL = 60 << 20
ALL = ("groups", "wide")
F32, BF16 = jnp.float32, jnp.bfloat16
VMEM = pl.BlockSpec(memory_space=pltpu.VMEM)
SMEM = pl.BlockSpec(memory_space=pltpu.SMEM)
HBM = pl.BlockSpec(memory_space=pltpu.HBM)


def gathered(tokens, norm_gain, gate_weight, up_weight, down_weight, owner_rows, seg_counts):
    row_count, model_width = tokens.shape
    owners = lax.axis_size("wide")
    block_rows = model_width // owners
    indices = jnp.arange(owners, dtype=jnp.int32)
    holder = jnp.sum(
        indices[:, None] * (owner_rows[:, None] == indices[None, :]).astype(jnp.int32), axis=0
    )
    features = tokens.astype(F32)
    mean_square = jnp.mean(features * features, axis=1, keepdims=True)
    normed = (features * lax.rsqrt(mean_square + 1e-05) * norm_gain[None, :]).astype(BF16)
    stored = normed.reshape(row_count, owners, block_rows)[:, holder, :].reshape(
        row_count, model_width
    )

    def partial_product(portion):
        return jnp.dot(stored, portion, preferred_element_type=F32)

    gate_sum = partial_product(lax.all_gather(gate_weight, "wide", axis=0, tiled=True))
    up_sum = partial_product(lax.all_gather(up_weight, "wide", axis=0, tiled=True))
    hidden = (jax.nn.silu(gate_sum) * up_sum).astype(BF16)
    stored_out = jnp.dot(
        hidden,
        lax.all_gather(down_weight, "wide", axis=1, tiled=True),
        preferred_element_type=F32,
    ).astype(BF16)
    product = stored_out.reshape(row_count, owners, block_rows)[:, owner_rows, :].reshape(
        row_count, model_width
    )
    live_mask = (jnp.arange(row_count, dtype=jnp.int32) < MEM + seg_counts[0]).astype(BF16)
    return product * live_mask[:, None]


def norm_kernel(owner_ref, tokens_ref, gain_ref, *rest):
    (own, near, far), (held, made, scale_ref, in_sem, out_sem) = rest[:3], rest[3:]
    here = lax.axis_index("wide")
    rows, model_width = held.shape
    blocks = owner_ref.shape[0]
    width = model_width // blocks
    step = rows // in_sem.shape[0]
    outs = (own, near, far, far.at[blocks // 4 :])
    copies = [
        pltpu.make_async_copy(
            tokens_ref.at[r : r + step], held.at[r : r + step], in_sem.at[r // step]
        )
        for r in range(0, rows, step)
    ]
    for copy in copies:
        copy.start()
    for r, copy in zip(range(0, rows, step), copies):
        copy.wait()
        parts = [jnp.zeros((step, 128), F32) for _ in range(8)]
        for start in range(0, model_width, 128):
            part = held[r : r + step, start : start + 128].astype(F32)
            parts[start // 128 % 8] += part * part
        mean = jnp.sum(sum(parts), axis=1, keepdims=True) / model_width
        scale_ref[r : r + step] = jnp.broadcast_to(lax.rsqrt(mean + 1e-05), (step, 128))
    scale = scale_ref[...]
    for p in range(blocks):
        for start in range(0, width, 128):
            columns = slice(p * width + start, p * width + start + 128)
            normed = held[:, columns].astype(F32) * scale * gain_ref[:, columns]
            made[p, :, start : start + 128] = normed.astype(BF16)
        stored = owner_ref[p]
        for turn, out in enumerate(outs):

            @pl.when(((stored ^ here) & 3) == turn)
            def _(out=out, p=p, stored=stored):
                pltpu.make_async_copy(made.at[p], out.at[stored >> 2], out_sem.at[p]).start()

    for p in range(blocks):
        pltpu.make_async_copy(made.at[p], outs[0].at[0], out_sem.at[p]).wait()


def normed_quarters(tokens, gain, owner_rows):
    rows, model_width = tokens.shape
    blocks = owner_rows.shape[0]
    width = model_width // blocks
    return pl.pallas_call(
        norm_kernel,
        in_specs=[SMEM, HBM, VMEM],
        out_specs=[HBM] * 3,
        out_shape=[pltpu.HBM((n * blocks // 4, rows, width), BF16) for n in (1, 1, 2)],
        scratch_shapes=[
            pltpu.VMEM((rows, model_width), BF16),
            pltpu.VMEM((blocks, rows, width), BF16),
            pltpu.VMEM((rows, 128), F32),
            pltpu.SemaphoreType.DMA((rows // 16,)),
            pltpu.SemaphoreType.DMA((blocks,)),
        ],
        compiler_params=pltpu.CompilerParams(vmem_limit_bytes=FULL),
        cost_estimate=pl.CostEstimate(
            flops=6 * rows * model_width, bytes_accessed=4 * rows * model_width, transcendentals=0
        ),
        name="norm_quarters",
    )(owner_rows, tokens, gain.reshape(1, model_width))


def fetch(pairs, sem):
    copies = [pltpu.make_async_copy(r, v, sem.at[i]) for i, (r, v) in enumerate(pairs)]
    for copy in copies:
        copy.start()
    return copies


def partial_kernel(given, kinds, *refs):
    count = len(kinds)
    made, (rows, held, mine, other, row_sem, sem, out_sem) = refs[-7 - count : -7], refs[-7:]
    outs = refs[-7 - 2 * count : -7 - count]
    inputs, weights = refs[:given], refs[given : -7 - 2 * count]
    z, plane = lax.axis_index("wide") >> 2, lax.axis_index("groups")
    size = inputs[0].shape[1]
    hid = held.shape[2]
    hops = len(weights) // 2
    parts = [ref.at[: rows.shape[0]] for ref in inputs]
    row_copies = fetch(
        [(part, rows.at[:, k * size : (k + 1) * size]) for k, part in enumerate(parts)], row_sem
    )
    copies = fetch([(ref, held.at[i]) for i, ref in enumerate(weights)], sem)
    for copy in row_copies:
        copy.wait()
    first = plane == 0
    step = hops // 2
    for start in range(0, hops, step):
        for i in range(2 * start, 2 * (start + step)):
            copies[i].wait()
        sent = []
        for k, (out, kind) in enumerate(zip(made, kinds)):
            here = slice(k * size, (k + 1) * size)
            sums = []
            for side in range(2):
                total = jnp.zeros((size, hid), F32) if start == 0 else (mine, other)[side][here]
                for hop in range(max(start, 1), start + step):
                    total += jnp.dot(
                        rows[z ^ hop, here], held[2 * hop + side], preferred_element_type=F32
                    )
                sums.append(total)
            if start == 0:
                (mine[here], other[here]) = sums
            else:
                a, b = sums
                gate, up = (
                    jnp.dot(rows[z, here], held[side], preferred_element_type=F32)
                    for side in range(2)
                )
                out[:, :hid] = (gate + jnp.where(first, a, b)).astype(kind)
                out[:, hid:] = (up + jnp.where(first, b, a)).astype(kind)
                sent.append(pltpu.make_async_copy(out, outs[k], out_sem.at[k]))
                sent[-1].start()
    for copy in sent:
        copy.wait()


def partial_sums(inputs, weights, kinds):
    count = len(kinds)
    hops, rows, depth = inputs[0].shape
    hid = weights[0].shape[1]
    return pl.pallas_call(
        functools.partial(partial_kernel, len(inputs), kinds),
        in_specs=[HBM] * (len(inputs) + len(weights)),
        out_specs=[HBM] * count,
        out_shape=[pltpu.HBM((rows, 2 * hid), kind) for kind in kinds],
        scratch_shapes=[pltpu.VMEM((rows, 2 * hid), kind) for kind in kinds]
        + [
            pltpu.VMEM((hops, count * rows, depth), BF16),
            pltpu.VMEM((len(weights), depth, hid), BF16),
            pltpu.VMEM((count * rows, hid), F32),
            pltpu.VMEM((count * rows, hid), F32),
            pltpu.SemaphoreType.DMA((count,)),
            pltpu.SemaphoreType.DMA((len(weights),)),
            pltpu.SemaphoreType.DMA((count,)),
        ],
        compiler_params=pltpu.CompilerParams(vmem_limit_bytes=FULL),
        cost_estimate=pl.CostEstimate(
            flops=4 * hops * count * rows * depth * hid,
            bytes_accessed=2 * hops * depth * (count * rows + 2 * hid),
            transcendentals=0,
        ),
        name="partial_sums",
    )(*inputs, *weights)


def multiply_out(hidden, copies, pieces, owner, out, held, results, out_sem, places):
    group, here = lax.axis_index("groups"), lax.axis_index("wide")
    blocks = owner.shape[0]
    block = out.shape[1] // blocks
    for p in range(blocks):
        places[owner[p]] = p * block
    start, sent = 0, []
    for copy, ref, parts in zip(copies, held, pieces):
        copy.wait()
        for k, (turn, plane) in enumerate(parts):
            width = ref.shape[2]
            for n in range(0, width, 256):
                product = jnp.dot(hidden, ref[k, :, n : n + 256], preferred_element_type=F32)
                results[:, start + n : start + n + 256] = product.astype(BF16)
            side = (plane - 2 if plane >= 2 else group ^ plane) if width < block else 0
            place = places[here ^ turn] + side * width
            sent.append(
                pltpu.make_async_copy(
                    results.at[:, start : start + width],
                    out.at[:, pl.ds(pl.multiple_of(place, 128), width)],
                    out_sem.at[len(sent)],
                )
            )
            sent[-1].start()
            start += width
    for copy in sent:
        copy.wait()


def first_kernel(pieces, live_ref, owner_ref, *refs):
    count = len(pieces)
    sums, weights, (out, hidden_ref) = refs[:4], refs[4 : 4 + count], refs[4 + count : 6 + count]
    owner, *rest = refs[6 + count :]
    sums_held, held = rest[:4], rest[4 : 4 + count]
    sem, results, out_sem, places, hidden, hidden_sem = rest[4 + count :]
    first, *copies = fetch(
        list(zip((owner_ref, *sums, *weights), (owner, *sums_held, *held))), sem
    )
    for copy in (first, *copies[:4]):
        copy.wait()
    hid = hidden.shape[1]
    total = sums_held[0][...]
    for part in sums_held[1:]:
        total += part[...].astype(F32)
    gate, up = total[:, :hid], total[:, hid:]
    units = gate / (1.0 + jnp.exp(-gate)) * up
    rows = lax.broadcasted_iota(jnp.int32, units.shape, 0)
    hidden[...] = jnp.where(rows < MEM + live_ref[0], units, 0.0).astype(BF16)
    handed = pltpu.make_async_copy(hidden, hidden_ref, hidden_sem)
    handed.start()
    multiply_out(hidden[...], copies[4:], pieces, owner, out, held, results, out_sem, places)
    handed.wait()


def second_kernel(pieces, owner_ref, hidden_ref, _, *refs):
    count = len(pieces)
    weights, out, owner, held = refs[:count], refs[count], refs[count + 1], refs[count + 2 : 2 * count + 2]
    sem, results, out_sem, places, hidden = refs[2 * count + 2 :]
    first, second, *copies = fetch(
        list(zip((owner_ref, hidden_ref, *weights), (owner, hidden, *held))), sem
    )
    first.wait()
    second.wait()
    multiply_out(hidden[...], copies, pieces, owner, out, held, results, out_sem, places)


def down_call(kernel, name, live, fetched, passed, downs, outs, scratch, aliases):
    weights, pieces = zip(*downs)
    rows = outs[0].shape[0]
    hid = weights[0].shape[1]
    columns = sum(w.size for w in weights) // hid
    places = [pltpu.SMEM(v.shape, v.dtype) for v in fetched[:1]]
    kept = [pltpu.VMEM(v.shape, v.dtype) for v in fetched[1:] if v.shape != (rows, hid)]
    return pl.pallas_call(
        functools.partial(kernel, pieces),
        in_specs=[SMEM] * len(live) + [HBM] * (len(fetched) + len(passed) + len(weights)),
        out_specs=[HBM] * len(outs),
        out_shape=outs,
        scratch_shapes=places
        + kept
        + [pltpu.VMEM(w.shape, w.dtype) for w in weights]
        + [
            pltpu.SemaphoreType.DMA((len(fetched) + len(weights),)),
            pltpu.VMEM((rows, columns), BF16),
            pltpu.SemaphoreType.DMA((sum(len(p) for p in pieces),)),
            *places,
            pltpu.VMEM((rows, hid), BF16),
            *scratch,
        ],
        input_output_aliases=aliases,
        compiler_params=pltpu.CompilerParams(vmem_limit_bytes=FULL),
        cost_estimate=pl.CostEstimate(
            flops=20 * rows * hid * columns,
            bytes_accessed=2 * columns * (rows + hid),
            transcendentals=0,
        ),
        name=name,
    )(*live, *fetched, *passed, *weights)


def stack_kernel(a_ref, b_ref, out_ref):
    out_ref[0] = a_ref[0]
    out_ref[1] = b_ref[0]


def stacked(a, b, flops):
    return pl.pallas_call(
        stack_kernel,
        out_shape=jax.ShapeDtypeStruct((2,) + a.shape[1:], a.dtype),
        compiler_params=pltpu.CompilerParams(vmem_limit_bytes=8 << 20),
        cost_estimate=pl.CostEstimate(flops=flops, bytes_accessed=4 * a.size, transcendentals=0),
        name="stack_halves",
    )(a, b)


def after(value, *others):
    return lax.optimization_barrier((value, *others))[0]


def split(groups, owners, tokens, norm_gain, gate_weight, up_weight, down_weight, owner_rows, seg_counts):
    model_width = tokens.shape[1]
    half = model_width // owners // 2
    group, here = lax.axis_index("groups"), lax.axis_index("wide")
    core, across, near, far, other = (0, 1), (0, 2), (0, 4), (0, 8), (1, 0)
    both = (0, 3)

    def swap(value, way):
        pairs = [
            (g * owners + w, (g ^ way[0]) * owners + (w ^ way[1]))
            for g in range(groups)
            for w in range(owners)
        ]
        return lax.ppermute(value, ALL, pairs)

    first = group == 0
    a0 = jnp.where(first, gate_weight, up_weight)
    mine = jnp.where(first, down_weight[:, :half], down_weight[:, half:])[None]

    a1 = swap(a0, near)
    a2 = swap(a0, far)
    mine_x = swap(mine, across)

    t0, t1, t2 = normed_quarters(tokens, norm_gain, owner_rows)
    r2 = swap(t2, across)
    r1 = swap(t1, core)
    rest_x = swap(after(mine_x, t2), other)

    def cross(weights, parts):
        return swap(weights, core), tuple((turn ^ 1, plane) for turn, plane in parts)

    own = [(down_weight[None], ((0, 0),))]
    own = own + [cross(*w) for w in own]
    d0 = stacked(
        after(mine, a1, a2, t2, own[1][0]), mine_x, 10**11
    )

    b1 = swap(after(a1, d0, rest_x), other)
    a3 = swap(after(a2, d0), near)
    d2 = swap(after(down_weight[None], d0), far)
    b2 = swap(after(a2, d0, rest_x), other)

    b3 = swap(after(a3, b1, b2), other)
    d1 = swap(after(d0, a3, d2), near)

    e1 = swap(after(d1, b3), other)
    d3 = swap(after(d2, d1), near)
    f2 = swap(after(d2, r2), across)

    second = [(mine_x, ((2, 0),)), (rest_x, ((2, 1),)), (d2, ((8, 0),))]
    second = second + [cross(*w) for w in second]
    r3 = swap(after(r2, b3, d1, *(w for w, _ in second))[owners // 4 :], core)
    weights = (gate_weight, up_weight, a1, b1, a2, b2, a3, b3)
    p0, p1, p2, p3 = partial_sums(
        (t0, r1, r2, r3), weights, (F32, F32, BF16, BF16)
    )
    q1 = swap(p1, core)
    q2 = swap(p2, across)
    q3 = swap(after(p3, q1), both)

    f3 = swap(after(f2, d3, q1)[:, :, :half], near)
    g3 = swap(after(d3, f2, q1)[:, :, half:], across)

    third = [
        (d1, ((4, 0), (6, 0))),
        (e1, ((4, 1), (6, 1))),
        (f2, ((10, 0),)),
        (d3, ((12, 0),)),
    ]
    early = own + second + third
    out = pltpu.HBM(tokens.shape, BF16)
    rows, hid = tokens.shape[0], gate_weight.shape[1]
    product, hidden = down_call(
        first_kernel, "down_first", [seg_counts], [owner_rows, p0, q1, q2, q3], [], early,
        [out, pltpu.HBM((rows, hid), BF16)], [pltpu.SemaphoreType.DMA], {},
    )
    late = [(after(f3, hidden), ((14, 2),)), (after(g3, hidden), ((14, 3),))]
    late = [cross(after(w, q2), parts) for w, parts in third[:2]] + [cross(after(w, hidden), parts) for w, parts in third[2:]] + late + [cross(*w) for w in late]
    return down_call(
        second_kernel, "down_second", [], [owner_rows, hidden], [product], late, [out], [], {2: 0}
    )[0]


def solution(mesh):
    placed = (
        P(("groups", "wide"), None),
        P(),
        P("wide", None),
        P("wide", None),
        P(None, "wide"),
        P(),
        P(("groups", "wide")),
    )
    groups, owners = mesh.shape["groups"], mesh.shape["wide"]
    plan = functools.partial(split, groups, owners) if (groups, owners) == (2, 16) else gathered
    return jax.shard_map(
        plan, mesh=mesh, in_specs=placed, out_specs=P(("groups", "wide"), None), check_vma=False
    )
```

```python
import functools

import jax
import jax.numpy as jnp
from jax import lax
from jax.experimental import pallas as pl
from jax.experimental.pallas import tpu as pltpu
from jax.sharding import PartitionSpec as P

MEM = 16
FULL = 60 << 20
ALL = ("groups", "wide")
F32, BF16 = jnp.float32, jnp.bfloat16
VMEM = pl.BlockSpec(memory_space=pltpu.VMEM)
SMEM = pl.BlockSpec(memory_space=pltpu.SMEM)
HBM = pl.BlockSpec(memory_space=pltpu.HBM)


def gathered(tokens, norm_gain, gate_weight, up_weight, down_weight, owner_rows, seg_counts):
    row_count, model_width = tokens.shape
    owners = lax.axis_size("wide")
    block_rows = model_width // owners
    indices = jnp.arange(owners, dtype=jnp.int32)
    holder = jnp.sum(
        indices[:, None] * (owner_rows[:, None] == indices[None, :]).astype(jnp.int32), axis=0
    )
    features = tokens.astype(F32)
    mean_square = jnp.mean(features * features, axis=1, keepdims=True)
    normed = (features * lax.rsqrt(mean_square + 1e-05) * norm_gain[None, :]).astype(BF16)
    stored = normed.reshape(row_count, owners, block_rows)[:, holder, :].reshape(
        row_count, model_width
    )

    def partial_product(portion):
        return jnp.dot(stored, portion, preferred_element_type=F32)

    gate_sum = partial_product(lax.all_gather(gate_weight, "wide", axis=0, tiled=True))
    up_sum = partial_product(lax.all_gather(up_weight, "wide", axis=0, tiled=True))
    hidden = (jax.nn.silu(gate_sum) * up_sum).astype(BF16)
    stored_out = jnp.dot(
        hidden,
        lax.all_gather(down_weight, "wide", axis=1, tiled=True),
        preferred_element_type=F32,
    ).astype(BF16)
    product = stored_out.reshape(row_count, owners, block_rows)[:, owner_rows, :].reshape(
        row_count, model_width
    )
    live_mask = (jnp.arange(row_count, dtype=jnp.int32) < MEM + seg_counts[0]).astype(BF16)
    return product * live_mask[:, None]


def norm_kernel(owner_ref, tokens_ref, gain_ref, *rest):
    outs, (held, made, scale_ref, in_sem, out_sem) = rest[:2], rest[2:]
    here = lax.axis_index("wide")
    rows, model_width = held.shape
    blocks = owner_ref.shape[0]
    width = model_width // blocks
    step = rows // in_sem.shape[0]
    copies = [
        pltpu.make_async_copy(
            tokens_ref.at[r : r + step], held.at[r : r + step], in_sem.at[r // step]
        )
        for r in range(0, rows, step)
    ]
    for copy in copies:
        copy.start()
    for r, copy in zip(range(0, rows, step), copies):
        copy.wait()
        parts = [jnp.zeros((step, 128), F32) for _ in range(8)]
        for start in range(0, model_width, 128):
            part = held[r : r + step, start : start + 128].astype(F32)
            parts[start // 128 % 8] += part * part
        mean = jnp.sum(sum(parts), axis=1, keepdims=True) / model_width
        scale_ref[r : r + step] = jnp.broadcast_to(lax.rsqrt(mean + 1e-05), (step, 128))
    scale = scale_ref[...]
    for p in range(blocks):
        for start in range(0, width, 128):
            columns = slice(p * width + start, p * width + start + 128)
            normed = held[:, columns].astype(F32) * scale * gain_ref[:, columns]
            made[p, :, start : start + 128] = normed.astype(BF16)
        stored = owner_ref[p]
        for turn, out in enumerate(outs):

            @pl.when(((stored ^ here) & 2) == 2 * turn)
            def _(out=out, p=p, stored=stored):
                place = (stored >> 2) * 2 + (stored & 1)
                pltpu.make_async_copy(made.at[p], out.at[place], out_sem.at[p]).start()

    for p in range(blocks):
        pltpu.make_async_copy(made.at[p], outs[0].at[0], out_sem.at[p]).wait()


def normed_halves(tokens, gain, owner_rows):
    rows, model_width = tokens.shape
    blocks = owner_rows.shape[0]
    width = model_width // blocks
    return pl.pallas_call(
        norm_kernel,
        in_specs=[SMEM, HBM, VMEM],
        out_specs=[HBM] * 2,
        out_shape=[pltpu.HBM((blocks // 2, rows, width), BF16)] * 2,
        scratch_shapes=[
            pltpu.VMEM((rows, model_width), BF16),
            pltpu.VMEM((blocks, rows, width), BF16),
            pltpu.VMEM((rows, 128), F32),
            pltpu.SemaphoreType.DMA((rows // 16,)),
            pltpu.SemaphoreType.DMA((blocks,)),
        ],
        compiler_params=pltpu.CompilerParams(vmem_limit_bytes=FULL),
        cost_estimate=pl.CostEstimate(
            flops=6 * rows * model_width, bytes_accessed=4 * rows * model_width, transcendentals=0
        ),
        name="norm_halves",
    )(owner_rows, tokens, gain.reshape(1, model_width))


def fetch(pairs, sem):
    copies = [pltpu.make_async_copy(r, v, sem.at[i]) for i, (r, v) in enumerate(pairs)]
    for copy in copies:
        copy.start()
    return copies


def partial_kernel(kinds, *refs):
    count = len(kinds)
    made, (rows, held, mine, other, row_sem, sem, out_sem) = refs[-7 - count : -7], refs[-7:]
    outs = refs[-7 - 2 * count : -7 - count]
    inputs, weights = refs[:count], refs[count : -7 - 2 * count]
    here, first = lax.axis_index("wide"), lax.axis_index("groups") == 0
    z, core = here >> 2, here & 1
    size = inputs[0].shape[1]
    hid = held.shape[2]
    hops = len(weights) // 4
    row_copies = fetch(
        [(ref, rows.at[:, k * size : (k + 1) * size]) for k, ref in enumerate(inputs)], row_sem
    )
    order = [(turn * hops + hop) * 2 + side for hop in range(hops) for turn in range(2) for side in range(2)]
    copies = dict(zip(order, fetch([(weights[i], held.at[i]) for i in order], sem)))
    for copy in row_copies:
        copy.wait()

    def summed(total, places, side, turns):
        for hop in turns:
            for turn in range(2):
                total += jnp.dot(
                    rows[(z ^ hop) * 2 + (core ^ turn), places],
                    held[(turn * hops + hop) * 2 + side],
                    preferred_element_type=F32,
                )
        return total

    step = hops // 2
    for start in range(0, hops, step):
        for i in order[4 * start : 4 * (start + step)]:
            copies[i].wait()
        sent = []
        for k, (out, kind) in enumerate(zip(made, kinds)):
            places = slice(k * size, (k + 1) * size)
            turns = range(max(start, 1), start + step)
            if start == 0:
                mine[places] = summed(jnp.zeros((size, hid), F32), places, 0, turns)
                other[places] = summed(jnp.zeros((size, hid), F32), places, 1, turns)
            else:
                a = summed(mine[places], places, 0, turns)
                b = summed(other[places], places, 1, turns)
                out[:, :hid] = summed(jnp.where(first, a, b), places, 0, (0,)).astype(kind)
                out[:, hid:] = summed(jnp.where(first, b, a), places, 1, (0,)).astype(kind)
                sent.append(pltpu.make_async_copy(out, outs[k], out_sem.at[k]))
                sent[-1].start()
    for copy in sent:
        copy.wait()


def partial_sums(inputs, weights, kinds):
    count = len(kinds)
    blocks, rows, depth = inputs[0].shape
    hid = weights[0].shape[1]
    return pl.pallas_call(
        functools.partial(partial_kernel, kinds),
        in_specs=[HBM] * (count + len(weights)),
        out_specs=[HBM] * count,
        out_shape=[pltpu.HBM((rows, 2 * hid), kind) for kind in kinds],
        scratch_shapes=[pltpu.VMEM((rows, 2 * hid), kind) for kind in kinds]
        + [
            pltpu.VMEM((blocks, count * rows, depth), BF16),
            pltpu.VMEM((len(weights), depth, hid), BF16),
            pltpu.VMEM((count * rows, hid), F32),
            pltpu.VMEM((count * rows, hid), F32),
            pltpu.SemaphoreType.DMA((count,)),
            pltpu.SemaphoreType.DMA((len(weights),)),
            pltpu.SemaphoreType.DMA((count,)),
        ],
        compiler_params=pltpu.CompilerParams(vmem_limit_bytes=FULL),
        cost_estimate=pl.CostEstimate(
            flops=4 * blocks * count * rows * depth * hid,
            bytes_accessed=2 * blocks * depth * (count * rows + 2 * hid),
            transcendentals=0,
        ),
        name="partial_sums",
    )(*inputs, *weights)


def multiply_out(hidden, copies, pieces, owner, out, held, results, out_sem, places):
    group, here = lax.axis_index("groups"), lax.axis_index("wide")
    blocks = owner.shape[0]
    block = out.shape[1] // blocks
    for p in range(blocks):
        places[owner[p]] = p * block
    start, sent = 0, []
    for copy, ref, parts in zip(copies, held, pieces):
        copy.wait()
        for k, (turn, plane) in enumerate(parts):
            width = ref.shape[2]
            for n in range(0, width, 256):
                product = jnp.dot(hidden, ref[k, :, n : n + 256], preferred_element_type=F32)
                results[:, start + n : start + n + 256] = product.astype(BF16)
            side = (plane - 2 if plane >= 2 else group ^ plane) if width < block else 0
            place = places[here ^ turn] + side * width
            sent.append(
                pltpu.make_async_copy(
                    results.at[:, start : start + width],
                    out.at[:, pl.ds(pl.multiple_of(place, 128), width)],
                    out_sem.at[len(sent)],
                )
            )
            sent[-1].start()
            start += width
    for copy in sent:
        copy.wait()


def first_kernel(pieces, live_ref, owner_ref, *refs):
    count = len(pieces)
    sums, weights, (out, hidden_ref) = refs[:2], refs[2 : 2 + count], refs[2 + count : 4 + count]
    owner, *rest = refs[4 + count :]
    sums_held, held = rest[:2], rest[2 : 2 + count]
    sem, results, out_sem, places, hidden, hidden_sem = rest[2 + count :]
    first, *copies = fetch(
        list(zip((owner_ref, *sums, *weights), (owner, *sums_held, *held))), sem
    )
    for copy in (first, *copies[:2]):
        copy.wait()
    hid = hidden.shape[1]
    total = sums_held[0][...] + sums_held[1][...].astype(F32)
    gate, up = total[:, :hid], total[:, hid:]
    units = gate / (1.0 + jnp.exp(-gate)) * up
    rows = lax.broadcasted_iota(jnp.int32, units.shape, 0)
    hidden[...] = jnp.where(rows < MEM + live_ref[0], units, 0.0).astype(BF16)
    handed = pltpu.make_async_copy(hidden, hidden_ref, hidden_sem)
    handed.start()
    multiply_out(hidden[...], copies[2:], pieces, owner, out, held, results, out_sem, places)
    handed.wait()


def second_kernel(pieces, owner_ref, hidden_ref, _, *refs):
    count = len(pieces)
    weights, out, owner, held = refs[:count], refs[count], refs[count + 1], refs[count + 2 : 2 * count + 2]
    sem, results, out_sem, places, hidden = refs[2 * count + 2 :]
    first, second, *copies = fetch(
        list(zip((owner_ref, hidden_ref, *weights), (owner, hidden, *held))), sem
    )
    first.wait()
    second.wait()
    multiply_out(hidden[...], copies, pieces, owner, out, held, results, out_sem, places)


def down_call(kernel, name, live, fetched, passed, downs, outs, scratch, aliases):
    weights, pieces = zip(*downs)
    rows = outs[0].shape[0]
    hid = weights[0].shape[1]
    columns = sum(w.size for w in weights) // hid
    places = [pltpu.SMEM(v.shape, v.dtype) for v in fetched[:1]]
    kept = [pltpu.VMEM(v.shape, v.dtype) for v in fetched[1:] if v.shape != (rows, hid)]
    return pl.pallas_call(
        functools.partial(kernel, pieces),
        in_specs=[SMEM] * len(live) + [HBM] * (len(fetched) + len(passed) + len(weights)),
        out_specs=[HBM] * len(outs),
        out_shape=outs,
        scratch_shapes=places
        + kept
        + [pltpu.VMEM(w.shape, w.dtype) for w in weights]
        + [
            pltpu.SemaphoreType.DMA((len(fetched) + len(weights),)),
            pltpu.VMEM((rows, columns), BF16),
            pltpu.SemaphoreType.DMA((sum(len(p) for p in pieces),)),
            *places,
            pltpu.VMEM((rows, hid), BF16),
            *scratch,
        ],
        input_output_aliases=aliases,
        compiler_params=pltpu.CompilerParams(vmem_limit_bytes=FULL),
        cost_estimate=pl.CostEstimate(
            flops=20 * rows * hid * columns,
            bytes_accessed=2 * columns * (rows + hid),
            transcendentals=0,
        ),
        name=name,
    )(*live, *fetched, *passed, *weights)


def stack_kernel(a_ref, b_ref, out_ref):
    out_ref[0] = a_ref[0]
    out_ref[1] = b_ref[0]


def stacked(a, b, flops):
    return pl.pallas_call(
        stack_kernel,
        out_shape=jax.ShapeDtypeStruct((2,) + a.shape[1:], a.dtype),
        compiler_params=pltpu.CompilerParams(vmem_limit_bytes=8 << 20),
        cost_estimate=pl.CostEstimate(flops=flops, bytes_accessed=4 * a.size, transcendentals=0),
        name="stack_halves",
    )(a, b)


def after(value, *others):
    return lax.optimization_barrier((value, *others))[0]


def split(groups, owners, tokens, norm_gain, gate_weight, up_weight, down_weight, owner_rows, seg_counts):
    model_width = tokens.shape[1]
    half = model_width // owners // 2
    group, here = lax.axis_index("groups"), lax.axis_index("wide")
    core, across, near, far, other = (0, 1), (0, 2), (0, 4), (0, 8), (1, 0)

    def swap(value, way):
        pairs = [
            (g * owners + w, (g ^ way[0]) * owners + (w ^ way[1]))
            for g in range(groups)
            for w in range(owners)
        ]
        return lax.ppermute(value, ALL, pairs)

    first = group == 0
    a0 = jnp.where(first, gate_weight, up_weight)
    mine = jnp.where(first, down_weight[:, :half], down_weight[:, half:])[None]

    a1 = swap(a0, near)
    a2 = swap(a0, far)
    mine_x = swap(mine, across)

    t0, t2 = normed_halves(tokens, norm_gain, owner_rows)
    r2 = swap(t2, across)
    rest_x = swap(after(mine_x, t2), other)

    def cross(weights, parts):
        return swap(weights, core), tuple((turn ^ 1, plane) for turn, plane in parts)

    own = [(down_weight[None], ((0, 0),))]
    own = own + [cross(*w) for w in own]
    gate_c, up_c = swap(gate_weight, core), swap(up_weight, core)
    d0 = stacked(
        after(mine, a1, a2, t2, gate_c), mine_x, 10**11
    )

    b1 = swap(after(a1, d0, rest_x), other)
    a3 = swap(after(a2, d0), near)
    d2 = swap(after(down_weight[None], d0), far)
    b2 = swap(after(a2, d0, rest_x), other)

    b3 = swap(after(a3, b1, b2), other)
    d1 = swap(after(d0, a3, d2), near)

    e1 = swap(after(d1, b3), other)
    d3 = swap(after(d2, d1), near)
    f2 = swap(after(d2, r2), across)

    second = [(mine_x, ((2, 0),)), (rest_x, ((2, 1),)), (d2, ((8, 0),))]
    second = second + [cross(*w) for w in second]
    weights = (gate_weight, up_weight, a1, b1, a2, b2, a3, b3)
    weights = weights + (gate_c, up_c) + tuple(swap(w, core) for w in weights[2:])
    p0, p2 = partial_sums((t0, r2), weights, (F32, BF16))
    q2 = swap(p2, across)

    f3 = swap(after(f2, d3, p2)[:, :, :half], near)
    g3 = swap(after(d3, f2, p2)[:, :, half:], across)

    third = [
        (d1, ((4, 0), (6, 0))),
        (e1, ((4, 1), (6, 1))),
        (f2, ((10, 0),)),
        (d3, ((12, 0),)),
    ]
    early = own + second + third
    out = pltpu.HBM(tokens.shape, BF16)
    rows, hid = tokens.shape[0], gate_weight.shape[1]
    product, hidden = down_call(
        first_kernel, "down_first", [seg_counts], [owner_rows, p0, q2], [], early,
        [out, pltpu.HBM((rows, hid), BF16)], [pltpu.SemaphoreType.DMA], {},
    )
    late = [(after(f3, hidden), ((14, 2),)), (after(g3, hidden), ((14, 3),))]
    late = [cross(after(w, q2), parts) for w, parts in third[:2]] + [cross(after(w, hidden), parts) for w, parts in third[2:]] + late + [cross(*w) for w in late]
    return down_call(
        second_kernel, "down_second", [], [owner_rows, hidden], [product], late, [out], [], {2: 0}
    )[0]


def solution(mesh):
    placed = (
        P(("groups", "wide"), None),
        P(),
        P("wide", None),
        P("wide", None),
        P(None, "wide"),
        P(),
        P(("groups", "wide")),
    )
    groups, owners = mesh.shape["groups"], mesh.shape["wide"]
    plan = functools.partial(split, groups, owners) if (groups, owners) == (2, 16) else gathered
    return jax.shard_map(
        plan, mesh=mesh, in_specs=placed, out_specs=P(("groups", "wide"), None), check_vma=False
    )
```

```python
import functools

import jax
import jax.numpy as jnp
from jax import lax
from jax.experimental import pallas as pl
from jax.experimental.pallas import tpu as pltpu
from jax.sharding import PartitionSpec as P

MEM = 16
FULL = 60 << 20
ALL = ("groups", "wide")
F32, BF16 = jnp.float32, jnp.bfloat16
VMEM = pl.BlockSpec(memory_space=pltpu.VMEM)
SMEM = pl.BlockSpec(memory_space=pltpu.SMEM)
HBM = pl.BlockSpec(memory_space=pltpu.HBM)


def gathered(tokens, norm_gain, gate_weight, up_weight, down_weight, owner_rows, seg_counts):
    row_count, model_width = tokens.shape
    owners = lax.axis_size("wide")
    block_rows = model_width // owners
    indices = jnp.arange(owners, dtype=jnp.int32)
    holder = jnp.sum(
        indices[:, None] * (owner_rows[:, None] == indices[None, :]).astype(jnp.int32), axis=0
    )
    features = tokens.astype(F32)
    mean_square = jnp.mean(features * features, axis=1, keepdims=True)
    normed = (features * lax.rsqrt(mean_square + 1e-05) * norm_gain[None, :]).astype(BF16)
    stored = normed.reshape(row_count, owners, block_rows)[:, holder, :].reshape(
        row_count, model_width
    )

    def partial_product(portion):
        return jnp.dot(stored, portion, preferred_element_type=F32)

    gate_sum = partial_product(lax.all_gather(gate_weight, "wide", axis=0, tiled=True))
    up_sum = partial_product(lax.all_gather(up_weight, "wide", axis=0, tiled=True))
    hidden = (jax.nn.silu(gate_sum) * up_sum).astype(BF16)
    stored_out = jnp.dot(
        hidden,
        lax.all_gather(down_weight, "wide", axis=1, tiled=True),
        preferred_element_type=F32,
    ).astype(BF16)
    product = stored_out.reshape(row_count, owners, block_rows)[:, owner_rows, :].reshape(
        row_count, model_width
    )
    live_mask = (jnp.arange(row_count, dtype=jnp.int32) < MEM + seg_counts[0]).astype(BF16)
    return product * live_mask[:, None]


def norm_kernel(owner_ref, tokens_ref, gain_ref, *rest):
    outs, (held, made, scale_ref, in_sem, out_sem) = rest[:2], rest[2:]
    here = lax.axis_index("wide")
    rows, model_width = held.shape
    blocks = owner_ref.shape[0]
    width = model_width // blocks
    step = rows // in_sem.shape[0]
    copies = [
        pltpu.make_async_copy(
            tokens_ref.at[r : r + step], held.at[r : r + step], in_sem.at[r // step]
        )
        for r in range(0, rows, step)
    ]
    for copy in copies:
        copy.start()
    for r, copy in zip(range(0, rows, step), copies):
        copy.wait()
        parts = [jnp.zeros((step, 128), F32) for _ in range(8)]
        for start in range(0, model_width, 128):
            part = held[r : r + step, start : start + 128].astype(F32)
            parts[start // 128 % 8] += part * part
        mean = jnp.sum(sum(parts), axis=1, keepdims=True) / model_width
        scale_ref[r : r + step] = jnp.broadcast_to(lax.rsqrt(mean + 1e-05), (step, 128))
    scale = scale_ref[...]
    for p in range(blocks):
        for start in range(0, width, 128):
            columns = slice(p * width + start, p * width + start + 128)
            normed = held[:, columns].astype(F32) * scale * gain_ref[:, columns]
            made[p, :, start : start + 128] = normed.astype(BF16)
        stored = owner_ref[p]
        for turn, out in enumerate(outs):

            @pl.when(((stored ^ here) & 2) == 2 * turn)
            def _(out=out, p=p, stored=stored):
                place = (stored >> 2) * 2 + (stored & 1)
                pltpu.make_async_copy(made.at[p], out.at[place], out_sem.at[p]).start()

    for p in range(blocks):
        pltpu.make_async_copy(made.at[p], outs[0].at[0], out_sem.at[p]).wait()


def normed_halves(tokens, gain, owner_rows):
    rows, model_width = tokens.shape
    blocks = owner_rows.shape[0]
    width = model_width // blocks
    return pl.pallas_call(
        norm_kernel,
        in_specs=[SMEM, HBM, VMEM],
        out_specs=[HBM] * 2,
        out_shape=[pltpu.HBM((blocks // 2, rows, width), BF16)] * 2,
        scratch_shapes=[
            pltpu.VMEM((rows, model_width), BF16),
            pltpu.VMEM((blocks, rows, width), BF16),
            pltpu.VMEM((rows, 128), F32),
            pltpu.SemaphoreType.DMA((rows // 16,)),
            pltpu.SemaphoreType.DMA((blocks,)),
        ],
        compiler_params=pltpu.CompilerParams(vmem_limit_bytes=FULL),
        cost_estimate=pl.CostEstimate(
            flops=6 * rows * model_width, bytes_accessed=4 * rows * model_width, transcendentals=0
        ),
        name="norm_halves",
    )(owner_rows, tokens, gain.reshape(1, model_width))


def fetch(pairs, sem):
    copies = [pltpu.make_async_copy(r, v, sem.at[i]) for i, (r, v) in enumerate(pairs)]
    for copy in copies:
        copy.start()
    return copies


def partial_kernel(kinds, *refs):
    count = len(kinds)
    made, (rows, held, mine, other, row_sem, sem, out_sem) = refs[-7 - count : -7], refs[-7:]
    outs = refs[-7 - 2 * count : -7 - count]
    inputs, weights = refs[:count], refs[count : -7 - 2 * count]
    here, first = lax.axis_index("wide"), lax.axis_index("groups") == 0
    z, core = here >> 2, here & 1
    size = inputs[0].shape[1]
    hid = held.shape[2]
    hops = len(weights) // 4
    row_copies = fetch(
        [(ref, rows.at[:, k * size : (k + 1) * size]) for k, ref in enumerate(inputs)], row_sem
    )
    order = [(turn * hops + hop) * 2 + side for hop in range(hops) for turn in range(2) for side in range(2)]
    copies = dict(zip(order, fetch([(weights[i], held.at[i]) for i in order], sem)))
    for copy in row_copies:
        copy.wait()

    def summed(total, places, side, turns):
        for hop in turns:
            for turn in range(2):
                total += jnp.dot(
                    rows[(z ^ hop) * 2 + (core ^ turn), places],
                    held[(turn * hops + hop) * 2 + side],
                    preferred_element_type=F32,
                )
        return total

    step = hops // 2
    for start in range(0, hops, step):
        for i in order[4 * start : 4 * (start + step)]:
            copies[i].wait()
        sent = []
        for k, (out, kind) in enumerate(zip(made, kinds)):
            places = slice(k * size, (k + 1) * size)
            turns = range(max(start, 1), start + step)
            if start == 0:
                mine[places] = summed(jnp.zeros((size, hid), F32), places, 0, turns)
                other[places] = summed(jnp.zeros((size, hid), F32), places, 1, turns)
            else:
                a = summed(mine[places], places, 0, turns)
                b = summed(other[places], places, 1, turns)
                out[:, :hid] = summed(jnp.where(first, a, b), places, 0, (0,)).astype(kind)
                out[:, hid:] = summed(jnp.where(first, b, a), places, 1, (0,)).astype(kind)
                sent.append(pltpu.make_async_copy(out, outs[k], out_sem.at[k]))
                sent[-1].start()
    for copy in sent:
        copy.wait()


def partial_sums(inputs, weights, kinds):
    count = len(kinds)
    blocks, rows, depth = inputs[0].shape
    hid = weights[0].shape[1]
    return pl.pallas_call(
        functools.partial(partial_kernel, kinds),
        in_specs=[HBM] * (count + len(weights)),
        out_specs=[HBM] * count,
        out_shape=[pltpu.HBM((rows, 2 * hid), kind) for kind in kinds],
        scratch_shapes=[pltpu.VMEM((rows, 2 * hid), kind) for kind in kinds]
        + [
            pltpu.VMEM((blocks, count * rows, depth), BF16),
            pltpu.VMEM((len(weights), depth, hid), BF16),
            pltpu.VMEM((count * rows, hid), F32),
            pltpu.VMEM((count * rows, hid), F32),
            pltpu.SemaphoreType.DMA((count,)),
            pltpu.SemaphoreType.DMA((len(weights),)),
            pltpu.SemaphoreType.DMA((count,)),
        ],
        compiler_params=pltpu.CompilerParams(vmem_limit_bytes=FULL),
        cost_estimate=pl.CostEstimate(
            flops=4 * blocks * count * rows * depth * hid,
            bytes_accessed=2 * blocks * depth * (count * rows + 2 * hid),
            transcendentals=0,
        ),
        name="partial_sums",
    )(*inputs, *weights)


def multiply_out(hidden, copies, pieces, owner, out, held, results, out_sem, places):
    group, here = lax.axis_index("groups"), lax.axis_index("wide")
    blocks = owner.shape[0]
    block = out.shape[1] // blocks
    for p in range(blocks):
        places[owner[p]] = p * block
    start, sent = 0, []
    for copy, ref, parts in zip(copies, held, pieces):
        copy.wait()
        for k, (turn, plane) in enumerate(parts):
            width = ref.shape[2]
            for n in range(0, width, 256):
                product = jnp.dot(hidden, ref[k, :, n : n + 256], preferred_element_type=F32)
                results[:, start + n : start + n + 256] = product.astype(BF16)
            side = (plane - 2 if plane >= 2 else group ^ plane) if width < block else 0
            place = places[here ^ turn] + side * width
            sent.append(
                pltpu.make_async_copy(
                    results.at[:, start : start + width],
                    out.at[:, pl.ds(pl.multiple_of(place, 128), width)],
                    out_sem.at[len(sent)],
                )
            )
            sent[-1].start()
            start += width
    for copy in sent:
        copy.wait()


def first_kernel(pieces, live_ref, owner_ref, *refs):
    count = len(pieces)
    sums, weights, (out, hidden_ref) = refs[:2], refs[2 : 2 + count], refs[2 + count : 4 + count]
    owner, *rest = refs[4 + count :]
    sums_held, held = rest[:2], rest[2 : 2 + count]
    sem, results, out_sem, places, hidden, hidden_sem = rest[2 + count :]
    first, *copies = fetch(
        list(zip((owner_ref, *sums, *weights), (owner, *sums_held, *held))), sem
    )
    for copy in (first, *copies[:2]):
        copy.wait()
    hid = hidden.shape[1]
    total = sums_held[0][...] + sums_held[1][...].astype(F32)
    gate, up = total[:, :hid], total[:, hid:]
    units = gate / (1.0 + jnp.exp(-gate)) * up
    rows = lax.broadcasted_iota(jnp.int32, units.shape, 0)
    hidden[...] = jnp.where(rows < MEM + live_ref[0], units, 0.0).astype(BF16)
    handed = pltpu.make_async_copy(hidden, hidden_ref, hidden_sem)
    handed.start()
    multiply_out(hidden[...], copies[2:], pieces, owner, out, held, results, out_sem, places)
    handed.wait()


def second_kernel(pieces, owner_ref, hidden_ref, _, *refs):
    count = len(pieces)
    weights, out, owner, held = refs[:count], refs[count], refs[count + 1], refs[count + 2 : 2 * count + 2]
    sem, results, out_sem, places, hidden = refs[2 * count + 2 :]
    first, second, *copies = fetch(
        list(zip((owner_ref, hidden_ref, *weights), (owner, hidden, *held))), sem
    )
    first.wait()
    second.wait()
    multiply_out(hidden[...], copies, pieces, owner, out, held, results, out_sem, places)


def down_call(kernel, name, live, fetched, passed, downs, outs, scratch, aliases):
    weights, pieces = zip(*downs)
    rows = outs[0].shape[0]
    hid = weights[0].shape[1]
    columns = sum(w.size for w in weights) // hid
    places = [pltpu.SMEM(v.shape, v.dtype) for v in fetched[:1]]
    kept = [pltpu.VMEM(v.shape, v.dtype) for v in fetched[1:] if v.shape != (rows, hid)]
    return pl.pallas_call(
        functools.partial(kernel, pieces),
        in_specs=[SMEM] * len(live) + [HBM] * (len(fetched) + len(passed) + len(weights)),
        out_specs=[HBM] * len(outs),
        out_shape=outs,
        scratch_shapes=places
        + kept
        + [pltpu.VMEM(w.shape, w.dtype) for w in weights]
        + [
            pltpu.SemaphoreType.DMA((len(fetched) + len(weights),)),
            pltpu.VMEM((rows, columns), BF16),
            pltpu.SemaphoreType.DMA((sum(len(p) for p in pieces),)),
            *places,
            pltpu.VMEM((rows, hid), BF16),
            *scratch,
        ],
        input_output_aliases=aliases,
        compiler_params=pltpu.CompilerParams(vmem_limit_bytes=FULL),
        cost_estimate=pl.CostEstimate(
            flops=20 * rows * hid * columns,
            bytes_accessed=2 * columns * (rows + hid),
            transcendentals=0,
        ),
        name=name,
    )(*live, *fetched, *passed, *weights)


def stack_kernel(a_ref, b_ref, out_ref):
    out_ref[0] = a_ref[0]
    out_ref[1] = b_ref[0]


def stacked(a, b, flops):
    return pl.pallas_call(
        stack_kernel,
        out_shape=jax.ShapeDtypeStruct((2,) + a.shape[1:], a.dtype),
        compiler_params=pltpu.CompilerParams(vmem_limit_bytes=8 << 20),
        cost_estimate=pl.CostEstimate(flops=flops, bytes_accessed=4 * a.size, transcendentals=0),
        name="stack_halves",
    )(a, b)


def after(value, *others):
    return lax.optimization_barrier((value, *others))[0]


def split(groups, owners, tokens, norm_gain, gate_weight, up_weight, down_weight, owner_rows, seg_counts):
    model_width = tokens.shape[1]
    half = model_width // owners // 2
    group, here = lax.axis_index("groups"), lax.axis_index("wide")
    core, across, near, far, other = (0, 1), (0, 2), (0, 4), (0, 8), (1, 0)

    def swap(value, way):
        pairs = [
            (g * owners + w, (g ^ way[0]) * owners + (w ^ way[1]))
            for g in range(groups)
            for w in range(owners)
        ]
        return lax.ppermute(value, ALL, pairs)

    first = group == 0
    a0 = jnp.where(first, gate_weight, up_weight)
    mine = jnp.where(first, down_weight[:, :half], down_weight[:, half:])[None]

    a1 = swap(a0, near)
    a2 = swap(a0, far)
    mine_x = swap(mine, across)

    t0, t2 = normed_halves(tokens, norm_gain, owner_rows)
    r2 = swap(t2, across)
    rest_x = swap(after(mine_x, t2), other)

    def cross(weights, parts):
        return swap(weights, core), tuple((turn ^ 1, plane) for turn, plane in parts)

    own = [(down_weight[None], ((0, 0),))]
    own = own + [cross(*w) for w in own]
    gate_c, up_c = swap(gate_weight, core), swap(up_weight, core)
    d0 = stacked(
        after(mine, a1, a2, t2, gate_c), mine_x, 10**11
    )

    b1 = swap(after(a1, d0, rest_x), other)
    a3 = swap(after(a2, d0), near)
    d2 = swap(after(down_weight[None], d0), far)
    b2 = swap(after(a2, d0, rest_x), other)

    b3 = swap(after(a3, b1, b2), other)
    d1 = swap(after(d0, a3, d2), near)

    e1 = swap(after(d1, b3), other)
    d3 = swap(after(d2, d1), near)
    f2 = swap(after(d2, r2), across)

    second = [(mine_x, ((2, 0),)), (rest_x, ((2, 1),)), (d2, ((8, 0),))]
    second = second + [cross(*w) for w in second]
    weights = (gate_weight, up_weight, a1, b1, a2, b2, a3, b3)
    weights = weights + (gate_c, up_c) + tuple(swap(w, core) for w in weights[2:])
    crossings = (own[1][0], *(w for w, _ in second[3:]))
    p0, p2 = partial_sums((after(t0, *crossings), r2), weights, (F32, BF16))
    q2 = swap(p2, across)

    f3 = swap(after(f2, d3, p2)[:, :, :half], near)
    g3 = swap(after(d3, f2, p2)[:, :, half:], across)

    third = [
        (d1, ((4, 0), (6, 0))),
        (e1, ((4, 1), (6, 1))),
        (f2, ((10, 0),)),
        (d3, ((12, 0),)),
    ]
    early = own + second + third
    out = pltpu.HBM(tokens.shape, BF16)
    rows, hid = tokens.shape[0], gate_weight.shape[1]
    product, hidden = down_call(
        first_kernel, "down_first", [seg_counts], [owner_rows, p0, q2], [], early,
        [out, pltpu.HBM((rows, hid), BF16)], [pltpu.SemaphoreType.DMA], {},
    )
    late = [(after(f3, hidden), ((14, 2),)), (after(g3, hidden), ((14, 3),))]
    late = [cross(after(w, hidden), parts) for w, parts in third[:2]] + [cross(after(w, hidden), parts) for w, parts in third[2:]] + late + [cross(*w) for w in late]
    return down_call(
        second_kernel, "down_second", [], [owner_rows, hidden], [product], late, [out], [], {2: 0}
    )[0]


def solution(mesh):
    placed = (
        P(("groups", "wide"), None),
        P(),
        P("wide", None),
        P("wide", None),
        P(None, "wide"),
        P(),
        P(("groups", "wide")),
    )
    groups, owners = mesh.shape["groups"], mesh.shape["wide"]
    plan = functools.partial(split, groups, owners) if (groups, owners) == (2, 16) else gathered
    return jax.shard_map(
        plan, mesh=mesh, in_specs=placed, out_specs=P(("groups", "wide"), None), check_vma=False
    )
```

```python
import functools

import jax
import jax.numpy as jnp
from jax import lax
from jax.experimental import pallas as pl
from jax.experimental.pallas import tpu as pltpu
from jax.sharding import PartitionSpec as P

MEM = 16
FULL = 60 << 20
ALL = ("groups", "wide")
F32, BF16 = jnp.float32, jnp.bfloat16
VMEM = pl.BlockSpec(memory_space=pltpu.VMEM)
SMEM = pl.BlockSpec(memory_space=pltpu.SMEM)
HBM = pl.BlockSpec(memory_space=pltpu.HBM)


def gathered(tokens, norm_gain, gate_weight, up_weight, down_weight, owner_rows, seg_counts):
    row_count, model_width = tokens.shape
    owners = lax.axis_size("wide")
    block_rows = model_width // owners
    indices = jnp.arange(owners, dtype=jnp.int32)
    holder = jnp.sum(
        indices[:, None] * (owner_rows[:, None] == indices[None, :]).astype(jnp.int32), axis=0
    )
    features = tokens.astype(F32)
    mean_square = jnp.mean(features * features, axis=1, keepdims=True)
    normed = (features * lax.rsqrt(mean_square + 1e-05) * norm_gain[None, :]).astype(BF16)
    stored = normed.reshape(row_count, owners, block_rows)[:, holder, :].reshape(
        row_count, model_width
    )

    def partial_product(portion):
        return jnp.dot(stored, portion, preferred_element_type=F32)

    gate_sum = partial_product(lax.all_gather(gate_weight, "wide", axis=0, tiled=True))
    up_sum = partial_product(lax.all_gather(up_weight, "wide", axis=0, tiled=True))
    hidden = (jax.nn.silu(gate_sum) * up_sum).astype(BF16)
    stored_out = jnp.dot(
        hidden,
        lax.all_gather(down_weight, "wide", axis=1, tiled=True),
        preferred_element_type=F32,
    ).astype(BF16)
    product = stored_out.reshape(row_count, owners, block_rows)[:, owner_rows, :].reshape(
        row_count, model_width
    )
    live_mask = (jnp.arange(row_count, dtype=jnp.int32) < MEM + seg_counts[0]).astype(BF16)
    return product * live_mask[:, None]


def norm_kernel(owner_ref, tokens_ref, gain_ref, *rest):
    outs, (held, made, scale_ref, in_sem, out_sem) = rest[:2], rest[2:]
    here = lax.axis_index("wide")
    rows, model_width = held.shape
    blocks = owner_ref.shape[0]
    width = model_width // blocks
    step = rows // in_sem.shape[0]
    copies = [
        pltpu.make_async_copy(
            tokens_ref.at[r : r + step], held.at[r : r + step], in_sem.at[r // step]
        )
        for r in range(0, rows, step)
    ]
    for copy in copies:
        copy.start()
    for r, copy in zip(range(0, rows, step), copies):
        copy.wait()
        parts = [jnp.zeros((step, 128), F32) for _ in range(8)]
        for start in range(0, model_width, 128):
            part = held[r : r + step, start : start + 128].astype(F32)
            parts[start // 128 % 8] += part * part
        mean = jnp.sum(sum(parts), axis=1, keepdims=True) / model_width
        scale_ref[r : r + step] = jnp.broadcast_to(lax.rsqrt(mean + 1e-05), (step, 128))
    scale = scale_ref[...]
    for p in range(blocks):
        for start in range(0, width, 128):
            columns = slice(p * width + start, p * width + start + 128)
            normed = held[:, columns].astype(F32) * scale * gain_ref[:, columns]
            made[p, :, start : start + 128] = normed.astype(BF16)
        stored = owner_ref[p]
        for turn, out in enumerate(outs):

            @pl.when(((stored ^ here) & 2) == 2 * turn)
            def _(out=out, p=p, stored=stored):
                place = (stored >> 2) * 2 + (stored & 1)
                pltpu.make_async_copy(made.at[p], out.at[place], out_sem.at[p]).start()

    for p in range(blocks):
        pltpu.make_async_copy(made.at[p], outs[0].at[0], out_sem.at[p]).wait()


def normed_halves(tokens, gain, owner_rows):
    rows, model_width = tokens.shape
    blocks = owner_rows.shape[0]
    width = model_width // blocks
    return pl.pallas_call(
        norm_kernel,
        in_specs=[SMEM, HBM, VMEM],
        out_specs=[HBM] * 2,
        out_shape=[pltpu.HBM((blocks // 2, rows, width), BF16)] * 2,
        scratch_shapes=[
            pltpu.VMEM((rows, model_width), BF16),
            pltpu.VMEM((blocks, rows, width), BF16),
            pltpu.VMEM((rows, 128), F32),
            pltpu.SemaphoreType.DMA((rows // 16,)),
            pltpu.SemaphoreType.DMA((blocks,)),
        ],
        compiler_params=pltpu.CompilerParams(vmem_limit_bytes=FULL),
        cost_estimate=pl.CostEstimate(
            flops=6 * rows * model_width, bytes_accessed=4 * rows * model_width, transcendentals=0
        ),
        name="norm_halves",
    )(owner_rows, tokens, gain.reshape(1, model_width))


def fetch(pairs, sem):
    copies = [pltpu.make_async_copy(r, v, sem.at[i]) for i, (r, v) in enumerate(pairs)]
    for copy in copies:
        copy.start()
    return copies


def partial_kernel(kinds, *refs):
    count = len(kinds)
    made, (rows, held, mine, other, row_sem, sem, out_sem) = refs[-7 - count : -7], refs[-7:]
    outs = refs[-7 - 2 * count : -7 - count]
    inputs, weights = refs[:count], refs[count : -7 - 2 * count]
    here, first = lax.axis_index("wide"), lax.axis_index("groups") == 0
    z, core = here >> 2, here & 1
    size = inputs[0].shape[1]
    hid = held.shape[2]
    hops = len(weights) // 4
    row_copies = fetch(
        [(ref, rows.at[:, k * size : (k + 1) * size]) for k, ref in enumerate(inputs)], row_sem
    )
    order = [(turn * hops + hop) * 2 + side for hop in range(hops) for turn in range(2) for side in range(2)]
    copies = dict(zip(order, fetch([(weights[i], held.at[i]) for i in order], sem)))
    for copy in row_copies:
        copy.wait()

    def summed(total, places, side, turns):
        for hop in turns:
            for turn in range(2):
                total += jnp.dot(
                    rows[(z ^ hop) * 2 + (core ^ turn), places],
                    held[(turn * hops + hop) * 2 + side],
                    preferred_element_type=F32,
                )
        return total

    step = hops // 2
    for start in range(0, hops, step):
        for i in order[4 * start : 4 * (start + step)]:
            copies[i].wait()
        sent = []
        for k, (out, kind) in enumerate(zip(made, kinds)):
            places = slice(k * size, (k + 1) * size)
            turns = range(max(start, 1), start + step)
            if start == 0:
                mine[places] = summed(jnp.zeros((size, hid), F32), places, 0, turns)
                other[places] = summed(jnp.zeros((size, hid), F32), places, 1, turns)
            else:
                a = summed(mine[places], places, 0, turns)
                b = summed(other[places], places, 1, turns)
                out[:, :hid] = summed(jnp.where(first, a, b), places, 0, (0,)).astype(kind)
                out[:, hid:] = summed(jnp.where(first, b, a), places, 1, (0,)).astype(kind)
                sent.append(pltpu.make_async_copy(out, outs[k], out_sem.at[k]))
                sent[-1].start()
    for copy in sent:
        copy.wait()


def partial_sums(inputs, weights, kinds):
    count = len(kinds)
    blocks, rows, depth = inputs[0].shape
    hid = weights[0].shape[1]
    return pl.pallas_call(
        functools.partial(partial_kernel, kinds),
        in_specs=[HBM] * (count + len(weights)),
        out_specs=[HBM] * count,
        out_shape=[pltpu.HBM((rows, 2 * hid), kind) for kind in kinds],
        scratch_shapes=[pltpu.VMEM((rows, 2 * hid), kind) for kind in kinds]
        + [
            pltpu.VMEM((blocks, count * rows, depth), BF16),
            pltpu.VMEM((len(weights), depth, hid), BF16),
            pltpu.VMEM((count * rows, hid), F32),
            pltpu.VMEM((count * rows, hid), F32),
            pltpu.SemaphoreType.DMA((count,)),
            pltpu.SemaphoreType.DMA((len(weights),)),
            pltpu.SemaphoreType.DMA((count,)),
        ],
        compiler_params=pltpu.CompilerParams(vmem_limit_bytes=FULL),
        cost_estimate=pl.CostEstimate(
            flops=4 * blocks * count * rows * depth * hid,
            bytes_accessed=2 * blocks * depth * (count * rows + 2 * hid),
            transcendentals=0,
        ),
        name="partial_sums",
    )(*inputs, *weights)


def multiply_out(hidden, copies, pieces, owner, out, held, results, out_sem, places):
    group, here = lax.axis_index("groups"), lax.axis_index("wide")
    blocks = owner.shape[0]
    block = out.shape[1] // blocks
    for p in range(blocks):
        places[owner[p]] = p * block
    start, sent = 0, []
    for copy, ref, parts in zip(copies, held, pieces):
        copy.wait()
        for k, (turn, plane) in enumerate(parts):
            width = ref.shape[2]
            for n in range(0, width, 256):
                product = jnp.dot(hidden, ref[k, :, n : n + 256], preferred_element_type=F32)
                results[:, start + n : start + n + 256] = product.astype(BF16)
            side = (plane - 2 if plane >= 2 else group ^ plane) if width < block else 0
            place = places[here ^ turn] + side * width
            sent.append(
                pltpu.make_async_copy(
                    results.at[:, start : start + width],
                    out.at[:, pl.ds(pl.multiple_of(place, 128), width)],
                    out_sem.at[len(sent)],
                )
            )
            sent[-1].start()
            start += width
    for copy in sent:
        copy.wait()


def first_kernel(pieces, live_ref, owner_ref, *refs):
    count = len(pieces)
    sums, weights, (out, hidden_ref) = refs[:2], refs[2 : 2 + count], refs[2 + count : 4 + count]
    owner, *rest = refs[4 + count :]
    sums_held, held = rest[:2], rest[2 : 2 + count]
    sem, results, out_sem, places, hidden, hidden_sem = rest[2 + count :]
    first, *copies = fetch(
        list(zip((owner_ref, *sums, *weights), (owner, *sums_held, *held))), sem
    )
    for copy in (first, *copies[:2]):
        copy.wait()
    hid = hidden.shape[1]
    total = sums_held[0][...] + sums_held[1][...].astype(F32)
    gate, up = total[:, :hid], total[:, hid:]
    units = gate / (1.0 + jnp.exp(-gate)) * up
    rows = lax.broadcasted_iota(jnp.int32, units.shape, 0)
    hidden[...] = jnp.where(rows < MEM + live_ref[0], units, 0.0).astype(BF16)
    handed = pltpu.make_async_copy(hidden, hidden_ref, hidden_sem)
    handed.start()
    multiply_out(hidden[...], copies[2:], pieces, owner, out, held, results, out_sem, places)
    handed.wait()


def second_kernel(pieces, owner_ref, hidden_ref, _, *refs):
    count = len(pieces)
    weights, out, owner, held = refs[:count], refs[count], refs[count + 1], refs[count + 2 : 2 * count + 2]
    sem, results, out_sem, places, hidden = refs[2 * count + 2 :]
    first, second, *copies = fetch(
        list(zip((owner_ref, hidden_ref, *weights), (owner, hidden, *held))), sem
    )
    first.wait()
    second.wait()
    multiply_out(hidden[...], copies, pieces, owner, out, held, results, out_sem, places)


def down_call(kernel, name, live, fetched, passed, downs, outs, scratch, aliases):
    weights, pieces = zip(*downs)
    rows = outs[0].shape[0]
    hid = weights[0].shape[1]
    columns = sum(w.size for w in weights) // hid
    places = [pltpu.SMEM(v.shape, v.dtype) for v in fetched[:1]]
    kept = [pltpu.VMEM(v.shape, v.dtype) for v in fetched[1:] if v.shape != (rows, hid)]
    return pl.pallas_call(
        functools.partial(kernel, pieces),
        in_specs=[SMEM] * len(live) + [HBM] * (len(fetched) + len(passed) + len(weights)),
        out_specs=[HBM] * len(outs),
        out_shape=outs,
        scratch_shapes=places
        + kept
        + [pltpu.VMEM(w.shape, w.dtype) for w in weights]
        + [
            pltpu.SemaphoreType.DMA((len(fetched) + len(weights),)),
            pltpu.VMEM((rows, columns), BF16),
            pltpu.SemaphoreType.DMA((sum(len(p) for p in pieces),)),
            *places,
            pltpu.VMEM((rows, hid), BF16),
            *scratch,
        ],
        input_output_aliases=aliases,
        compiler_params=pltpu.CompilerParams(vmem_limit_bytes=FULL),
        cost_estimate=pl.CostEstimate(
            flops=20 * rows * hid * columns,
            bytes_accessed=2 * columns * (rows + hid),
            transcendentals=0,
        ),
        name=name,
    )(*live, *fetched, *passed, *weights)


def stack_kernel(a_ref, b_ref, out_ref):
    out_ref[0] = a_ref[0]
    out_ref[1] = b_ref[0]


def stacked(a, b, flops):
    return pl.pallas_call(
        stack_kernel,
        out_shape=jax.ShapeDtypeStruct((2,) + a.shape[1:], a.dtype),
        compiler_params=pltpu.CompilerParams(vmem_limit_bytes=8 << 20),
        cost_estimate=pl.CostEstimate(flops=flops, bytes_accessed=4 * a.size, transcendentals=0),
        name="stack_halves",
    )(a, b)


def after(value, *others):
    return lax.optimization_barrier((value, *others))[0]


def split(groups, owners, tokens, norm_gain, gate_weight, up_weight, down_weight, owner_rows, seg_counts):
    model_width = tokens.shape[1]
    half = model_width // owners // 2
    group, here = lax.axis_index("groups"), lax.axis_index("wide")
    core, across, near, far, other = (0, 1), (0, 2), (0, 4), (0, 8), (1, 0)

    def swap(value, way):
        pairs = [
            (g * owners + w, (g ^ way[0]) * owners + (w ^ way[1]))
            for g in range(groups)
            for w in range(owners)
        ]
        return lax.ppermute(value, ALL, pairs)

    first = group == 0
    a0 = jnp.where(first, gate_weight, up_weight)
    mine = jnp.where(first, down_weight[:, :half], down_weight[:, half:])[None]

    a1 = swap(a0, near)
    a2 = swap(a0, far)
    mine_x = swap(mine, across)

    t0, t2 = normed_halves(tokens, norm_gain, owner_rows)
    r2 = swap(t2, across)
    rest_x = swap(after(mine_x, t2), other)

    def cross(weights, parts):
        return swap(weights, core), tuple((turn ^ 1, plane) for turn, plane in parts)

    own = [(down_weight[None], ((0, 0),))]
    gate_c = swap(gate_weight, core)
    d0 = stacked(
        after(mine, a1, a2, t2, gate_c, rest_x), mine_x, 10**11
    )

    b1 = swap(after(a1, d0, rest_x), other)
    a3 = swap(after(a2, d0), near)
    d2 = swap(after(down_weight[None], d0), far)
    b2 = swap(after(a2, d0, rest_x), other)

    b3 = swap(after(a3, b1, b2), other)
    d1 = swap(after(d0, a3, d2), near)

    e1 = swap(after(d1, b3), other)
    d3 = swap(after(d2, d1), near)
    f2 = swap(after(d2, r2), across)

    second = own + [(mine_x, ((2, 0),)), (rest_x, ((2, 1),)), (d2, ((8, 0),))]
    second = second + [cross(after(w, a3), parts) for w, parts in second]
    weights = (gate_weight, up_weight, a1, b1, a2, b2, a3, b3)
    weights = weights + (gate_c, swap(after(up_weight, a3), core)) + tuple(swap(w, core) for w in weights[2:])
    crossings = [w for w, _ in second[4:]]
    p0, p2 = partial_sums((after(t0, *crossings), r2), weights, (F32, BF16))
    q2 = swap(p2, across)

    f3 = swap(after(f2, d3, p2)[:, :, :half], near)
    g3 = swap(after(d3, f2, p2)[:, :, half:], across)

    third = [
        (d1, ((4, 0), (6, 0))),
        (e1, ((4, 1), (6, 1))),
        (f2, ((10, 0),)),
        (d3, ((12, 0),)),
    ]
    early = second + third
    out = pltpu.HBM(tokens.shape, BF16)
    rows, hid = tokens.shape[0], gate_weight.shape[1]
    product, hidden = down_call(
        first_kernel, "down_first", [seg_counts], [owner_rows, p0, q2], [], early,
        [out, pltpu.HBM((rows, hid), BF16)], [pltpu.SemaphoreType.DMA], {},
    )
    late = [(after(f3, hidden), ((14, 2),)), (after(g3, hidden), ((14, 3),))]
    late = [cross(after(w, hidden), parts) for w, parts in third[:2]] + [cross(after(w, hidden), parts) for w, parts in third[2:]] + late + [cross(*w) for w in late]
    return down_call(
        second_kernel, "down_second", [], [owner_rows, hidden], [product], late, [out], [], {2: 0}
    )[0]


def solution(mesh):
    placed = (
        P(("groups", "wide"), None),
        P(),
        P("wide", None),
        P("wide", None),
        P(None, "wide"),
        P(),
        P(("groups", "wide")),
    )
    groups, owners = mesh.shape["groups"], mesh.shape["wide"]
    plan = functools.partial(split, groups, owners) if (groups, owners) == (2, 16) else gathered
    return jax.shard_map(
        plan, mesh=mesh, in_specs=placed, out_specs=P(("groups", "wide"), None), check_vma=False
    )
```

```python
import functools

import jax
import jax.numpy as jnp
from jax import lax
from jax.experimental import pallas as pl
from jax.experimental.pallas import tpu as pltpu
from jax.sharding import PartitionSpec as P

MEM = 16
FULL = 60 << 20
ALL = ("groups", "wide")
F32, BF16 = jnp.float32, jnp.bfloat16
VMEM = pl.BlockSpec(memory_space=pltpu.VMEM)
SMEM = pl.BlockSpec(memory_space=pltpu.SMEM)
HBM = pl.BlockSpec(memory_space=pltpu.HBM)


def gathered(tokens, norm_gain, gate_weight, up_weight, down_weight, owner_rows, seg_counts):
    row_count, model_width = tokens.shape
    owners = lax.axis_size("wide")
    block_rows = model_width // owners
    indices = jnp.arange(owners, dtype=jnp.int32)
    holder = jnp.sum(
        indices[:, None] * (owner_rows[:, None] == indices[None, :]).astype(jnp.int32), axis=0
    )
    features = tokens.astype(F32)
    mean_square = jnp.mean(features * features, axis=1, keepdims=True)
    normed = (features * lax.rsqrt(mean_square + 1e-05) * norm_gain[None, :]).astype(BF16)
    stored = normed.reshape(row_count, owners, block_rows)[:, holder, :].reshape(
        row_count, model_width
    )

    def partial_product(portion):
        return jnp.dot(stored, portion, preferred_element_type=F32)

    gate_sum = partial_product(lax.all_gather(gate_weight, "wide", axis=0, tiled=True))
    up_sum = partial_product(lax.all_gather(up_weight, "wide", axis=0, tiled=True))
    hidden = (jax.nn.silu(gate_sum) * up_sum).astype(BF16)
    stored_out = jnp.dot(
        hidden,
        lax.all_gather(down_weight, "wide", axis=1, tiled=True),
        preferred_element_type=F32,
    ).astype(BF16)
    product = stored_out.reshape(row_count, owners, block_rows)[:, owner_rows, :].reshape(
        row_count, model_width
    )
    live_mask = (jnp.arange(row_count, dtype=jnp.int32) < MEM + seg_counts[0]).astype(BF16)
    return product * live_mask[:, None]


def norm_kernel(owner_ref, tokens_ref, gain_ref, *rest):
    outs, (held, made, scale_ref, in_sem, out_sem) = rest[:2], rest[2:]
    here = lax.axis_index("wide")
    rows, model_width = held.shape
    blocks = owner_ref.shape[0]
    width = model_width // blocks
    step = rows // in_sem.shape[0]
    copies = [
        pltpu.make_async_copy(
            tokens_ref.at[r : r + step], held.at[r : r + step], in_sem.at[r // step]
        )
        for r in range(0, rows, step)
    ]
    for copy in copies:
        copy.start()
    for r, copy in zip(range(0, rows, step), copies):
        copy.wait()
        parts = [jnp.zeros((step, 128), F32) for _ in range(8)]
        for start in range(0, model_width, 128):
            part = held[r : r + step, start : start + 128].astype(F32)
            parts[start // 128 % 8] += part * part
        mean = jnp.sum(sum(parts), axis=1, keepdims=True) / model_width
        scale_ref[r : r + step] = jnp.broadcast_to(lax.rsqrt(mean + 1e-05), (step, 128))
    scale = scale_ref[...]
    for p in range(blocks):
        for start in range(0, width, 128):
            columns = slice(p * width + start, p * width + start + 128)
            normed = held[:, columns].astype(F32) * scale * gain_ref[:, columns]
            made[p, :, start : start + 128] = normed.astype(BF16)
        stored = owner_ref[p]
        for turn, out in enumerate(outs):

            @pl.when(((stored ^ here) & 2) == 2 * turn)
            def _(out=out, p=p, stored=stored):
                place = (stored >> 2) * 2 + (stored & 1)
                pltpu.make_async_copy(made.at[p], out.at[place], out_sem.at[p]).start()

    for p in range(blocks):
        pltpu.make_async_copy(made.at[p], outs[0].at[0], out_sem.at[p]).wait()


def normed_halves(tokens, gain, owner_rows):
    rows, model_width = tokens.shape
    blocks = owner_rows.shape[0]
    width = model_width // blocks
    return pl.pallas_call(
        norm_kernel,
        in_specs=[SMEM, HBM, VMEM],
        out_specs=[HBM] * 2,
        out_shape=[pltpu.HBM((blocks // 2, rows, width), BF16)] * 2,
        scratch_shapes=[
            pltpu.VMEM((rows, model_width), BF16),
            pltpu.VMEM((blocks, rows, width), BF16),
            pltpu.VMEM((rows, 128), F32),
            pltpu.SemaphoreType.DMA((rows // 16,)),
            pltpu.SemaphoreType.DMA((blocks,)),
        ],
        compiler_params=pltpu.CompilerParams(vmem_limit_bytes=FULL),
        cost_estimate=pl.CostEstimate(
            flops=6 * rows * model_width, bytes_accessed=4 * rows * model_width, transcendentals=0
        ),
        name="norm_halves",
    )(owner_rows, tokens, gain.reshape(1, model_width))


def fetch(pairs, sem):
    copies = [pltpu.make_async_copy(r, v, sem.at[i]) for i, (r, v) in enumerate(pairs)]
    for copy in copies:
        copy.start()
    return copies


def partial_kernel(kinds, *refs):
    count = len(kinds)
    made, (rows, held, mine, other, row_sem, sem, out_sem) = refs[-7 - count : -7], refs[-7:]
    outs = refs[-7 - 2 * count : -7 - count]
    inputs, weights = refs[:count], refs[count : -7 - 2 * count]
    here, first = lax.axis_index("wide"), lax.axis_index("groups") == 0
    z, core = here >> 2, here & 1
    size = inputs[0].shape[1]
    hid = held.shape[2]
    hops = len(weights) // 4
    row_copies = fetch(
        [(ref, rows.at[:, k * size : (k + 1) * size]) for k, ref in enumerate(inputs)], row_sem
    )
    order = [(turn * hops + hop) * 2 + side for hop in range(hops) for turn in range(2) for side in range(2)]
    copies = dict(zip(order, fetch([(weights[i], held.at[i]) for i in order], sem)))
    for copy in row_copies:
        copy.wait()

    def summed(total, places, side, turns):
        for hop in turns:
            for turn in range(2):
                total += jnp.dot(
                    rows[(z ^ hop) * 2 + (core ^ turn), places],
                    held[(turn * hops + hop) * 2 + side],
                    preferred_element_type=F32,
                )
        return total

    step = hops // 2
    for start in range(0, hops, step):
        for i in order[4 * start : 4 * (start + step)]:
            copies[i].wait()
        sent = []
        for k, (out, kind) in enumerate(zip(made, kinds)):
            places = slice(k * size, (k + 1) * size)
            turns = range(max(start, 1), start + step)
            if start == 0:
                mine[places] = summed(jnp.zeros((size, hid), F32), places, 0, turns)
                other[places] = summed(jnp.zeros((size, hid), F32), places, 1, turns)
            else:
                a = summed(mine[places], places, 0, turns)
                b = summed(other[places], places, 1, turns)
                out[:, :hid] = summed(jnp.where(first, a, b), places, 0, (0,)).astype(kind)
                out[:, hid:] = summed(jnp.where(first, b, a), places, 1, (0,)).astype(kind)
                sent.append(pltpu.make_async_copy(out, outs[k], out_sem.at[k]))
                sent[-1].start()
    for copy in sent:
        copy.wait()


def partial_sums(inputs, weights, kinds):
    count = len(kinds)
    blocks, rows, depth = inputs[0].shape
    hid = weights[0].shape[1]
    return pl.pallas_call(
        functools.partial(partial_kernel, kinds),
        in_specs=[HBM] * (count + len(weights)),
        out_specs=[HBM] * count,
        out_shape=[pltpu.HBM((rows, 2 * hid), kind) for kind in kinds],
        scratch_shapes=[pltpu.VMEM((rows, 2 * hid), kind) for kind in kinds]
        + [
            pltpu.VMEM((blocks, count * rows, depth), BF16),
            pltpu.VMEM((len(weights), depth, hid), BF16),
            pltpu.VMEM((count * rows, hid), F32),
            pltpu.VMEM((count * rows, hid), F32),
            pltpu.SemaphoreType.DMA((count,)),
            pltpu.SemaphoreType.DMA((len(weights),)),
            pltpu.SemaphoreType.DMA((count,)),
        ],
        compiler_params=pltpu.CompilerParams(vmem_limit_bytes=FULL),
        cost_estimate=pl.CostEstimate(
            flops=4 * blocks * count * rows * depth * hid,
            bytes_accessed=2 * blocks * depth * (count * rows + 2 * hid),
            transcendentals=0,
        ),
        name="partial_sums",
    )(*inputs, *weights)


def multiply_out(hidden, copies, pieces, owner, out, held, results, out_sem, places):
    group, here = lax.axis_index("groups"), lax.axis_index("wide")
    blocks = owner.shape[0]
    block = out.shape[1] // blocks
    for p in range(blocks):
        places[owner[p]] = p * block
    start, sent = 0, []
    for copy, ref, parts in zip(copies, held, pieces):
        copy.wait()
        for k, (turn, plane) in enumerate(parts):
            width = ref.shape[2]
            for n in range(0, width, 256):
                product = jnp.dot(hidden, ref[k, :, n : n + 256], preferred_element_type=F32)
                results[:, start + n : start + n + 256] = product.astype(BF16)
            side = (plane - 2 if plane >= 2 else group ^ plane) if width < block else 0
            place = places[here ^ turn] + side * width
            sent.append(
                pltpu.make_async_copy(
                    results.at[:, start : start + width],
                    out.at[:, pl.ds(pl.multiple_of(place, 128), width)],
                    out_sem.at[len(sent)],
                )
            )
            sent[-1].start()
            start += width
    for copy in sent:
        copy.wait()


def first_kernel(pieces, live_ref, owner_ref, *refs):
    count = len(pieces)
    sums, weights, (out, hidden_ref) = refs[:2], refs[2 : 2 + count], refs[2 + count : 4 + count]
    owner, *rest = refs[4 + count :]
    sums_held, held = rest[:2], rest[2 : 2 + count]
    sem, results, out_sem, places, hidden, hidden_sem = rest[2 + count :]
    first, *copies = fetch(
        list(zip((owner_ref, *sums, *weights), (owner, *sums_held, *held))), sem
    )
    for copy in (first, *copies[:2]):
        copy.wait()
    hid = hidden.shape[1]
    total = sums_held[0][...] + sums_held[1][...].astype(F32)
    gate, up = total[:, :hid], total[:, hid:]
    units = gate / (1.0 + jnp.exp(-gate)) * up
    rows = lax.broadcasted_iota(jnp.int32, units.shape, 0)
    hidden[...] = jnp.where(rows < MEM + live_ref[0], units, 0.0).astype(BF16)
    handed = pltpu.make_async_copy(hidden, hidden_ref, hidden_sem)
    handed.start()
    multiply_out(hidden[...], copies[2:], pieces, owner, out, held, results, out_sem, places)
    handed.wait()


def second_kernel(pieces, owner_ref, hidden_ref, _, *refs):
    count = len(pieces)
    weights, out, owner, held = refs[:count], refs[count], refs[count + 1], refs[count + 2 : 2 * count + 2]
    sem, results, out_sem, places, hidden = refs[2 * count + 2 :]
    first, second, *copies = fetch(
        list(zip((owner_ref, hidden_ref, *weights), (owner, hidden, *held))), sem
    )
    first.wait()
    second.wait()
    multiply_out(hidden[...], copies, pieces, owner, out, held, results, out_sem, places)


def down_call(kernel, name, live, fetched, passed, downs, outs, scratch, aliases):
    weights, pieces = zip(*downs)
    rows = outs[0].shape[0]
    hid = weights[0].shape[1]
    columns = sum(w.size for w in weights) // hid
    places = [pltpu.SMEM(v.shape, v.dtype) for v in fetched[:1]]
    kept = [pltpu.VMEM(v.shape, v.dtype) for v in fetched[1:] if v.shape != (rows, hid)]
    return pl.pallas_call(
        functools.partial(kernel, pieces),
        in_specs=[SMEM] * len(live) + [HBM] * (len(fetched) + len(passed) + len(weights)),
        out_specs=[HBM] * len(outs),
        out_shape=outs,
        scratch_shapes=places
        + kept
        + [pltpu.VMEM(w.shape, w.dtype) for w in weights]
        + [
            pltpu.SemaphoreType.DMA((len(fetched) + len(weights),)),
            pltpu.VMEM((rows, columns), BF16),
            pltpu.SemaphoreType.DMA((sum(len(p) for p in pieces),)),
            *places,
            pltpu.VMEM((rows, hid), BF16),
            *scratch,
        ],
        input_output_aliases=aliases,
        compiler_params=pltpu.CompilerParams(vmem_limit_bytes=FULL),
        cost_estimate=pl.CostEstimate(
            flops=20 * rows * hid * columns,
            bytes_accessed=2 * columns * (rows + hid),
            transcendentals=0,
        ),
        name=name,
    )(*live, *fetched, *passed, *weights)


def stack_kernel(a_ref, b_ref, out_ref):
    out_ref[0] = a_ref[0]
    out_ref[1] = b_ref[0]


def stacked(a, b, flops):
    return pl.pallas_call(
        stack_kernel,
        out_shape=jax.ShapeDtypeStruct((2,) + a.shape[1:], a.dtype),
        compiler_params=pltpu.CompilerParams(vmem_limit_bytes=8 << 20),
        cost_estimate=pl.CostEstimate(flops=flops, bytes_accessed=4 * a.size, transcendentals=0),
        name="stack_halves",
    )(a, b)


def after(value, *others):
    return lax.optimization_barrier((value, *others))[0]


def split(groups, owners, tokens, norm_gain, gate_weight, up_weight, down_weight, owner_rows, seg_counts):
    model_width = tokens.shape[1]
    half = model_width // owners // 2
    group, here = lax.axis_index("groups"), lax.axis_index("wide")
    core, across, near, far, other = (0, 1), (0, 2), (0, 4), (0, 8), (1, 0)

    def swap(value, way):
        pairs = [
            (g * owners + w, (g ^ way[0]) * owners + (w ^ way[1]))
            for g in range(groups)
            for w in range(owners)
        ]
        return lax.ppermute(value, ALL, pairs)

    first = group == 0
    a0 = jnp.where(first, gate_weight, up_weight)
    mine = jnp.where(first, down_weight[:, :half], down_weight[:, half:])[None]

    a1 = swap(a0, near)
    a2 = swap(a0, far)
    mine_x = swap(mine, across)

    t0, t2 = normed_halves(tokens, norm_gain, owner_rows)
    r2 = swap(t2, across)
    rest_x = swap(after(mine_x, t2), other)

    def cross(weights, parts):
        return swap(weights, core), tuple((turn ^ 1, plane) for turn, plane in parts)

    own = [(down_weight[None], ((0, 0),))]
    gate_c, up_c = swap(gate_weight, core), swap(up_weight, core)
    d0 = stacked(
        after(mine, a1, a2, t2, gate_c), mine_x, 10**11
    )

    b1 = swap(after(a1, d0, rest_x), other)
    a3 = swap(after(a2, d0), near)
    d2 = swap(after(down_weight[None], d0), far)
    b2 = swap(after(a2, d0, rest_x), other)

    b3 = swap(after(a3, b1, b2), other)
    d1 = swap(after(d0, a3, d2), near)

    e1 = swap(after(d1, b3), other)
    d3 = swap(after(d2, d1), near)
    f2 = swap(after(d2, r2), across)

    second = own + [(mine_x, ((2, 0),)), (rest_x, ((2, 1),)), (d2, ((8, 0),))]
    weights = (gate_weight, up_weight, a1, b1, a2, b2, a3, b3)
    weights = weights + (gate_c, up_c) + tuple(swap(w, core) for w in weights[2:])
    held = [cross(after(w, b1, b2, a3), parts) for w, parts in (second[0], second[3])]
    p0, p2 = partial_sums((after(t0, held[0][0], held[1][0]), r2), weights, (F32, BF16))
    q2 = swap(p2, across)

    f3 = swap(after(f2, d3, p2)[:, :, :half], near)
    g3 = swap(after(d3, f2, p2)[:, :, half:], across)

    third = [
        (d1, ((4, 0), (6, 0))),
        (e1, ((4, 1), (6, 1))),
        (f2, ((10, 0),)),
        (d3, ((12, 0),)),
    ]
    early = second + held + [cross(after(w, q2), parts) for w, parts in second[1:3]] + third
    out = pltpu.HBM(tokens.shape, BF16)
    rows, hid = tokens.shape[0], gate_weight.shape[1]
    product, hidden = down_call(
        first_kernel, "down_first", [seg_counts], [owner_rows, p0, q2], [], early,
        [out, pltpu.HBM((rows, hid), BF16)], [pltpu.SemaphoreType.DMA], {},
    )
    late = [(after(f3, hidden), ((14, 2),)), (after(g3, hidden), ((14, 3),))]
    late = [cross(after(w, hidden), parts) for w, parts in third[:2]] + [cross(after(w, hidden), parts) for w, parts in third[2:]] + late + [cross(*w) for w in late]
    return down_call(
        second_kernel, "down_second", [], [owner_rows, hidden], [product], late, [out], [], {2: 0}
    )[0]


def solution(mesh):
    placed = (
        P(("groups", "wide"), None),
        P(),
        P("wide", None),
        P("wide", None),
        P(None, "wide"),
        P(),
        P(("groups", "wide")),
    )
    groups, owners = mesh.shape["groups"], mesh.shape["wide"]
    plan = functools.partial(split, groups, owners) if (groups, owners) == (2, 16) else gathered
    return jax.shard_map(
        plan, mesh=mesh, in_specs=placed, out_specs=P(("groups", "wide"), None), check_vma=False
    )
```

```python
import functools

import jax
import jax.numpy as jnp
from jax import lax
from jax.experimental import pallas as pl
from jax.experimental.pallas import tpu as pltpu
from jax.sharding import PartitionSpec as P

MEM = 16
FULL = 60 << 20
ALL = ("groups", "wide")
F32, BF16 = jnp.float32, jnp.bfloat16
VMEM = pl.BlockSpec(memory_space=pltpu.VMEM)
SMEM = pl.BlockSpec(memory_space=pltpu.SMEM)
HBM = pl.BlockSpec(memory_space=pltpu.HBM)


def gathered(tokens, norm_gain, gate_weight, up_weight, down_weight, owner_rows, seg_counts):
    row_count, model_width = tokens.shape
    owners = lax.axis_size("wide")
    block_rows = model_width // owners
    indices = jnp.arange(owners, dtype=jnp.int32)
    holder = jnp.sum(
        indices[:, None] * (owner_rows[:, None] == indices[None, :]).astype(jnp.int32), axis=0
    )
    features = tokens.astype(F32)
    mean_square = jnp.mean(features * features, axis=1, keepdims=True)
    normed = (features * lax.rsqrt(mean_square + 1e-05) * norm_gain[None, :]).astype(BF16)
    stored = normed.reshape(row_count, owners, block_rows)[:, holder, :].reshape(
        row_count, model_width
    )

    def partial_product(portion):
        return jnp.dot(stored, portion, preferred_element_type=F32)

    gate_sum = partial_product(lax.all_gather(gate_weight, "wide", axis=0, tiled=True))
    up_sum = partial_product(lax.all_gather(up_weight, "wide", axis=0, tiled=True))
    hidden = (jax.nn.silu(gate_sum) * up_sum).astype(BF16)
    stored_out = jnp.dot(
        hidden,
        lax.all_gather(down_weight, "wide", axis=1, tiled=True),
        preferred_element_type=F32,
    ).astype(BF16)
    product = stored_out.reshape(row_count, owners, block_rows)[:, owner_rows, :].reshape(
        row_count, model_width
    )
    live_mask = (jnp.arange(row_count, dtype=jnp.int32) < MEM + seg_counts[0]).astype(BF16)
    return product * live_mask[:, None]


def norm_kernel(owner_ref, tokens_ref, gain_ref, *rest):
    (own, near, far), (held, made, scale_ref, in_sem, out_sem) = rest[:3], rest[3:]
    here = lax.axis_index("wide")
    rows, model_width = held.shape
    blocks = owner_ref.shape[0]
    width = model_width // blocks
    step = rows // in_sem.shape[0]
    outs = (own, near, far, far.at[blocks // 4 :])
    copies = [
        pltpu.make_async_copy(
            tokens_ref.at[r : r + step], held.at[r : r + step], in_sem.at[r // step]
        )
        for r in range(0, rows, step)
    ]
    for copy in copies:
        copy.start()
    for r, copy in zip(range(0, rows, step), copies):
        copy.wait()
        parts = [jnp.zeros((step, 128), F32) for _ in range(8)]
        for start in range(0, model_width, 128):
            part = held[r : r + step, start : start + 128].astype(F32)
            parts[start // 128 % 8] += part * part
        mean = jnp.sum(sum(parts), axis=1, keepdims=True) / model_width
        scale_ref[r : r + step] = jnp.broadcast_to(lax.rsqrt(mean + 1e-05), (step, 128))
    scale = scale_ref[...]
    for p in range(blocks):
        for start in range(0, width, 128):
            columns = slice(p * width + start, p * width + start + 128)
            normed = held[:, columns].astype(F32) * scale * gain_ref[:, columns]
            made[p, :, start : start + 128] = normed.astype(BF16)
        stored = owner_ref[p]
        for turn, out in enumerate(outs):

            @pl.when(((stored ^ here) & 3) == turn)
            def _(out=out, p=p, stored=stored):
                pltpu.make_async_copy(made.at[p], out.at[stored >> 2], out_sem.at[p]).start()

    for p in range(blocks):
        pltpu.make_async_copy(made.at[p], outs[0].at[0], out_sem.at[p]).wait()


def normed_quarters(tokens, gain, owner_rows):
    rows, model_width = tokens.shape
    blocks = owner_rows.shape[0]
    width = model_width // blocks
    return pl.pallas_call(
        norm_kernel,
        in_specs=[SMEM, HBM, VMEM],
        out_specs=[HBM] * 3,
        out_shape=[pltpu.HBM((n * blocks // 4, rows, width), BF16) for n in (1, 1, 2)],
        scratch_shapes=[
            pltpu.VMEM((rows, model_width), BF16),
            pltpu.VMEM((blocks, rows, width), BF16),
            pltpu.VMEM((rows, 128), F32),
            pltpu.SemaphoreType.DMA((rows // 16,)),
            pltpu.SemaphoreType.DMA((blocks,)),
        ],
        compiler_params=pltpu.CompilerParams(vmem_limit_bytes=FULL),
        cost_estimate=pl.CostEstimate(
            flops=6 * rows * model_width, bytes_accessed=4 * rows * model_width, transcendentals=0
        ),
        name="norm_quarters",
    )(owner_rows, tokens, gain.reshape(1, model_width))


def fetch(pairs, sem):
    copies = [pltpu.make_async_copy(r, v, sem.at[i]) for i, (r, v) in enumerate(pairs)]
    for copy in copies:
        copy.start()
    return copies


def partial_kernel(given, kinds, *refs):
    count = len(kinds)
    made, (rows, held, mine, other, row_sem, sem, out_sem) = refs[-7 - count : -7], refs[-7:]
    outs = refs[-7 - 2 * count : -7 - count]
    inputs, weights = refs[:given], refs[given : -7 - 2 * count]
    z, plane = lax.axis_index("wide") >> 2, lax.axis_index("groups")
    size = inputs[0].shape[1]
    hid = held.shape[2]
    hops = len(weights) // 2
    parts = [ref.at[: rows.shape[0]] for ref in inputs]
    row_copies = fetch(
        [(part, rows.at[:, k * size : (k + 1) * size]) for k, part in enumerate(parts)], row_sem
    )
    copies = fetch([(ref, held.at[i]) for i, ref in enumerate(weights)], sem)
    for copy in row_copies:
        copy.wait()
    first = plane == 0
    step = hops // 2
    for start in range(0, hops, step):
        for i in range(2 * start, 2 * (start + step)):
            copies[i].wait()
        sent = []
        for k, (out, kind) in enumerate(zip(made, kinds)):
            here = slice(k * size, (k + 1) * size)
            sums = []
            for side in range(2):
                total = jnp.zeros((size, hid), F32) if start == 0 else (mine, other)[side][here]
                for hop in range(max(start, 1), start + step):
                    total += jnp.dot(
                        rows[z ^ hop, here], held[2 * hop + side], preferred_element_type=F32
                    )
                sums.append(total)
            if start == 0:
                (mine[here], other[here]) = sums
            else:
                a, b = sums
                gate, up = (
                    jnp.dot(rows[z, here], held[side], preferred_element_type=F32)
                    for side in range(2)
                )
                out[:, :hid] = (gate + jnp.where(first, a, b)).astype(kind)
                out[:, hid:] = (up + jnp.where(first, b, a)).astype(kind)
                sent.append(pltpu.make_async_copy(out, outs[k], out_sem.at[k]))
                sent[-1].start()
    for copy in sent:
        copy.wait()


def partial_sums(inputs, weights, kinds):
    count = len(kinds)
    hops, rows, depth = inputs[0].shape
    hid = weights[0].shape[1]
    return pl.pallas_call(
        functools.partial(partial_kernel, len(inputs), kinds),
        in_specs=[HBM] * (len(inputs) + len(weights)),
        out_specs=[HBM] * count,
        out_shape=[pltpu.HBM((rows, 2 * hid), kind) for kind in kinds],
        scratch_shapes=[pltpu.VMEM((rows, 2 * hid), kind) for kind in kinds]
        + [
            pltpu.VMEM((hops, count * rows, depth), BF16),
            pltpu.VMEM((len(weights), depth, hid), BF16),
            pltpu.VMEM((count * rows, hid), F32),
            pltpu.VMEM((count * rows, hid), F32),
            pltpu.SemaphoreType.DMA((count,)),
            pltpu.SemaphoreType.DMA((len(weights),)),
            pltpu.SemaphoreType.DMA((count,)),
        ],
        compiler_params=pltpu.CompilerParams(vmem_limit_bytes=FULL),
        cost_estimate=pl.CostEstimate(
            flops=4 * hops * count * rows * depth * hid,
            bytes_accessed=2 * hops * depth * (count * rows + 2 * hid),
            transcendentals=0,
        ),
        name="partial_sums",
    )(*inputs, *weights)


def multiply_out(hidden, copies, pieces, owner, out, held, results, out_sem, places):
    group, here = lax.axis_index("groups"), lax.axis_index("wide")
    blocks = owner.shape[0]
    block = out.shape[1] // blocks
    for p in range(blocks):
        places[owner[p]] = p * block
    start, sent = 0, []
    for copy, ref, parts in zip(copies, held, pieces):
        copy.wait()
        for k, (turn, plane) in enumerate(parts):
            width = ref.shape[2]
            for n in range(0, width, 256):
                product = jnp.dot(hidden, ref[k, :, n : n + 256], preferred_element_type=F32)
                results[:, start + n : start + n + 256] = product.astype(BF16)
            side = group ^ plane if width < block else 0
            place = places[here ^ turn] + side * width
            sent.append(
                pltpu.make_async_copy(
                    results.at[:, start : start + width],
                    out.at[:, pl.ds(pl.multiple_of(place, 128), width)],
                    out_sem.at[len(sent)],
                )
            )
            sent[-1].start()
            start += width
    for copy in sent:
        copy.wait()


def first_kernel(pieces, live_ref, owner_ref, *refs):
    count = len(pieces)
    sums, weights, (out, hidden_ref) = refs[:4], refs[4 : 4 + count], refs[4 + count : 6 + count]
    owner, *rest = refs[6 + count :]
    sums_held, held = rest[:4], rest[4 : 4 + count]
    sem, results, out_sem, places, hidden, hidden_sem = rest[4 + count :]
    first, *copies = fetch(
        list(zip((owner_ref, *sums, *weights), (owner, *sums_held, *held))), sem
    )
    for copy in (first, *copies[:4]):
        copy.wait()
    hid = hidden.shape[1]
    total = sums_held[0][...]
    for part in sums_held[1:]:
        total += part[...].astype(F32)
    gate, up = total[:, :hid], total[:, hid:]
    units = gate / (1.0 + jnp.exp(-gate)) * up
    rows = lax.broadcasted_iota(jnp.int32, units.shape, 0)
    hidden[...] = jnp.where(rows < MEM + live_ref[0], units, 0.0).astype(BF16)
    handed = pltpu.make_async_copy(hidden, hidden_ref, hidden_sem)
    handed.start()
    multiply_out(hidden[...], copies[4:], pieces, owner, out, held, results, out_sem, places)
    handed.wait()


def second_kernel(pieces, owner_ref, hidden_ref, _, *refs):
    count = len(pieces)
    weights, out, owner, held = refs[:count], refs[count], refs[count + 1], refs[count + 2 : 2 * count + 2]
    sem, results, out_sem, places, hidden = refs[2 * count + 2 :]
    first, second, *copies = fetch(
        list(zip((owner_ref, hidden_ref, *weights), (owner, hidden, *held))), sem
    )
    first.wait()
    second.wait()
    multiply_out(hidden[...], copies, pieces, owner, out, held, results, out_sem, places)


def down_call(kernel, name, live, fetched, passed, downs, outs, scratch, aliases):
    weights, pieces = zip(*downs)
    rows = outs[0].shape[0]
    hid = weights[0].shape[1]
    columns = sum(w.size for w in weights) // hid
    places = [pltpu.SMEM(v.shape, v.dtype) for v in fetched[:1]]
    kept = [pltpu.VMEM(v.shape, v.dtype) for v in fetched[1:] if v.shape != (rows, hid)]
    return pl.pallas_call(
        functools.partial(kernel, pieces),
        in_specs=[SMEM] * len(live) + [HBM] * (len(fetched) + len(passed) + len(weights)),
        out_specs=[HBM] * len(outs),
        out_shape=outs,
        scratch_shapes=places
        + kept
        + [pltpu.VMEM(w.shape, w.dtype) for w in weights]
        + [
            pltpu.SemaphoreType.DMA((len(fetched) + len(weights),)),
            pltpu.VMEM((rows, columns), BF16),
            pltpu.SemaphoreType.DMA((sum(len(p) for p in pieces),)),
            *places,
            pltpu.VMEM((rows, hid), BF16),
            *scratch,
        ],
        input_output_aliases=aliases,
        compiler_params=pltpu.CompilerParams(vmem_limit_bytes=FULL),
        cost_estimate=pl.CostEstimate(
            flops=20 * rows * hid * columns,
            bytes_accessed=2 * columns * (rows + hid),
            transcendentals=0,
        ),
        name=name,
    )(*live, *fetched, *passed, *weights)


def stack_kernel(a_ref, b_ref, out_ref):
    out_ref[0] = a_ref[0]
    out_ref[1] = b_ref[0]


def stacked(a, b, flops):
    return pl.pallas_call(
        stack_kernel,
        out_shape=jax.ShapeDtypeStruct((2,) + a.shape[1:], a.dtype),
        compiler_params=pltpu.CompilerParams(vmem_limit_bytes=8 << 20),
        cost_estimate=pl.CostEstimate(flops=flops, bytes_accessed=4 * a.size, transcendentals=0),
        name="stack_halves",
    )(a, b)


def after(value, *others):
    return lax.optimization_barrier((value, *others))[0]


def split(groups, owners, tokens, norm_gain, gate_weight, up_weight, down_weight, owner_rows, seg_counts):
    model_width = tokens.shape[1]
    half = model_width // owners // 2
    group, here = lax.axis_index("groups"), lax.axis_index("wide")
    core, across, near, far, other = (0, 1), (0, 2), (0, 4), (0, 8), (1, 0)
    both = (0, 3)

    def swap(value, way):
        pairs = [
            (g * owners + w, (g ^ way[0]) * owners + (w ^ way[1]))
            for g in range(groups)
            for w in range(owners)
        ]
        return lax.ppermute(value, ALL, pairs)

    first = group == 0
    a0 = jnp.where(first, gate_weight, up_weight)
    mine = jnp.where(first, down_weight[:, :half], down_weight[:, half:])[None]

    a1 = swap(a0, near)
    a2 = swap(a0, far)
    mine_x = swap(mine, across)

    t0, t1, t2 = normed_quarters(tokens, norm_gain, owner_rows)
    r2 = swap(t2, across)
    r1 = swap(t1, core)
    rest_x = swap(after(mine_x, t2), other)

    def cross(weights, parts):
        return swap(weights, core), tuple((turn ^ 1, plane) for turn, plane in parts)

    own = [(down_weight[None], ((0, 0),))]
    own = own + [cross(*w) for w in own]
    d0 = stacked(
        after(mine, a1, a2, t2, own[1][0]), mine_x, 10**11
    )

    b1 = swap(after(a1, d0, rest_x), other)
    a3 = swap(after(a2, d0), near)
    d2 = swap(after(down_weight[None], d0), far)
    b2 = swap(after(a2, d0, rest_x), other)

    b3 = swap(after(a3, b1, b2), other)
    d1 = swap(after(d0, a3), near)

    e1 = swap(after(d1, b3), other)
    d3 = swap(after(d2, d1), near)
    f2 = swap(after(d2, r2), across)

    second = [(mine_x, ((2, 0),)), (rest_x, ((2, 1),)), (d2, ((8, 0),))]
    second = second + [cross(*w) for w in second]
    r3 = swap(after(r2, b3, d1, *(w for w, _ in second))[owners // 4 :], core)
    weights = (gate_weight, up_weight, a1, b1, a2, b2, a3, b3)
    p0, p1, p2, p3 = partial_sums(
        (t0, r1, r2, r3), weights, (F32, F32, BF16, BF16)
    )
    q1 = swap(p1, core)
    q2 = swap(p2, across)
    q3 = swap(after(p3, q1), both)

    f3 = swap(after(f2, d3, q1), near)

    third = [
        (d1, ((4, 0), (6, 0))),
        (e1, ((4, 1), (6, 1))),
        (f2, ((10, 0),)),
        (d3, ((12, 0),)),
    ]
    early = own + second + third
    out = pltpu.HBM(tokens.shape, BF16)
    rows, hid = tokens.shape[0], gate_weight.shape[1]
    product, hidden = down_call(
        first_kernel, "down_first", [seg_counts], [owner_rows, p0, q1, q2, q3], [], early,
        [out, pltpu.HBM((rows, hid), BF16)], [pltpu.SemaphoreType.DMA], {},
    )
    late = [(after(f3, hidden), ((14, 0),))]
    late = [cross(after(w, hidden), parts) for w, parts in third] + late + [cross(*w) for w in late]
    return down_call(
        second_kernel, "down_second", [], [owner_rows, hidden], [product], late, [out], [], {2: 0}
    )[0]


def solution(mesh):
    placed = (
        P(("groups", "wide"), None),
        P(),
        P("wide", None),
        P("wide", None),
        P(None, "wide"),
        P(),
        P(("groups", "wide")),
    )
    groups, owners = mesh.shape["groups"], mesh.shape["wide"]
    plan = functools.partial(split, groups, owners) if (groups, owners) == (2, 16) else gathered
    return jax.shard_map(
        plan, mesh=mesh, in_specs=placed, out_specs=P(("groups", "wide"), None), check_vma=False
    )
```

```python
import functools

import jax
import jax.numpy as jnp
from jax import lax
from jax.experimental import pallas as pl
from jax.experimental.pallas import tpu as pltpu
from jax.sharding import PartitionSpec as P

MEM = 16
FULL = 60 << 20
ALL = ("groups", "wide")
F32, BF16 = jnp.float32, jnp.bfloat16
VMEM = pl.BlockSpec(memory_space=pltpu.VMEM)
SMEM = pl.BlockSpec(memory_space=pltpu.SMEM)
HBM = pl.BlockSpec(memory_space=pltpu.HBM)


def gathered(tokens, norm_gain, gate_weight, up_weight, down_weight, owner_rows, seg_counts):
    row_count, model_width = tokens.shape
    owners = lax.axis_size("wide")
    block_rows = model_width // owners
    indices = jnp.arange(owners, dtype=jnp.int32)
    holder = jnp.sum(
        indices[:, None] * (owner_rows[:, None] == indices[None, :]).astype(jnp.int32), axis=0
    )
    features = tokens.astype(F32)
    mean_square = jnp.mean(features * features, axis=1, keepdims=True)
    normed = (features * lax.rsqrt(mean_square + 1e-05) * norm_gain[None, :]).astype(BF16)
    stored = normed.reshape(row_count, owners, block_rows)[:, holder, :].reshape(
        row_count, model_width
    )

    def partial_product(portion):
        return jnp.dot(stored, portion, preferred_element_type=F32)

    gate_sum = partial_product(lax.all_gather(gate_weight, "wide", axis=0, tiled=True))
    up_sum = partial_product(lax.all_gather(up_weight, "wide", axis=0, tiled=True))
    hidden = (jax.nn.silu(gate_sum) * up_sum).astype(BF16)
    stored_out = jnp.dot(
        hidden,
        lax.all_gather(down_weight, "wide", axis=1, tiled=True),
        preferred_element_type=F32,
    ).astype(BF16)
    product = stored_out.reshape(row_count, owners, block_rows)[:, owner_rows, :].reshape(
        row_count, model_width
    )
    live_mask = (jnp.arange(row_count, dtype=jnp.int32) < MEM + seg_counts[0]).astype(BF16)
    return product * live_mask[:, None]


def norm_kernel(owner_ref, tokens_ref, gain_ref, *rest):
    (own, near, far), (held, made, scale_ref, in_sem, out_sem) = rest[:3], rest[3:]
    here = lax.axis_index("wide")
    rows, model_width = held.shape
    blocks = owner_ref.shape[0]
    width = model_width // blocks
    step = rows // in_sem.shape[0]
    outs = (own, near, far, far.at[blocks // 4 :])
    copies = [
        pltpu.make_async_copy(
            tokens_ref.at[r : r + step], held.at[r : r + step], in_sem.at[r // step]
        )
        for r in range(0, rows, step)
    ]
    for copy in copies:
        copy.start()
    for r, copy in zip(range(0, rows, step), copies):
        copy.wait()
        parts = [jnp.zeros((step, 128), F32) for _ in range(8)]
        for start in range(0, model_width, 128):
            part = held[r : r + step, start : start + 128].astype(F32)
            parts[start // 128 % 8] += part * part
        mean = jnp.sum(sum(parts), axis=1, keepdims=True) / model_width
        scale_ref[r : r + step] = jnp.broadcast_to(lax.rsqrt(mean + 1e-05), (step, 128))
    scale = scale_ref[...]
    for p in range(blocks):
        for start in range(0, width, 128):
            columns = slice(p * width + start, p * width + start + 128)
            normed = held[:, columns].astype(F32) * scale * gain_ref[:, columns]
            made[p, :, start : start + 128] = normed.astype(BF16)
        stored = owner_ref[p]
        for turn, out in enumerate(outs):

            @pl.when(((stored ^ here) & 3) == turn)
            def _(out=out, p=p, stored=stored):
                pltpu.make_async_copy(made.at[p], out.at[stored >> 2], out_sem.at[p]).start()

    for p in range(blocks):
        pltpu.make_async_copy(made.at[p], outs[0].at[0], out_sem.at[p]).wait()


def normed_quarters(tokens, gain, owner_rows):
    rows, model_width = tokens.shape
    blocks = owner_rows.shape[0]
    width = model_width // blocks
    return pl.pallas_call(
        norm_kernel,
        in_specs=[SMEM, HBM, VMEM],
        out_specs=[HBM] * 3,
        out_shape=[pltpu.HBM((n * blocks // 4, rows, width), BF16) for n in (1, 1, 2)],
        scratch_shapes=[
            pltpu.VMEM((rows, model_width), BF16),
            pltpu.VMEM((blocks, rows, width), BF16),
            pltpu.VMEM((rows, 128), F32),
            pltpu.SemaphoreType.DMA((rows // 16,)),
            pltpu.SemaphoreType.DMA((blocks,)),
        ],
        compiler_params=pltpu.CompilerParams(vmem_limit_bytes=FULL),
        cost_estimate=pl.CostEstimate(
            flops=6 * rows * model_width, bytes_accessed=4 * rows * model_width, transcendentals=0
        ),
        name="norm_quarters",
    )(owner_rows, tokens, gain.reshape(1, model_width))


def fetch(pairs, sem):
    copies = [pltpu.make_async_copy(r, v, sem.at[i]) for i, (r, v) in enumerate(pairs)]
    for copy in copies:
        copy.start()
    return copies


def partial_kernel(given, kinds, *refs):
    count = len(kinds)
    made, (rows, held, mine, other, row_sem, sem, out_sem) = refs[-7 - count : -7], refs[-7:]
    outs = refs[-7 - 2 * count : -7 - count]
    inputs, weights = refs[:given], refs[given : -7 - 2 * count]
    z, plane = lax.axis_index("wide") >> 2, lax.axis_index("groups")
    size = inputs[0].shape[1]
    hid = held.shape[2]
    hops = len(weights) // 2
    parts = [ref.at[: rows.shape[0]] for ref in inputs]
    row_copies = fetch(
        [(part, rows.at[:, k * size : (k + 1) * size]) for k, part in enumerate(parts)], row_sem
    )
    copies = fetch([(ref, held.at[i]) for i, ref in enumerate(weights)], sem)
    for copy in row_copies:
        copy.wait()
    first = plane == 0
    step = hops // 2
    for start in range(0, hops, step):
        for i in range(2 * start, 2 * (start + step)):
            copies[i].wait()
        sent = []
        for k, (out, kind) in enumerate(zip(made, kinds)):
            here = slice(k * size, (k + 1) * size)
            sums = []
            for side in range(2):
                total = jnp.zeros((size, hid), F32) if start == 0 else (mine, other)[side][here]
                for hop in range(max(start, 1), start + step):
                    total += jnp.dot(
                        rows[z ^ hop, here], held[2 * hop + side], preferred_element_type=F32
                    )
                sums.append(total)
            if start == 0:
                (mine[here], other[here]) = sums
            else:
                a, b = sums
                gate, up = (
                    jnp.dot(rows[z, here], held[side], preferred_element_type=F32)
                    for side in range(2)
                )
                out[:, :hid] = (gate + jnp.where(first, a, b)).astype(kind)
                out[:, hid:] = (up + jnp.where(first, b, a)).astype(kind)
                sent.append(pltpu.make_async_copy(out, outs[k], out_sem.at[k]))
                sent[-1].start()
    for copy in sent:
        copy.wait()


def partial_sums(inputs, weights, kinds):
    count = len(kinds)
    hops, rows, depth = inputs[0].shape
    hid = weights[0].shape[1]
    return pl.pallas_call(
        functools.partial(partial_kernel, len(inputs), kinds),
        in_specs=[HBM] * (len(inputs) + len(weights)),
        out_specs=[HBM] * count,
        out_shape=[pltpu.HBM((rows, 2 * hid), kind) for kind in kinds],
        scratch_shapes=[pltpu.VMEM((rows, 2 * hid), kind) for kind in kinds]
        + [
            pltpu.VMEM((hops, count * rows, depth), BF16),
            pltpu.VMEM((len(weights), depth, hid), BF16),
            pltpu.VMEM((count * rows, hid), F32),
            pltpu.VMEM((count * rows, hid), F32),
            pltpu.SemaphoreType.DMA((count,)),
            pltpu.SemaphoreType.DMA((len(weights),)),
            pltpu.SemaphoreType.DMA((count,)),
        ],
        compiler_params=pltpu.CompilerParams(vmem_limit_bytes=FULL),
        cost_estimate=pl.CostEstimate(
            flops=4 * hops * count * rows * depth * hid,
            bytes_accessed=2 * hops * depth * (count * rows + 2 * hid),
            transcendentals=0,
        ),
        name="partial_sums",
    )(*inputs, *weights)


def multiply_out(hidden, copies, pieces, owner, out, held, results, out_sem, places):
    group, here = lax.axis_index("groups"), lax.axis_index("wide")
    blocks = owner.shape[0]
    block = out.shape[1] // blocks
    for p in range(blocks):
        places[owner[p]] = p * block
    start, sent = 0, []
    for copy, ref, parts in zip(copies, held, pieces):
        copy.wait()
        for k, (turn, plane) in enumerate(parts):
            width = ref.shape[2]
            for n in range(0, width, 256):
                product = jnp.dot(hidden, ref[k, :, n : n + 256], preferred_element_type=F32)
                results[:, start + n : start + n + 256] = product.astype(BF16)
            side = group ^ plane if width < block else 0
            place = places[here ^ turn] + side * width
            sent.append(
                pltpu.make_async_copy(
                    results.at[:, start : start + width],
                    out.at[:, pl.ds(pl.multiple_of(place, 128), width)],
                    out_sem.at[len(sent)],
                )
            )
            sent[-1].start()
            start += width
    for copy in sent:
        copy.wait()


def first_kernel(pieces, live_ref, owner_ref, *refs):
    count = len(pieces)
    sums, weights, (out, hidden_ref) = refs[:4], refs[4 : 4 + count], refs[4 + count : 6 + count]
    owner, *rest = refs[6 + count :]
    sums_held, held = rest[:4], rest[4 : 4 + count]
    sem, results, out_sem, places, hidden, hidden_sem = rest[4 + count :]
    first, *copies = fetch(
        list(zip((owner_ref, *sums, *weights), (owner, *sums_held, *held))), sem
    )
    for copy in (first, *copies[:4]):
        copy.wait()
    hid = hidden.shape[1]
    total = sums_held[0][...]
    for part in sums_held[1:]:
        total += part[...].astype(F32)
    gate, up = total[:, :hid], total[:, hid:]
    units = gate / (1.0 + jnp.exp(-gate)) * up
    rows = lax.broadcasted_iota(jnp.int32, units.shape, 0)
    hidden[...] = jnp.where(rows < MEM + live_ref[0], units, 0.0).astype(BF16)
    handed = pltpu.make_async_copy(hidden, hidden_ref, hidden_sem)
    handed.start()
    multiply_out(hidden[...], copies[4:], pieces, owner, out, held, results, out_sem, places)
    handed.wait()


def second_kernel(pieces, owner_ref, hidden_ref, _, *refs):
    count = len(pieces)
    weights, out, owner, held = refs[:count], refs[count], refs[count + 1], refs[count + 2 : 2 * count + 2]
    sem, results, out_sem, places, hidden = refs[2 * count + 2 :]
    first, second, *copies = fetch(
        list(zip((owner_ref, hidden_ref, *weights), (owner, hidden, *held))), sem
    )
    first.wait()
    second.wait()
    multiply_out(hidden[...], copies, pieces, owner, out, held, results, out_sem, places)


def down_call(kernel, name, live, fetched, passed, downs, outs, scratch, aliases):
    weights, pieces = zip(*downs)
    rows = outs[0].shape[0]
    hid = weights[0].shape[1]
    columns = sum(w.size for w in weights) // hid
    places = [pltpu.SMEM(v.shape, v.dtype) for v in fetched[:1]]
    kept = [pltpu.VMEM(v.shape, v.dtype) for v in fetched[1:] if v.shape != (rows, hid)]
    return pl.pallas_call(
        functools.partial(kernel, pieces),
        in_specs=[SMEM] * len(live) + [HBM] * (len(fetched) + len(passed) + len(weights)),
        out_specs=[HBM] * len(outs),
        out_shape=outs,
        scratch_shapes=places
        + kept
        + [pltpu.VMEM(w.shape, w.dtype) for w in weights]
        + [
            pltpu.SemaphoreType.DMA((len(fetched) + len(weights),)),
            pltpu.VMEM((rows, columns), BF16),
            pltpu.SemaphoreType.DMA((sum(len(p) for p in pieces),)),
            *places,
            pltpu.VMEM((rows, hid), BF16),
            *scratch,
        ],
        input_output_aliases=aliases,
        compiler_params=pltpu.CompilerParams(vmem_limit_bytes=FULL),
        cost_estimate=pl.CostEstimate(
            flops=20 * rows * hid * columns,
            bytes_accessed=2 * columns * (rows + hid),
            transcendentals=0,
        ),
        name=name,
    )(*live, *fetched, *passed, *weights)


def stack_kernel(a_ref, b_ref, out_ref):
    out_ref[0] = a_ref[0]
    out_ref[1] = b_ref[0]


def stacked(a, b, flops):
    return pl.pallas_call(
        stack_kernel,
        out_shape=jax.ShapeDtypeStruct((2,) + a.shape[1:], a.dtype),
        compiler_params=pltpu.CompilerParams(vmem_limit_bytes=8 << 20),
        cost_estimate=pl.CostEstimate(flops=flops, bytes_accessed=4 * a.size, transcendentals=0),
        name="stack_halves",
    )(a, b)


def after(value, *others):
    return lax.optimization_barrier((value, *others))[0]


def split(groups, owners, tokens, norm_gain, gate_weight, up_weight, down_weight, owner_rows, seg_counts):
    model_width = tokens.shape[1]
    half = model_width // owners // 2
    group, here = lax.axis_index("groups"), lax.axis_index("wide")
    core, across, near, far, other = (0, 1), (0, 2), (0, 4), (0, 8), (1, 0)
    both = (0, 3)

    def swap(value, way):
        pairs = [
            (g * owners + w, (g ^ way[0]) * owners + (w ^ way[1]))
            for g in range(groups)
            for w in range(owners)
        ]
        return lax.ppermute(value, ALL, pairs)

    first = group == 0
    a0 = jnp.where(first, gate_weight, up_weight)
    mine = jnp.where(first, down_weight[:, :half], down_weight[:, half:])[None]

    a1 = swap(a0, near)
    a2 = swap(a0, far)
    mine_x = swap(mine, across)

    t0, t1, t2 = normed_quarters(tokens, norm_gain, owner_rows)
    r2 = swap(t2, across)
    r1 = swap(t1, core)
    rest_x = swap(after(mine_x, t2), other)

    def cross(weights, parts):
        return swap(weights, core), tuple((turn ^ 1, plane) for turn, plane in parts)

    own = [(down_weight[None], ((0, 0),))]
    own = own + [cross(*w) for w in own]
    d0 = stacked(
        after(mine, a1, a2, t2, own[1][0]), mine_x, 10**11
    )

    b1 = swap(after(a1, d0, rest_x), other)
    a3 = swap(after(a2, d0), near)
    d2 = swap(after(down_weight[None], d0), far)
    b2 = swap(after(a2, d0, rest_x), other)

    b3 = swap(after(a3, b1, b2), other)
    d1 = swap(after(d0, a3), near)

    e1 = swap(after(d1, b3), other)
    d3 = swap(after(d2, d1), near)
    f2 = swap(after(d2, r2), across)

    second = [(mine_x, ((2, 0),)), (rest_x, ((2, 1),)), (d2, ((8, 0),))]
    second = second + [cross(*w) for w in second]
    r3 = swap(after(r2, b3, d1, *(w for w, _ in second))[owners // 4 :], core)
    weights = (gate_weight, up_weight, a1, b1, a2, b2, a3, b3)
    p0, p1, p2, p3 = partial_sums(
        (t0, r1, r2, r3), weights, (F32, F32, BF16, BF16)
    )
    q1 = swap(p1, core)
    q2 = swap(p2, across)
    q3 = swap(after(p3, q1), both)

    f3 = swap(after(f2, d3, q1), near)

    third = [
        (d1, ((4, 0), (6, 0))),
        (e1, ((4, 1), (6, 1))),
        (f2, ((10, 0),)),
        (d3, ((12, 0),)),
    ]
    early = own + second + third
    out = pltpu.HBM(tokens.shape, BF16)
    rows, hid = tokens.shape[0], gate_weight.shape[1]
    product, hidden = down_call(
        first_kernel, "down_first", [seg_counts], [owner_rows, p0, q1, q2, q3], [], early,
        [out, pltpu.HBM((rows, hid), BF16)], [pltpu.SemaphoreType.DMA], {},
    )
    late = [(after(f3, hidden), ((14, 0),))]
    late = [cross(after(w, q1), parts) for w, parts in third[:1]] + [cross(after(w, hidden), parts) for w, parts in third[1:]] + late + [cross(*w) for w in late]
    return down_call(
        second_kernel, "down_second", [], [owner_rows, hidden], [product], late, [out], [], {2: 0}
    )[0]


def solution(mesh):
    placed = (
        P(("groups", "wide"), None),
        P(),
        P("wide", None),
        P("wide", None),
        P(None, "wide"),
        P(),
        P(("groups", "wide")),
    )
    groups, owners = mesh.shape["groups"], mesh.shape["wide"]
    plan = functools.partial(split, groups, owners) if (groups, owners) == (2, 16) else gathered
    return jax.shard_map(
        plan, mesh=mesh, in_specs=placed, out_specs=P(("groups", "wide"), None), check_vma=False
    )
```
